512 devices in a mesh: gz: 16 (over y, core), xy: 32 (over z, x).
Axes of the slice: x: 4, y: 8, z: 8, core: 2. Of those that a mesh axis runs over, the one named last changes fastest.
Arguments:
- patches: bfloat16 [16, 256, 128, 128], P('gz', 'xy'), may hold values from -30 to 30
- peak_offsets: int32 [16, 256, 2], P('gz', 'xy'), may hold values from -4 to 4
- tiles: bfloat16 [16, 64, 512, 512], P('gz', 'xy'), may hold values from -6 to 6
- band_offsets: int32 [16, 64, 2], P('gz', 'xy'), may hold values from -3 to 3
- routes: int32 [16, 2048, 1], P('gz', 'xy'), may hold values from 0 to 63; in each aligned block of 64 rows (0 to 63, 64 to 127, ..., all dimensions but the last counted through in order) at most 3 rows name the same one
Outputs:
- positions: float32 [16, 2, 256], P('gz', None, 'xy')
- rendered: bfloat16 [16, 64, 512, 512], P('gz', 'xy')
The draws below stay inside these ranges and needn't reach their ends.
Inputs may be any that keep to these rules, and one draw needn't show every extreme that they name: `routes`: in the rows of one device (the 64 pieces of its tiles) no group is named more than 3 times, a bound that some block reaches.
All inputs are finite; a program needn't handle non-finite values.
Results may differ from the reference program's by a relative error of at most 0.0067.
Values may be sent and summed in bfloat16 or wider, within the bound.
No kernel may reach another device: no remote copies, remote signals or barrier semaphores. Data moves between devices by JAX's collectives and lax.ppermute only.
A program may use at most 64 MiB of HBM per device.

```python
import math
import jax
import jax.numpy as jnp
import numpy as np
from jax import lax

PS = 128
TL = 512
NP = 8
NT = 2
PIECES = 32
BAND = 6
RELAX = 3
SECTIONS = 16
NODES = 256
TILES = 64
GROUPS = 64
MOST = 3


def draw_patches(key, part):
    key = jax.random.fold_in(key, 11)
    key_noise, key_scale = jax.random.split(key, 2)
    noise_field = jnp.clip(jax.random.normal(key_noise, (SECTIONS, NODES, PS, PS), jnp.float32), -3.5, 3.5)
    patch_scale = jnp.exp(jax.random.uniform(key_scale, (SECTIONS, NODES, 1, 1), jnp.float32, jnp.log(0.3), jnp.log(3.0)))
    return (patch_scale * noise_field).astype(jnp.bfloat16)


def with_ends(drawn, stream_key, least, high):
    place = [jax.random.randint(jax.random.fold_in(stream_key, axis), (), 0, length) for axis, length in enumerate(drawn.shape)]
    main_axis = drawn.shape.index(max(drawn.shape))
    neighbour = place[:main_axis] + [(place[main_axis] + 1) % drawn.shape[main_axis]] + place[main_axis + 1:]
    return drawn.at[tuple(place)].set(least).at[tuple(neighbour)].set(high)


def levels(key, shape, cuts, least, high):
    loudness, own = 1.0, jax.random.fold_in(key, 6)
    for position, shards_of in cuts:
        steps = jnp.exp(jax.random.uniform(jax.random.fold_in(own, position), (shards_of,), jnp.float32, least / len(cuts), high / len(cuts)))
        loudness = loudness * jnp.repeat(steps, shape[position] // shards_of).reshape([-1 if axis == position else 1 for axis in range(len(shape))])
    return loudness


def routed_block(rng, own, number, rows, amount, top, reach, skew):
    ranking = jax.random.permutation(rng, amount)
    heavy_load, ordinary = load_shares(amount, rows * top, reach, skew, True), load_shares(amount, rows * top, reach, skew, False)
    places = jnp.arange(amount)

    def named(sizes, offset_by):
        used = int((sizes > 0).sum())
        fixed = max(1, used // 4)
        passed = fixed + (places - fixed + offset_by * (used - fixed)) % max(1, amount - fixed)
        return jnp.zeros((amount,), jnp.int32).at[ranking[jnp.where(places < fixed, places, passed)]].set(jnp.asarray(sizes, jnp.int32))

    sizes = jnp.where(number % 4 == 0, named(heavy_load, number // 4), named(ordinary, number - number // 4 - 1))
    mixed = jax.random.permutation(jax.random.fold_in(own, 3), amount)
    source_of, sink = mixed[0:amount // 2 * 2:2], mixed[1:amount // 2 * 2:2]
    slack = jnp.minimum(sizes[source_of] - 1, reach - sizes[sink]) // 2
    slack = jnp.where((source_of == ranking[0]) | (sink == ranking[0]) | (sizes[sink] == 0), 0, jnp.maximum(slack, 0))
    passed = jax.random.randint(jax.random.fold_in(own, 4), (amount // 2,), 0, 1 << 20) % (slack + 1)
    sizes = sizes.at[source_of].add(-passed).at[sink].add(passed)
    items = jnp.searchsorted(jnp.cumsum(sizes), jnp.arange(rows * top), side="right").astype(jnp.int32)
    grid = items.reshape(top, rows).T
    grid = grid[jax.random.permutation(jax.random.fold_in(own, 1), rows)]
    offset_by = jax.random.randint(jax.random.fold_in(own, 2), (rows, 1), 0, top)
    return jnp.take_along_axis(grid, (jnp.arange(top)[None, :] + offset_by) % top, axis=1)


def load_shares(count, total, most, slope, full):
    portions = [(1 << 20) // math.isqrt(standing ** slope) + 1 for standing in range(1, count + 1)]
    largest = most if full else min(most, max(-(-total // count), total * portions[0] // sum(portions)))
    least = 1 if total - largest >= count - 1 else 0
    given, surplus = [largest] + [least] * (count - 1), total - largest - least * (count - 1)
    while surplus > 0:
        free = [i for i in range(1, count) if given[i] < largest] or [i for i in range(1, count) if given[i] < most]
        mass, left = sum([portions[i] for i in free]), surplus
        for i in free:
            addition = min(most - given[i], max(1, left * portions[i] // mass), surplus)
            given[i] = given[i] + addition
            surplus = surplus - addition
    return np.array(given)


def noise(stream_key, shape, spread, bound, pieces=(), kind=jnp.bfloat16):
    loudness = levels(stream_key, shape, pieces, -0.22, 0.18) if pieces else 1.0
    entries = jax.random.normal(stream_key, shape, jnp.float32) * spread * loudness
    return jnp.minimum(jnp.maximum(entries, -bound), bound).astype(kind)


def setup_inputs(seed: int = 0) -> dict:
    key_of = jax.random.split(jax.random.key(seed), 6)
    patches = draw_patches(jax.random.fold_in(key_of[5], 71), 0)
    peak_offsets = with_ends(jax.random.randint(key_of[1], (SECTIONS, NODES, 2), -4, 5), jax.random.fold_in(key_of[1], 1), -4, 4).astype(jnp.int32)
    tiles = noise(key_of[2], (SECTIONS, TILES, TL, TL), 1.0, 6.0, ((0, 16), (1, 32)))
    band_offsets = with_ends(jax.random.randint(key_of[3], (SECTIONS, TILES, 2), -3, 4), jax.random.fold_in(key_of[3], 1), -3, 3).astype(jnp.int32)
    routes_keys = jax.random.split(jax.random.fold_in(key_of[4], 1), SECTIONS * (TILES * PIECES) // (NT * PIECES))
    routes_turns = jax.random.permutation(jax.random.fold_in(key_of[4], 3), SECTIONS * (TILES * PIECES) // (NT * PIECES))
    routes = jax.vmap(lambda own, number: routed_block(jax.random.fold_in(key_of[4], 2), own, number, NT * PIECES, GROUPS, 1, MOST, 2))(routes_keys, routes_turns).reshape((SECTIONS, TILES * PIECES, 1))
    return {"patches": patches, "peak_offsets": peak_offsets, "tiles": tiles, "band_offsets": band_offsets, "routes": routes}


EPSILON = 1e-06
STEP_SIZE = 0.25
ANCHOR_WEIGHT = 0.5
MIP_SCALE = 0.0625
SCORE_GAIN = 6.0

def centroid(correlation, energy_now, energy_low, offsets):
    extent = correlation.shape[-1]
    scores = SCORE_GAIN / extent * correlation / jnp.sqrt(energy_now * energy_low + EPSILON)[:, None, None]
    half_extent = extent // 2
    offset_grid = jnp.arange(extent, dtype=jnp.int32)
    relative_y = jnp.mod(offset_grid[None, :] - offsets[:, 0:1] + half_extent, extent) - half_extent
    relative_x = jnp.mod(offset_grid[None, :] - offsets[:, 1:2] + half_extent, extent) - half_extent
    inside_y = (relative_y >= -(extent // 4)) & (relative_y < extent // 4)
    inside_x = (relative_x >= -(extent // 4)) & (relative_x < extent // 4)
    in_window = inside_y[:, :, None] & inside_x[:, None, :]
    masked = jnp.where(in_window, scores, -jnp.inf)
    peak_score = lax.optimization_barrier(jnp.max(masked, axis=(1, 2), keepdims=True))
    weights = jnp.exp(masked - peak_score)
    weight_sum = lax.optimization_barrier(jnp.sum(weights, axis=(1, 2)))
    centre_y = lax.optimization_barrier(jnp.sum(weights * relative_y[:, :, None].astype(jnp.float32), axis=(1, 2))) / weight_sum
    centre_x = lax.optimization_barrier(jnp.sum(weights * relative_x[:, None, :].astype(jnp.float32), axis=(1, 2))) / weight_sum
    flow_y = offsets[:, 0].astype(jnp.float32) + centre_y
    flow_x = offsets[:, 1].astype(jnp.float32) + centre_x
    return jnp.stack([flow_y, flow_x], 0)

def band_taps(residual):
    tap_offsets = jnp.arange(-BAND, BAND + 1).astype(jnp.float32)
    raw_weights = 1.0 / (1.0 + (tap_offsets - residual) ** 2)
    return raw_weights / jnp.sum(raw_weights)

def band_matrix(residual, offset, tile_edge):
    tap_values = band_taps(residual).astype(jnp.bfloat16)
    row_index = jnp.arange(tile_edge, dtype=jnp.int32)[:, None]
    col_index = jnp.arange(tile_edge, dtype=jnp.int32)[None, :]
    band_index = col_index - row_index - offset + BAND
    matrix = jnp.zeros((tile_edge, tile_edge), jnp.bfloat16)
    for tap_index in range(2 * BAND + 1):
        matrix = jnp.where(band_index == tap_index, tap_values[tap_index], matrix)
    return matrix

def reference(patches, peak_offsets, tiles, band_offsets, routes):
    previous = jnp.concatenate([jnp.zeros_like(patches[:1]), patches[:-1]], 0)

    def section_flows(operands):
        current, lower_patch, offsets = operands
        current = current.astype(jnp.float32)
        lower_patch = lower_patch.astype(jnp.float32)
        energy_now = lax.optimization_barrier(jnp.mean(current * current, axis=(1, 2)))
        energy_low = lax.optimization_barrier(jnp.mean(lower_patch * lower_patch, axis=(1, 2)))
        spectrum = jnp.fft.fft2(current) * jnp.conj(jnp.fft.fft2(lower_patch))
        correlation = jnp.real(jnp.fft.ifft2(spectrum)).astype(jnp.float32)
        return centroid(correlation, energy_now, energy_low, offsets)
    flow_field = lax.map(section_flows, (patches, previous, peak_offsets))
    positions = jnp.cumsum(flow_field, axis=0)
    section_index = jnp.arange(SECTIONS)[:, None, None]
    empty = jnp.zeros_like(flow_field[:1])
    flow_above = jnp.concatenate([flow_field[1:], empty], 0)
    for sweep in range(RELAX):
        below = jnp.concatenate([empty, positions[:-1]], 0)
        above = jnp.concatenate([positions[1:], empty], 0)
        lower_term = jnp.where(section_index > 0, below + flow_field - positions, 0.0)
        upper_term = jnp.where(section_index < SECTIONS - 1, above - flow_above - positions, 0.0)
        positions = positions + STEP_SIZE * (lower_term + upper_term - ANCHOR_WEIGHT * positions)
    shifts = MIP_SCALE * lax.optimization_barrier(jnp.mean(positions.reshape(SECTIONS, 2, TILES, NP // NT), axis=3))

    def section_render(operands):
        section_tiles, section_shifts, section_bands, section_routes = operands

        def render(items):
            tile_image, shift_y, shift_x, band_y, band_x = items
            col_band = band_matrix(shift_x - band_x.astype(jnp.float32), band_x, TL)
            row_band = band_matrix(shift_y - band_y.astype(jnp.float32), band_y, TL)
            first_pass = jnp.dot(tile_image, col_band.T, preferred_element_type=jnp.float32).astype(jnp.bfloat16)
            return jnp.dot(row_band, first_pass, preferred_element_type=jnp.float32).astype(jnp.bfloat16)
        rendered_tiles = lax.map(render, (section_tiles, section_shifts[0], section_shifts[1], section_bands[:, 0], section_bands[:, 1]))
        piece_rows = rendered_tiles.reshape(TILES * PIECES, TL // PIECES * TL).astype(jnp.float32)
        piece_index = jnp.arange(TILES * PIECES, dtype=jnp.int32) % PIECES
        segment = section_routes[:, 0] * PIECES + piece_index
        group_sums = jax.ops.segment_sum(piece_rows, segment, GROUPS * PIECES)
        group_counts = jax.ops.segment_sum(jnp.ones((TILES * PIECES,), jnp.float32), segment, GROUPS * PIECES)
        averaged = group_sums / jnp.maximum(group_counts, 1.0)[:, None]
        return averaged.astype(jnp.bfloat16).reshape(GROUPS, TL, TL)
    rendered = lax.map(section_render, (tiles, shifts, band_offsets, routes))
    return (positions, rendered)
```

```python
import functools
import math

import jax
import jax.numpy as jnp
import numpy as np
from jax import lax
from jax.experimental import pallas as pl
from jax.experimental.pallas import tpu as pltpu
from jax.sharding import PartitionSpec as P

PIECES = 32
BAND = 6
RELAX = 3
EPSILON = 1e-06
STEP_SIZE = 0.25
ANCHOR_WEIGHT = 0.5
MIP_SCALE = 0.0625
SCORE_GAIN = 6.0

EXTENT = 128
HALF = 72
REACH = 40
BF = jnp.bfloat16
F32 = jnp.float32


def high_low(table):
    high = table.astype(jnp.bfloat16)
    low = (table - high.astype(np.float64)).astype(jnp.bfloat16)
    return high, low


def dft_constants():
    line = np.arange(EXTENT)
    phase = 2.0 * np.pi * ((line[:, None] * line[None, :]) % EXTENT) / EXTENT
    cos, sin = np.cos(phase), np.sin(phase)
    first = np.concatenate([cos[:HALF], sin[:HALF]], 0)
    first = np.concatenate(high_low(first), 1)
    second_high, second_low = high_low(np.concatenate([cos, sin], 1))
    second = np.concatenate([second_high, second_high, second_low], 0)
    third_high, third_low = high_low(np.block([[cos, sin], [-sin, cos]]))
    third = np.concatenate([third_high, third_high, third_low], 0)
    weight = np.where(line[:HALF] <= EXTENT // 2, 2.0, 0.0)
    weight[0] = weight[EXTENT // 2] = 1.0
    rows = (np.arange(-REACH, REACH) % EXTENT)[:, None]
    angle = 2.0 * np.pi * ((rows * line[None, :HALF]) % EXTENT) / EXTENT
    fourth = np.concatenate([weight * np.cos(angle), -weight * np.sin(angle)], 1)
    fourth_high, fourth_low = high_low(fourth / float(EXTENT * EXTENT))
    fourth = np.concatenate([fourth_high, fourth_high, fourth_low], 1)
    return first, second, third, fourth


def relaxation_map(sections):
    flow = np.eye(sections)
    positions = np.tril(np.ones((sections, sections)))
    for _ in range(RELAX):
        lower = np.zeros_like(positions)
        upper = np.zeros_like(positions)
        lower[1:] = positions[:-1] + flow[1:] - positions[1:]
        upper[:-1] = positions[1:] - flow[1:] - positions[:-1]
        positions = positions + STEP_SIZE * (lower + upper - ANCHOR_WEIGHT * positions)
    return positions.astype(np.float32)


def split(value):
    high = value.astype(BF)
    return high, (value - high.astype(F32)).astype(BF)


def dot(a, b):
    return jnp.dot(a, b, preferred_element_type=F32)


def flow_kernel(peak_ref, now_ref, low_ref, first_ref, second_ref, third_ref, fourth_ref, out_ref):
    count = now_ref.shape[0]
    correlations = []
    for pair in range(count // 2):
        halves = []
        for ref in (now_ref, low_ref):
            both = jnp.concatenate([ref[2 * pair], ref[2 * pair + 1]], 1)
            lines = dot(first_ref[...], jnp.concatenate([both, both], 0))
            halves += [lines[:, :EXTENT], lines[:, EXTENT:]]
        high, low = split(jnp.concatenate(halves, 0))
        spectra = dot(jnp.concatenate([high, low, high], 1), second_ref[...])
        parts = []
        for k in range(4):
            a = spectra[2 * HALF * k : 2 * HALF * k + HALF]
            b = spectra[2 * HALF * k + HALF : 2 * HALF * (k + 1)]
            parts.append(
                (a[:, :EXTENT] - b[:, EXTENT:], -(a[:, EXTENT:] + b[:, :EXTENT]))
            )
        crosses = []
        for k in range(2):
            (nr, ni), (lr, li) = parts[k], parts[k + 2]
            crosses.append(jnp.concatenate([nr * lr + ni * li, ni * lr - nr * li], 1))
        high, low = split(jnp.concatenate(crosses, 0))
        outer = dot(jnp.concatenate([high, low, high], 1), third_ref[...])
        columns = []
        for k in range(2):
            block = outer[HALF * k : HALF * (k + 1)]
            columns.append(jnp.concatenate([block[:, :EXTENT], block[:, EXTENT:]], 0))
        high, low = split(jnp.concatenate(columns, 1))
        result = dot(fourth_ref[...], jnp.concatenate([high, low, high], 0))
        correlations += [result[:, :EXTENT], result[:, EXTENT:]]

    def energy(ref):
        rows = []
        for n in range(count):
            value = ref[n].astype(F32)
            rows.append(jnp.sum(value * value, axis=0, keepdims=True))
        total = jnp.sum(jnp.concatenate(rows, 0), axis=1, keepdims=True)
        return total * (1.0 / (EXTENT * EXTENT))

    scale = (SCORE_GAIN / EXTENT) / jnp.sqrt(energy(now_ref) * energy(low_ref) + EPSILON)
    shape = (2 * REACH, EXTENT)
    row = lax.broadcasted_iota(jnp.int32, shape, 0) - REACH
    column = lax.broadcasted_iota(jnp.int32, shape, 1)
    scores, relatives, tops = [], [], []
    for n in range(count):
        rel_y = row - peak_ref[n, 0]
        rel_x = ((column - peak_ref[n, 1] + EXTENT // 2) & (EXTENT - 1)) - EXTENT // 2
        quarter = EXTENT // 4
        inside = (rel_y >= -quarter) & (rel_y < quarter) & (rel_x >= -quarter) & (rel_x < quarter)
        score = jnp.where(inside, correlations[n] * scale[n : n + 1], -1e30)
        scores.append(score)
        relatives.append((rel_y.astype(F32), rel_x[:1].astype(F32)))
        tops.append(jnp.max(score, axis=0, keepdims=True))
    top = jnp.max(jnp.concatenate(tops, 0), axis=1, keepdims=True)
    sums, sums_y, sums_x = [], [], []
    for n in range(count):
        weight = jnp.exp(scores[n] - top[n : n + 1])
        rel_y, rel_x = relatives[n]
        along = jnp.sum(weight, axis=0, keepdims=True)
        sums.append(along)
        sums_y.append(jnp.sum(weight * rel_y, axis=0, keepdims=True))
        sums_x.append(along * rel_x)
    total, total_y, total_x = (
        jnp.sum(jnp.concatenate(s, 0), axis=1, keepdims=True) for s in (sums, sums_y, sums_x)
    )
    node = lax.broadcasted_iota(jnp.int32, (count, EXTENT), 0)
    lane = lax.broadcasted_iota(jnp.int32, (count, EXTENT), 1)
    peak_y = jnp.zeros((count, EXTENT), jnp.int32)
    peak_x = jnp.zeros((count, EXTENT), jnp.int32)
    for n in range(count):
        peak_y = jnp.where(node == n, peak_ref[n, 0], peak_y)
        peak_x = jnp.where(node == n, peak_ref[n, 1], peak_x)
    flow_y = peak_y.astype(F32) + total_y / total
    flow_x = peak_x.astype(F32) + total_x / total
    flow = jnp.where(lane == 0, flow_y, jnp.where(lane == 1, flow_x, 0.0))
    out_ref[...] = jnp.broadcast_to(flow[None], out_ref.shape)


def fill_band(target_ref, residual, offset, sub_sign):
    block = 128
    lane = lax.broadcasted_iota(jnp.int32, (1, block), 1)
    tap = (lane - BAND).astype(F32) - residual
    raw = jnp.where(lane <= 2 * BAND, 1.0 / (1.0 + tap * tap), 0.0)
    norm = jnp.sum(raw, axis=1, keepdims=True)
    a = lax.broadcasted_iota(jnp.int32, (block, block), 0)
    b = lax.broadcasted_iota(jnp.int32, (block, block), 1)
    d = sub_sign * (a - b) - offset
    k = ((d + block // 2) & (block - 1)) - block // 2
    away = k.astype(F32) - residual
    value = (1.0 / (1.0 + away * away)) / norm
    blocks = {}
    for step in (-1, 0, 1):
        near = jnp.abs(d + sub_sign * step * block) <= BAND
        blocks[step] = jnp.where(near, value, 0.0).astype(BF)
    zero = jnp.zeros((block, block), BF)
    count = target_ref.shape[0] // block
    for i in range(count):
        for j in range(count):
            target_ref[i * block : (i + 1) * block, j * block : (j + 1) * block] = blocks.get(
                i - j, zero
            )


def render_kernel(map_ref, band_ref, flow_ref, tile_ref, position_ref, send_ref, col_ref, row_ref, pass_ref):
    sections, nodes, _ = flow_ref.shape
    tile_count, edge, _ = tile_ref.shape
    position = jnp.zeros(flow_ref.shape[1:], F32)
    for s in range(sections):
        position = position + map_ref[0, s] * flow_ref[s]
    position_ref[...] = position
    per_tile = nodes // tile_count
    height = edge // PIECES
    chunk = 128
    for t in range(tile_count):
        mean = jnp.sum(position[t * per_tile : (t + 1) * per_tile], axis=0, keepdims=True)
        shift = (MIP_SCALE / per_tile) * mean
        offset_y, offset_x = band_ref[t, 0], band_ref[t, 1]
        fill_band(col_ref, shift[:, 1:2] - offset_x.astype(F32), offset_x, 1)
        fill_band(row_ref, shift[:, 0:1] - offset_y.astype(F32), offset_y, -1)
        for c in range(edge // chunk):
            rows = slice(c * chunk, (c + 1) * chunk)
            pass_ref[rows, :] = dot(tile_ref[t, rows, :], col_ref[...]).astype(BF)
        for c in range(edge // chunk):
            rows = slice(c * chunk, (c + 1) * chunk)
            done = dot(row_ref[rows, :], pass_ref[...]).astype(BF)
            send_ref[c * chunk // height : (c + 1) * chunk // height, t * height : (t + 1) * height, :] = (
                done.reshape(chunk // height, height, edge)
            )


def gather_kernel(label_ref, inverse_ref, piece_ref, out_ref, total_ref):
    owners, rows, _ = piece_ref.shape
    groups, height, _ = total_ref.shape
    total_ref[...] = jnp.zeros(total_ref.shape, F32)
    per_owner = rows // height

    def add(owner, carry):
        for t in range(per_owner):
            group = label_ref[owner, t]
            piece = piece_ref[owner, t * height : (t + 1) * height, :].astype(F32)
            total_ref[group] = total_ref[group] + piece
        return carry

    lax.fori_loop(0, owners, add, 0)
    share = groups // owners

    def finish(owner, carry):
        for t in range(share):
            value = total_ref[owner * share + t] * inverse_ref[owner, t]
            out_ref[owner, t * height : (t + 1) * height, :] = value.astype(BF)
        return carry

    lax.fori_loop(0, owners, finish, 0)


def in_vmem():
    return pl.BlockSpec(memory_space=pltpu.VMEM)


def in_smem():
    return pl.BlockSpec(memory_space=pltpu.SMEM)


def params():
    return pltpu.CompilerParams(vmem_limit_bytes=40 * 1024 * 1024)


def exchange(value, axis):
    return lax.all_to_all(value, axis, split_axis=0, concat_axis=0, tiled=True)


def body(patches, peak_offsets, tiles, band_offsets, routes):
    sections = lax.axis_size("gz")
    owners = lax.axis_size("xy")
    section = lax.axis_index("gz")
    tile_count, edge = tiles.shape[1], tiles.shape[-1]
    height = edge // PIECES
    groups = 2 * owners

    below = lax.ppermute(patches, "gz", [(i, i + 1) for i in range(sections - 1)])
    label = routes[0, :, 0].reshape(tile_count, PIECES).T.astype(F32)
    label = jnp.pad(label, ((0, 0), (0, EXTENT - tile_count)))[:, None, :]
    label = exchange(label, "xy")[:, 0, :tile_count].astype(jnp.int32)
    match = label.reshape(-1)[:, None] == jnp.arange(groups, dtype=jnp.int32)[None, :]
    inverse = 1.0 / jnp.maximum(jnp.sum(match.astype(F32), axis=0), 1.0)
    inverse = inverse.reshape(owners, groups // owners)

    tables = [jnp.asarray(t) for t in dft_constants()]
    count = patches.shape[1]
    flow = pl.pallas_call(
        flow_kernel,
        out_shape=jax.ShapeDtypeStruct((sections, count, EXTENT), F32),
        in_specs=[in_smem()] + [in_vmem()] * 6,
        out_specs=in_vmem(),
        compiler_params=params(),
        name="flow",
    )(peak_offsets[0], patches[0], below[0], *tables)
    flow = exchange(flow, "gz")

    linear = lax.dynamic_slice_in_dim(jnp.asarray(relaxation_map(sections)), section, 1, 0)
    position, pieces = pl.pallas_call(
        render_kernel,
        out_shape=(
            jax.ShapeDtypeStruct((count, EXTENT), F32),
            jax.ShapeDtypeStruct((PIECES, tile_count * height, edge), BF),
        ),
        in_specs=[in_smem(), in_smem(), in_vmem(), in_vmem()],
        out_specs=(in_vmem(), in_vmem()),
        scratch_shapes=[pltpu.VMEM((edge, edge), BF)] * 3,
        compiler_params=params(),
        name="render",
    )(linear, band_offsets[0], flow, tiles[0])
    pieces = exchange(pieces, "xy")

    cells = pl.pallas_call(
        gather_kernel,
        out_shape=jax.ShapeDtypeStruct((owners, groups // owners * height, edge), BF),
        in_specs=[in_smem(), in_smem(), in_vmem()],
        out_specs=in_vmem(),
        scratch_shapes=[pltpu.VMEM((groups, height, edge), F32)],
        compiler_params=params(),
        name="gather",
    )(label, inverse, pieces)
    cells = exchange(cells, "xy")
    rendered = cells.reshape(PIECES, groups // owners, height, edge).transpose(1, 0, 2, 3)
    rendered = rendered.reshape(1, groups // owners, edge, edge)
    return position[:, :2].T[None], rendered


def solution(mesh):
    placed = (
        P("gz", "xy", None, None),
        P("gz", "xy", None),
        P("gz", "xy", None, None),
        P("gz", "xy", None),
        P("gz", "xy", None),
    )
    return jax.shard_map(
        body,
        mesh=mesh,
        in_specs=placed,
        out_specs=(P("gz", None, "xy"), P("gz", "xy", None, None)),
        check_vma=False,
    )
```

```python
import jax
import jax.numpy as jnp
import numpy as np
from jax import lax
from jax.experimental import pallas as pl
from jax.experimental.pallas import tpu as pltpu
from jax.sharding import PartitionSpec as P

PIECES = 32
BAND = 6
RELAX = 3
EPSILON = 1e-06
STEP_SIZE = 0.25
ANCHOR_WEIGHT = 0.5
MIP_SCALE = 0.0625
SCORE_GAIN = 6.0

EXTENT = 128
HALF = 72
REACH = 40
BF = jnp.bfloat16
F32 = jnp.float32


def high_low(table):
    high = table.astype(jnp.bfloat16)
    low = (table - high.astype(np.float64)).astype(jnp.bfloat16)
    return high, low


def dft_constants():
    line = np.arange(EXTENT)
    phase = 2.0 * np.pi * ((line[:, None] * line[None, :]) % EXTENT) / EXTENT
    cos, sin = np.cos(phase), np.sin(phase)
    first = np.concatenate([cos[:HALF], sin[:HALF]], 0)
    first = np.concatenate(high_low(first), 1)
    second_high, second_low = high_low(np.concatenate([cos, sin], 1))
    second = np.concatenate([second_high, second_high, second_low], 0)
    third_high, third_low = high_low(np.block([[cos, sin], [-sin, cos]]))
    third = np.concatenate([third_high, third_high, third_low], 0)
    weight = np.where(line[:HALF] <= EXTENT // 2, 2.0, 0.0)
    weight[0] = weight[EXTENT // 2] = 1.0
    rows = (np.arange(-REACH, REACH) % EXTENT)[:, None]
    angle = 2.0 * np.pi * ((rows * line[None, :HALF]) % EXTENT) / EXTENT
    fourth = np.concatenate([weight * np.cos(angle), -weight * np.sin(angle)], 1)
    fourth_high, fourth_low = high_low(fourth / float(EXTENT * EXTENT))
    fourth = np.concatenate([fourth_high, fourth_high, fourth_low], 1)
    fourth = np.pad(fourth, ((0, 0), (0, 4 * EXTENT - fourth.shape[1])))
    parts = [first, second, third, fourth[:, : 2 * EXTENT], fourth[:, 2 * EXTENT :]]
    return np.concatenate(parts, 0)


def relaxation_map(sections):
    flow = np.eye(sections)
    positions = np.tril(np.ones((sections, sections)))
    for _ in range(RELAX):
        lower = np.zeros_like(positions)
        upper = np.zeros_like(positions)
        lower[1:] = positions[:-1] + flow[1:] - positions[1:]
        upper[:-1] = positions[1:] - flow[1:] - positions[:-1]
        positions = positions + STEP_SIZE * (lower + upper - ANCHOR_WEIGHT * positions)
    line = np.arange(sections)
    by_distance = positions[line[:, None], line[:, None] ^ line[None, :]]
    table = np.zeros((sections, EXTENT), np.float32)
    table[:, : 2 * sections] = np.repeat(by_distance, 2, axis=1)
    return table


def split(value):
    high = value.astype(BF)
    return high, (value - high.astype(F32)).astype(BF)


def dot(a, b):
    return jnp.dot(a, b, preferred_element_type=F32)


def flow_kernel(peak_ref, now_ref, low_ref, table_ref, out_ref):
    count = now_ref.shape[0]
    ends = np.cumsum([0, 2 * HALF, 3 * EXTENT, 6 * EXTENT, 2 * REACH, 2 * REACH])
    first_ref, second_ref, third_ref, left_ref, right_ref = (
        table_ref.at[int(a) : int(b)] for a, b in zip(ends[:-1], ends[1:])
    )
    fourth = jnp.concatenate([left_ref[...], right_ref[:, : 6 * HALF - 2 * EXTENT]], 1)
    correlations = []
    for pair in range(count // 2):
        halves = []
        for ref in (now_ref, low_ref):
            both = jnp.concatenate([ref[2 * pair], ref[2 * pair + 1]], 1)
            lines = dot(first_ref[...], jnp.concatenate([both, both], 0))
            halves += [lines[:, :EXTENT], lines[:, EXTENT:]]
        high, low = split(jnp.concatenate(halves, 0))
        spectra = dot(jnp.concatenate([high, low, high], 1), second_ref[...])
        parts = []
        for k in range(4):
            a = spectra[2 * HALF * k : 2 * HALF * k + HALF]
            b = spectra[2 * HALF * k + HALF : 2 * HALF * (k + 1)]
            parts.append(
                (a[:, :EXTENT] - b[:, EXTENT:], -(a[:, EXTENT:] + b[:, :EXTENT]))
            )
        crosses = []
        for k in range(2):
            (nr, ni), (lr, li) = parts[k], parts[k + 2]
            crosses.append(jnp.concatenate([nr * lr + ni * li, ni * lr - nr * li], 1))
        high, low = split(jnp.concatenate(crosses, 0))
        outer = dot(jnp.concatenate([high, low, high], 1), third_ref[...])
        columns = []
        for k in range(2):
            block = outer[HALF * k : HALF * (k + 1)]
            columns.append(jnp.concatenate([block[:, :EXTENT], block[:, EXTENT:]], 0))
        high, low = split(jnp.concatenate(columns, 1))
        result = dot(fourth, jnp.concatenate([high, low, high], 0))
        correlations += [result[:, :EXTENT], result[:, EXTENT:]]

    def energy(ref):
        rows = []
        for n in range(count):
            value = ref[n].astype(F32)
            rows.append(jnp.sum(value * value, axis=0, keepdims=True))
        total = jnp.sum(jnp.concatenate(rows, 0), axis=1, keepdims=True)
        return total * (1.0 / (EXTENT * EXTENT))

    scale = (SCORE_GAIN / EXTENT) / jnp.sqrt(energy(now_ref) * energy(low_ref) + EPSILON)
    shape = (2 * REACH, EXTENT)
    row = lax.broadcasted_iota(jnp.int32, shape, 0) - REACH
    column = lax.broadcasted_iota(jnp.int32, shape, 1)
    scores, relatives, tops = [], [], []
    for n in range(count):
        rel_y = row - peak_ref[n, 0]
        rel_x = ((column - peak_ref[n, 1] + EXTENT // 2) & (EXTENT - 1)) - EXTENT // 2
        quarter = EXTENT // 4
        inside = (rel_y >= -quarter) & (rel_y < quarter) & (rel_x >= -quarter) & (rel_x < quarter)
        score = jnp.where(inside, correlations[n] * scale[n : n + 1], -1e30)
        scores.append(score)
        relatives.append((rel_y.astype(F32), rel_x[:1].astype(F32)))
        tops.append(jnp.max(score, axis=0, keepdims=True))
    top = jnp.max(jnp.concatenate(tops, 0), axis=1, keepdims=True)
    sums, sums_y, sums_x = [], [], []
    for n in range(count):
        weight = jnp.exp(scores[n] - top[n : n + 1])
        rel_y, rel_x = relatives[n]
        along = jnp.sum(weight, axis=0, keepdims=True)
        sums.append(along)
        sums_y.append(jnp.sum(weight * rel_y, axis=0, keepdims=True))
        sums_x.append(along * rel_x)
    total, total_y, total_x = (
        jnp.sum(jnp.concatenate(s, 0), axis=1, keepdims=True) for s in (sums, sums_y, sums_x)
    )
    node = lax.broadcasted_iota(jnp.int32, (count, EXTENT), 0)
    lane = lax.broadcasted_iota(jnp.int32, (count, EXTENT), 1)
    peak_y = jnp.zeros((count, EXTENT), jnp.int32)
    peak_x = jnp.zeros((count, EXTENT), jnp.int32)
    for n in range(count):
        peak_y = jnp.where(node == n, peak_ref[n, 0], peak_y)
        peak_x = jnp.where(node == n, peak_ref[n, 1], peak_x)
    flow_y = peak_y.astype(F32) + total_y / total
    flow_x = peak_x.astype(F32) + total_x / total
    out_ref[...] = jnp.where(lane == 0, flow_y, jnp.where(lane == 1, flow_x, 0.0))


def taps(residual):
    lane = lax.broadcasted_iota(jnp.int32, (1, EXTENT), 1)
    away = (lane - BAND).astype(F32) - residual
    raw = jnp.where(lane <= 2 * BAND, 1.0 / (1.0 + away * away), 0.0)
    norm = jnp.sum(raw, axis=1, keepdims=True)
    return raw / norm, norm


def fill_band(target_ref, residual, offset, sub_sign):
    block = 128
    _, norm = taps(residual)
    a = lax.broadcasted_iota(jnp.int32, (block, block), 0)
    b = lax.broadcasted_iota(jnp.int32, (block, block), 1)
    d = sub_sign * (a - b) - offset
    k = ((d + block // 2) & (block - 1)) - block // 2
    away = k.astype(F32) - residual
    value = (1.0 / (1.0 + away * away)) / norm
    blocks = {}
    for step in (-1, 0, 1):
        near = jnp.abs(d + sub_sign * step * block) <= BAND
        blocks[step] = jnp.where(near, value, 0.0).astype(BF)
    zero = jnp.zeros((block, block), BF)
    count = target_ref.shape[0] // block
    for i in range(count):
        for j in range(count):
            target_ref[i * block : (i + 1) * block, j * block : (j + 1) * block] = blocks.get(
                i - j, zero
            )


def early_kernel(band_ref, route_ref, tile_ref, send_ref):
    slots, rows, edge = send_ref.shape
    height = edge // slots
    wide = height + 2 * BAND
    per_chunk = 128 // rows
    offset_y, offset_x = band_ref[0, 0], band_ref[0, 1]
    lane = lax.broadcasted_iota(jnp.int32, (slots, EXTENT), 1)
    info = jnp.where(
        lane == 0,
        route_ref[:slots, :],
        jnp.where(lane == 1, route_ref[slots : 2 * slots, :], jnp.where(lane == 2, offset_x, 0)),
    )
    info = info.astype(F32).astype(BF)
    a = lax.broadcasted_iota(jnp.int32, (128, edge), 0)
    m = lax.broadcasted_iota(jnp.int32, (128, edge), 1)
    row = a & (rows - 1)
    source = jnp.where(row < wide, (a // rows) * height + row + offset_y - BAND, -edge)
    a = a[:, :slots]
    m_slot = m[:, :slots]
    for c in range(slots // per_chunk):
        pick = jnp.where(m == source + c * per_chunk * height, 1.0, 0.0).astype(BF)
        data = dot(pick, tile_ref[...])
        named = jnp.where(((a & (rows - 1)) == wide) & (a // rows + c * per_chunk == m_slot), 1.0, 0.0)
        left = data[:, :EXTENT] + dot(named.astype(BF), info)
        data = jnp.concatenate([left, data[:, EXTENT:]], 1).astype(BF)
        send_ref[c * per_chunk : (c + 1) * per_chunk] = data.reshape(per_chunk, rows, edge)


def late_kernel(band_ref, coef_ref, flow_ref, tile_ref, position_ref, send_ref, col_ref, row_ref, pass_ref):
    nodes = flow_ref.shape[0]
    edge = tile_ref.shape[0]
    slots = send_ref.shape[0]
    height = edge // slots
    lane = lax.broadcasted_iota(jnp.int32, flow_ref.shape, 1)
    terms = flow_ref[...] * coef_ref[...]
    odd = (lane & 1) == 1
    position_y = jnp.sum(jnp.where(odd, 0.0, terms), axis=1, keepdims=True)
    position_x = jnp.sum(jnp.where(odd, terms, 0.0), axis=1, keepdims=True)
    position_ref[...] = jnp.where(lane == 0, position_y, jnp.where(lane == 1, position_x, 0.0))

    def residuals(t):
        result = []
        for c, position in enumerate((position_y, position_x)):
            half = nodes // 2
            mean = jnp.sum(position[t * half : (t + 1) * half], axis=0, keepdims=True)
            result.append((MIP_SCALE / half) * mean - band_ref[t, c].astype(F32))
        return result

    residual_y, residual_x = residuals(1)
    fill_band(col_ref, residual_x, band_ref[1, 1], 1)
    fill_band(row_ref, residual_y, band_ref[1, 0], -1)
    chunk = 128
    for c in range(edge // chunk):
        rows = slice(c * chunk, (c + 1) * chunk)
        pass_ref[rows, :] = dot(tile_ref[rows, :], col_ref[...]).astype(BF)
    for c in range(edge // chunk):
        rows = slice(c * chunk, (c + 1) * chunk)
        first, last = c * chunk // height, (c + 1) * chunk // height
        done = dot(row_ref[rows, :], pass_ref[...]).astype(BF).reshape(last - first, height, edge)
        for j in range(edge // EXTENT):
            send_ref[first:last, j * height : (j + 1) * height, :] = done[
                :, :, j * EXTENT : (j + 1) * EXTENT
            ]
    residual_y, residual_x = residuals(0)
    sub = lax.broadcasted_iota(jnp.int32, (8, EXTENT), 0)
    tail = jnp.where(sub == 0, taps(residual_x)[0], jnp.where(sub == 1, taps(residual_y)[0], 0.0))
    first = height * edge // EXTENT
    send_ref[:, first : first + 8, :] = jnp.broadcast_to(tail.astype(BF)[None], (slots, 8, EXTENT))


def gather_kernel(info_ref, inverse_ref, raw_ref, late_ref, out_ref, total_ref):
    owners, rows, edge = raw_ref.shape
    groups, height, _ = total_ref.shape
    total_ref[...] = jnp.zeros(total_ref.shape, F32)
    blocks = edge // EXTENT
    tail = height * blocks
    batch = 2 * EXTENT // rows
    for start in range(0, owners, batch):
        bands, columns = [], []
        for d in range(start, start + batch):
            info = late_ref[d, tail : tail + 8, :].astype(F32)
            columns.append(info[0:1])
            place = d - start
            band = pltpu.roll(
                jnp.broadcast_to(info[1:2], (height, EXTENT)),
                place % (batch // 2) * rows,
                1,
                stride=1,
                stride_axis=0,
            )
            empty = jnp.zeros_like(band)
            bands.append(
                jnp.concatenate([band, empty] if place < batch // 2 else [empty, band], 1)
            )
        raw = raw_ref[start : start + batch].reshape(batch * rows, edge)
        lines = dot(jnp.concatenate(bands, 0).astype(BF), raw).astype(BF).astype(F32)
        for d in range(start, start + batch):
            line = lines[(d - start) * height : (d - start + 1) * height]
            line = jnp.concatenate([line, jnp.zeros((height, EXTENT), F32)], 1)
            length = edge + EXTENT
            line = pltpu.roll(line, (length + BAND - info_ref[d, 2]) % length, 1)
            total = None
            for k in range(2 * BAND + 1):
                moved = line if k == 0 else pltpu.roll(line, length - k, 1)
                term = moved[:, :edge] * columns[d - start][:, k : k + 1]
                total = term if total is None else total + term
            group = info_ref[d, 0]
            total_ref[group] = total_ref[group] + total.astype(BF).astype(F32)
            group = info_ref[d, 1]
            for j in range(blocks):
                piece = late_ref[d, j * height : (j + 1) * height, :].astype(F32)
                lanes = slice(j * EXTENT, (j + 1) * EXTENT)
                total_ref[group, :, lanes] = total_ref[group, :, lanes] + piece
    share = groups // owners

    def finish(owner, carry):
        for t in range(share):
            value = total_ref[owner * share + t] * inverse_ref[owner, t]
            out_ref[owner, t * height : (t + 1) * height, :] = value.astype(BF)
        return carry

    lax.fori_loop(0, owners, finish, 0)


def in_vmem():
    return pl.BlockSpec(memory_space=pltpu.VMEM)


def in_smem():
    return pl.BlockSpec(memory_space=pltpu.SMEM)


def params():
    return pltpu.CompilerParams(vmem_limit_bytes=40 * 1024 * 1024)


def exchange(value, axis):
    return lax.all_to_all(value, axis, split_axis=0, concat_axis=0, tiled=True)


def body(patches, peak_offsets, tiles, band_offsets, routes):
    sections = lax.axis_size("gz")
    owners = lax.axis_size("xy")
    section = lax.axis_index("gz")
    edge = tiles.shape[-1]
    height = edge // PIECES
    groups = 2 * owners
    count = patches.shape[1]

    raw = pl.pallas_call(
        early_kernel,
        out_shape=jax.ShapeDtypeStruct((PIECES, 2 * height, edge), BF),
        in_specs=[in_smem(), in_vmem(), in_vmem()],
        out_specs=in_vmem(),
        compiler_params=params(),
        name="early",
    )(band_offsets[0], routes[0], tiles[0, 0])
    raw = exchange(raw, "xy")
    info = raw[:, height + 2 * BAND, :3].astype(jnp.int32)
    match = info[:, :2].reshape(-1)[:, None] == jnp.arange(groups, dtype=jnp.int32)[None, :]
    inverse = 1.0 / jnp.maximum(jnp.sum(match.astype(F32), axis=0), 1.0)
    inverse = inverse.reshape(owners, groups // owners)

    below = lax.ppermute(patches, "gz", [(i, i + 1) for i in range(sections - 1)])
    flow = pl.pallas_call(
        flow_kernel,
        out_shape=jax.ShapeDtypeStruct((count, EXTENT), F32),
        in_specs=[in_smem()] + [in_vmem()] * 3,
        out_specs=in_vmem(),
        compiler_params=params(),
        name="flow",
    )(peak_offsets[0], patches[0], below[0], jnp.asarray(dft_constants()))
    distance = 1
    while distance < sections:
        other = lax.ppermute(flow, "gz", [(i, i ^ distance) for i in range(sections)])
        flow = flow + jnp.pad(other[:, : EXTENT - 2 * distance], ((0, 0), (2 * distance, 0)))
        distance *= 2

    coef = lax.dynamic_slice_in_dim(jnp.asarray(relaxation_map(sections)), section, 1, 0)
    position, late = pl.pallas_call(
        late_kernel,
        out_shape=(
            jax.ShapeDtypeStruct((count, EXTENT), F32),
            jax.ShapeDtypeStruct((PIECES, height * edge // EXTENT + 8, EXTENT), BF),
        ),
        in_specs=[in_smem()] + [in_vmem()] * 3,
        out_specs=(in_vmem(), in_vmem()),
        scratch_shapes=[pltpu.VMEM((edge, edge), BF)] * 3,
        compiler_params=params(),
        name="late",
    )(band_offsets[0], coef, flow, tiles[0, 1])
    late = exchange(late, "xy")

    cells = pl.pallas_call(
        gather_kernel,
        out_shape=jax.ShapeDtypeStruct((owners, groups // owners * height, edge), BF),
        in_specs=[in_smem(), in_smem(), in_vmem(), in_vmem()],
        out_specs=in_vmem(),
        scratch_shapes=[pltpu.VMEM((groups, height, edge), F32)],
        compiler_params=params(),
        name="gather",
    )(info, inverse, raw, late)
    cells = exchange(cells, "xy")
    rendered = cells.reshape(PIECES, groups // owners, height, edge).transpose(1, 0, 2, 3)
    rendered = rendered.reshape(1, groups // owners, edge, edge)
    return position[:, :2].T[None], rendered


def solution(mesh):
    placed = (
        P("gz", "xy", None, None),
        P("gz", "xy", None),
        P("gz", "xy", None, None),
        P("gz", "xy", None),
        P("gz", "xy", None),
    )
    return jax.shard_map(
        body,
        mesh=mesh,
        in_specs=placed,
        out_specs=(P("gz", None, "xy"), P("gz", "xy", None, None)),
        check_vma=False,
    )
```

```python
import jax
import jax.numpy as jnp
import numpy as np
from jax import lax
from jax.experimental import pallas as pl
from jax.experimental.pallas import tpu as pltpu
from jax.sharding import PartitionSpec as P

PIECES = 32
BAND = 6
RELAX = 3
EPSILON = 1e-06
STEP_SIZE = 0.25
ANCHOR_WEIGHT = 0.5
MIP_SCALE = 0.0625
SCORE_GAIN = 6.0

EXTENT = 128
HALF = 72
REACH = 40
BF = jnp.bfloat16
F32 = jnp.float32


def high_low(table):
    high = table.astype(jnp.bfloat16)
    low = (table - high.astype(np.float64)).astype(jnp.bfloat16)
    return high, low


def dft_constants():
    line = np.arange(EXTENT)
    phase = 2.0 * np.pi * ((line[:, None] * line[None, :]) % EXTENT) / EXTENT
    cos, sin = np.cos(phase), np.sin(phase)
    first = np.concatenate([cos[:HALF], sin[:HALF]], 0)
    first = np.concatenate(high_low(first), 1)
    second_high, second_low = high_low(np.concatenate([cos, sin], 1))
    second = np.concatenate([second_high, second_high, second_low], 0)
    third_high, third_low = high_low(np.block([[cos, sin], [-sin, cos]]))
    third = np.concatenate([third_high, third_high, third_low], 0)
    weight = np.where(line[:HALF] <= EXTENT // 2, 2.0, 0.0)
    weight[0] = weight[EXTENT // 2] = 1.0
    rows = (np.arange(-REACH, REACH) % EXTENT)[:, None]
    angle = 2.0 * np.pi * ((rows * line[None, :HALF]) % EXTENT) / EXTENT
    fourth = np.concatenate([weight * np.cos(angle), -weight * np.sin(angle)], 1)
    fourth_high, fourth_low = high_low(fourth / float(EXTENT * EXTENT))
    fourth = np.concatenate([fourth_high, fourth_high, fourth_low], 1)
    fourth = np.pad(fourth, ((0, 0), (0, 4 * EXTENT - fourth.shape[1])))
    parts = [first, second, third, fourth[:, : 2 * EXTENT], fourth[:, 2 * EXTENT :]]
    return np.concatenate(parts, 0)


def relaxation_map(sections):
    flow = np.eye(sections)
    positions = np.tril(np.ones((sections, sections)))
    for _ in range(RELAX):
        lower = np.zeros_like(positions)
        upper = np.zeros_like(positions)
        lower[1:] = positions[:-1] + flow[1:] - positions[1:]
        upper[:-1] = positions[1:] - flow[1:] - positions[:-1]
        positions = positions + STEP_SIZE * (lower + upper - ANCHOR_WEIGHT * positions)
    return positions.astype(np.float32)


def split(value):
    high = value.astype(BF)
    return high, (value - high.astype(F32)).astype(BF)


def dot(a, b):
    return jnp.dot(a, b, preferred_element_type=F32)


def flow_kernel(peak_ref, now_ref, low_ref, table_ref, out_ref):
    count = now_ref.shape[0]
    ends = np.cumsum([0, 2 * HALF, 3 * EXTENT, 6 * EXTENT, 2 * REACH, 2 * REACH])
    first_ref, second_ref, third_ref, left_ref, right_ref = (
        table_ref.at[int(a) : int(b)] for a, b in zip(ends[:-1], ends[1:])
    )
    fourth = jnp.concatenate([left_ref[...], right_ref[:, : 6 * HALF - 2 * EXTENT]], 1)
    correlations = []
    for pair in range(count // 2):
        halves = []
        for ref in (now_ref, low_ref):
            both = jnp.concatenate([ref[2 * pair], ref[2 * pair + 1]], 1)
            lines = dot(first_ref[...], jnp.concatenate([both, both], 0))
            halves += [lines[:, :EXTENT], lines[:, EXTENT:]]
        high, low = split(jnp.concatenate(halves, 0))
        spectra = dot(jnp.concatenate([high, low, high], 1), second_ref[...])
        parts = []
        for k in range(4):
            a = spectra[2 * HALF * k : 2 * HALF * k + HALF]
            b = spectra[2 * HALF * k + HALF : 2 * HALF * (k + 1)]
            parts.append(
                (a[:, :EXTENT] - b[:, EXTENT:], -(a[:, EXTENT:] + b[:, :EXTENT]))
            )
        crosses = []
        for k in range(2):
            (nr, ni), (lr, li) = parts[k], parts[k + 2]
            crosses.append(jnp.concatenate([nr * lr + ni * li, ni * lr - nr * li], 1))
        high, low = split(jnp.concatenate(crosses, 0))
        outer = dot(jnp.concatenate([high, low, high], 1), third_ref[...])
        columns = []
        for k in range(2):
            block = outer[HALF * k : HALF * (k + 1)]
            columns.append(jnp.concatenate([block[:, :EXTENT], block[:, EXTENT:]], 0))
        high, low = split(jnp.concatenate(columns, 1))
        result = dot(fourth, jnp.concatenate([high, low, high], 0))
        correlations += [result[:, :EXTENT], result[:, EXTENT:]]

    def energy(ref):
        rows = []
        for n in range(count):
            value = ref[n].astype(F32)
            rows.append(jnp.sum(value * value, axis=0, keepdims=True))
        total = jnp.sum(jnp.concatenate(rows, 0), axis=1, keepdims=True)
        return total * (1.0 / (EXTENT * EXTENT))

    scale = (SCORE_GAIN / EXTENT) / jnp.sqrt(energy(now_ref) * energy(low_ref) + EPSILON)
    shape = (2 * REACH, EXTENT)
    row = lax.broadcasted_iota(jnp.int32, shape, 0) - REACH
    column = lax.broadcasted_iota(jnp.int32, shape, 1)
    scores, relatives, tops = [], [], []
    for n in range(count):
        rel_y = row - peak_ref[0, n]
        rel_x = ((column - peak_ref[1, n] + EXTENT // 2) & (EXTENT - 1)) - EXTENT // 2
        quarter = EXTENT // 4
        inside = (rel_y >= -quarter) & (rel_y < quarter) & (rel_x >= -quarter) & (rel_x < quarter)
        score = jnp.where(inside, correlations[n] * scale[n : n + 1], -1e30)
        scores.append(score)
        relatives.append((rel_y.astype(F32), rel_x[:1].astype(F32)))
        tops.append(jnp.max(score, axis=0, keepdims=True))
    top = jnp.max(jnp.concatenate(tops, 0), axis=1, keepdims=True)
    sums, sums_y, sums_x = [], [], []
    for n in range(count):
        weight = jnp.exp(scores[n] - top[n : n + 1])
        rel_y, rel_x = relatives[n]
        along = jnp.sum(weight, axis=0, keepdims=True)
        sums.append(along)
        sums_y.append(jnp.sum(weight * rel_y, axis=0, keepdims=True))
        sums_x.append(along * rel_x)
    total, total_y, total_x = (
        jnp.sum(jnp.concatenate(s, 0), axis=1, keepdims=True) for s in (sums, sums_y, sums_x)
    )
    node = lax.broadcasted_iota(jnp.int32, (count, EXTENT), 0)
    lane = lax.broadcasted_iota(jnp.int32, (count, EXTENT), 1)
    peak_y = jnp.zeros((count, EXTENT), jnp.int32)
    peak_x = jnp.zeros((count, EXTENT), jnp.int32)
    for n in range(count):
        peak_y = jnp.where(node == n, peak_ref[0, n], peak_y)
        peak_x = jnp.where(node == n, peak_ref[1, n], peak_x)
    flow_y = peak_y.astype(F32) + total_y / total
    flow_x = peak_x.astype(F32) + total_x / total
    flow = jnp.where(lane == 0, flow_y, jnp.where(lane == 1, flow_x, 0.0))
    out_ref[...] = jnp.broadcast_to(flow[None], out_ref.shape)


def fill_band(target_ref, residual, offset, sub_sign):
    block = EXTENT
    lane = lax.broadcasted_iota(jnp.int32, (1, block), 1)
    tap = (lane - BAND).astype(F32) - residual
    raw = jnp.where(lane <= 2 * BAND, 1.0 / (1.0 + tap * tap), 0.0)
    norm = jnp.sum(raw, axis=1, keepdims=True)
    a = lax.broadcasted_iota(jnp.int32, (block, block), 0)
    b = lax.broadcasted_iota(jnp.int32, (block, block), 1)
    d = sub_sign * (a - b) - offset
    k = ((d + block // 2) & (block - 1)) - block // 2
    away = k.astype(F32) - residual
    value = (1.0 / (1.0 + away * away)) / norm
    blocks = {}
    for step in (-1, 0, 1):
        near = jnp.abs(d + sub_sign * step * block) <= BAND
        blocks[step] = jnp.where(near, value, 0.0).astype(BF)
    zero = jnp.zeros((block, block), BF)
    count = target_ref.shape[0] // block
    for i in range(count):
        for j in range(count):
            target_ref[i * block : (i + 1) * block, j * block : (j + 1) * block] = blocks.get(
                i - j, zero
            )


def render_kernel(map_ref, band_ref, flow_ref, route_ref, tile_ref, position_ref, send_ref, col_ref, row_ref, pass_ref):
    sections, nodes, _ = flow_ref.shape
    tile_count, edge, _ = tile_ref.shape
    slots = send_ref.shape[0]
    section, owner = lax.axis_index("gz"), lax.axis_index("xy")
    position = jnp.zeros(flow_ref.shape[1:], F32)
    for s in range(sections):
        position = position + map_ref[section, s] * flow_ref[s]
    position_ref[...] = position
    per_tile = nodes // tile_count
    height = edge // slots
    columns = edge // EXTENT
    chunk = EXTENT
    for t in range(tile_count):
        mean = jnp.sum(position[t * per_tile : (t + 1) * per_tile], axis=0, keepdims=True)
        shift = (MIP_SCALE / per_tile) * mean
        offset_y, offset_x = band_ref[t, 0], band_ref[t, 1]
        fill_band(col_ref, shift[:, 1:2] - offset_x.astype(F32), offset_x, 1)
        fill_band(row_ref, shift[:, 0:1] - offset_y.astype(F32), offset_y, -1)
        for c in range(edge // chunk):
            rows = slice(c * chunk, (c + 1) * chunk)
            pass_ref[rows, :] = dot(tile_ref[t, rows, :], col_ref[...]).astype(BF)
        for c in range(edge // chunk):
            rows = slice(c * chunk, (c + 1) * chunk)
            first, last = c * chunk // height, (c + 1) * chunk // height
            done = dot(row_ref[rows, :], pass_ref[...]).astype(BF)
            done = done.reshape(last - first, height, edge)
            for j in range(columns):
                at = (t * columns + j) * height
                send_ref[first:last, at : at + height, :] = done[:, :, j * EXTENT : (j + 1) * EXTENT]
    lane = lax.broadcasted_iota(jnp.int32, (slots, tile_count * slots), 1)
    slot = lax.broadcasted_iota(jnp.int32, (slots, tile_count * slots), 0)
    names = jnp.broadcast_to(route_ref[...], lane.shape).astype(F32)
    place = lax.broadcasted_iota(jnp.int32, (slots, EXTENT), 1)
    share = EXTENT // (tile_count * height)
    here = place // (tile_count * height) == owner % share
    info = jnp.zeros((slots, EXTENT), F32)
    for t in range(tile_count):
        own = jnp.sum(jnp.where(lane == slot + t * slots, names, 0.0), axis=1, keepdims=True)
        info = jnp.where(here & (place // height % tile_count == t), own, info)
    tail = tile_count * columns * height
    for p in range(slots):
        send_ref[p, tail:, :] = jnp.broadcast_to(info[p : p + 1], (8, EXTENT)).astype(BF)


def gather_kernel(piece_ref, out_ref, data_ref, name_ref):
    owners, rows, _ = piece_ref.shape
    _, out_rows, edge = out_ref.shape
    height = edge // owners
    columns = edge // EXTENT
    tile_count = (rows - 8) // (columns * height)
    tail = rows - 8
    share = EXTENT // (tile_count * height)
    lane_row = lax.broadcasted_iota(jnp.int32, (EXTENT, EXTENT), 1) % height
    sub = lax.broadcasted_iota(jnp.int32, (EXTENT, EXTENT), 0)
    same = lane_row == sub % height
    for d in range(owners):
        for t in range(tile_count):
            at = (d * tile_count + t) * height
            for j in range(columns):
                source = (t * columns + j) * height
                data_ref[at : at + height, j * EXTENT : (j + 1) * EXTENT] = piece_ref[
                    d, source : source + height, :
                ]
    for start in range(0, owners, share):
        names = sum(piece_ref[d, tail : tail + 8, :].astype(F32) for d in range(start, start + share))
        names = jnp.where(same, jnp.broadcast_to(names[0:1], same.shape), -1.0)
        at = start * tile_count * height
        for c in range(owners * out_rows // EXTENT):
            group = (sub // height + c * (EXTENT // height)).astype(F32)
            name_ref[c * EXTENT : (c + 1) * EXTENT, at : at + EXTENT] = jnp.where(
                names == group, 1.0, 0.0
            ).astype(BF)
    ones = jnp.ones((data_ref.shape[0], EXTENT), BF)
    for c in range(owners * out_rows // EXTENT):
        pick = name_ref[c * EXTENT : (c + 1) * EXTENT, :]
        total = dot(pick, data_ref[...])
        share_of = 1.0 / jnp.maximum(dot(pick, ones), 1.0)
        total = total * jnp.concatenate([share_of] * columns, 1)
        first, last = c * EXTENT // out_rows, (c + 1) * EXTENT // out_rows
        out_ref[first:last] = total.astype(BF).reshape(last - first, out_rows, edge)


def in_vmem():
    return pl.BlockSpec(memory_space=pltpu.VMEM)


def in_smem():
    return pl.BlockSpec(memory_space=pltpu.SMEM)


def params():
    return pltpu.CompilerParams(vmem_limit_bytes=40 * 1024 * 1024)


def exchange(value, axis):
    return lax.all_to_all(value, axis, split_axis=0, concat_axis=0, tiled=True)


def body(patches, peak_offsets, tiles, band_offsets, routes):
    sections = lax.axis_size("gz")
    owners = lax.axis_size("xy")
    tile_count, edge = tiles.shape[1], tiles.shape[-1]
    height = edge // PIECES
    share = 2
    count = patches.shape[1]

    below = lax.ppermute(patches, "gz", [(i, i + 1) for i in range(sections - 1)])
    flow = pl.pallas_call(
        flow_kernel,
        out_shape=jax.ShapeDtypeStruct((sections, count, EXTENT), F32),
        in_specs=[in_smem()] + [in_vmem()] * 3,
        out_specs=in_vmem(),
        compiler_params=params(),
        name="flow",
    )(peak_offsets[0].T, patches[0], below[0], jnp.asarray(dft_constants()))
    flow = exchange(flow, "gz")

    position, pieces = pl.pallas_call(
        render_kernel,
        out_shape=(
            jax.ShapeDtypeStruct((count, EXTENT), F32),
            jax.ShapeDtypeStruct((PIECES, tile_count * height * edge // EXTENT + 8, EXTENT), BF),
        ),
        in_specs=[in_smem(), in_smem()] + [in_vmem()] * 3,
        out_specs=(in_vmem(), in_vmem()),
        scratch_shapes=[pltpu.VMEM((edge, edge), BF)] * 3,
        compiler_params=params(),
        name="render",
    )(jnp.asarray(relaxation_map(sections)), band_offsets[0], flow, routes[0].T, tiles[0])
    pieces = exchange(pieces, "xy")

    cells = pl.pallas_call(
        gather_kernel,
        out_shape=jax.ShapeDtypeStruct((owners, share * height, edge), BF),
        in_specs=[in_vmem()],
        out_specs=in_vmem(),
        scratch_shapes=[
            pltpu.VMEM((owners * tile_count * height, edge), BF),
            pltpu.VMEM((owners * share * height, owners * tile_count * height), BF),
        ],
        compiler_params=params(),
        name="gather",
    )(pieces)
    cells = exchange(cells, "xy")
    rendered = cells.reshape(PIECES, share, height, edge).transpose(1, 0, 2, 3)
    rendered = rendered.reshape(1, share, edge, edge)
    return position[:, :2].T[None], rendered


def solution(mesh):
    placed = (
        P("gz", "xy", None, None),
        P("gz", "xy", None),
        P("gz", "xy", None, None),
        P("gz", "xy", None),
        P("gz", "xy", None),
    )
    return jax.shard_map(
        body,
        mesh=mesh,
        in_specs=placed,
        out_specs=(P("gz", None, "xy"), P("gz", "xy", None, None)),
        check_vma=False,
    )
```

```python
import jax
import jax.numpy as jnp
import numpy as np
from jax import lax
from jax.experimental import pallas as pl
from jax.experimental.pallas import tpu as pltpu
from jax.sharding import PartitionSpec as P

PIECES = 32
NODES = 8
BAND = 6
RELAX = 3
EPSILON = 1e-06
STEP_SIZE = 0.25
ANCHOR_WEIGHT = 0.5
MIP_SCALE = 0.0625
SCORE_GAIN = 6.0

EXTENT = 128
HALF = 72
REACH = 40
BF = jnp.bfloat16
F32 = jnp.float32


def high_low(table):
    high = table.astype(jnp.bfloat16)
    low = (table - high.astype(np.float64)).astype(jnp.bfloat16)
    return high, low


def dft_constants():
    line = np.arange(EXTENT)
    phase = 2.0 * np.pi * ((line[:, None] * line[None, :]) % EXTENT) / EXTENT
    cos, sin = np.cos(phase), np.sin(phase)
    first = np.concatenate([cos[:HALF], sin[:HALF]], 0)
    first = np.concatenate(high_low(first), 1)
    second_high, second_low = high_low(np.concatenate([cos, sin], 1))
    second = np.concatenate([second_high, second_high, second_low], 0)
    third_high, third_low = high_low(np.block([[cos, sin], [-sin, cos]]))
    third = np.concatenate([third_high, third_high, third_low], 0)
    weight = np.where(line[:HALF] <= EXTENT // 2, 2.0, 0.0)
    weight[0] = weight[EXTENT // 2] = 1.0
    rows = (np.arange(-REACH, REACH) % EXTENT)[:, None]
    angle = 2.0 * np.pi * ((rows * line[None, :HALF]) % EXTENT) / EXTENT
    fourth = np.concatenate([weight * np.cos(angle), -weight * np.sin(angle)], 1)
    fourth_high, fourth_low = high_low(fourth / float(EXTENT * EXTENT))
    fourth = np.concatenate([fourth_high, fourth_high, fourth_low], 1)
    fourth = np.pad(fourth, ((0, 0), (0, 4 * EXTENT - fourth.shape[1])))
    early = np.concatenate([first, second], 0)
    late = np.concatenate([third, fourth[:, : 2 * EXTENT], fourth[:, 2 * EXTENT :]], 0)
    return early, late


def relaxation_map(sections):
    flow = np.eye(sections)
    positions = np.tril(np.ones((sections, sections)))
    for _ in range(RELAX):
        lower = np.zeros_like(positions)
        upper = np.zeros_like(positions)
        lower[1:] = positions[:-1] + flow[1:] - positions[1:]
        upper[:-1] = positions[1:] - flow[1:] - positions[:-1]
        positions = positions + STEP_SIZE * (lower + upper - ANCHOR_WEIGHT * positions)
    return positions.astype(np.float32)


def split(value):
    high = value.astype(BF)
    return high, (value - high.astype(F32)).astype(BF)


def dot(a, b):
    return jnp.dot(a, b, preferred_element_type=F32)


def spectra(patches, table_ref):
    lines = []
    for pair in range(0, len(patches), 2):
        both = jnp.concatenate(patches[pair : pair + 2], 1)
        line = dot(table_ref[: 2 * HALF], jnp.concatenate([both, both], 0))
        lines += [line[:, :EXTENT], line[:, EXTENT:]]
    high, low = split(jnp.concatenate(lines, 0))
    product = dot(jnp.concatenate([high, low, high], 1), table_ref[2 * HALF :])
    result = []
    for k in range(len(patches)):
        a = product[2 * HALF * k : 2 * HALF * k + HALF]
        b = product[2 * HALF * k + HALF : 2 * HALF * (k + 1)]
        result.append((a[:, :EXTENT] - b[:, EXTENT:], -(a[:, EXTENT:] + b[:, :EXTENT])))
    return result


def energy(ref):
    rows = []
    for n in range(ref.shape[0]):
        value = ref[n].astype(F32)
        rows.append(jnp.sum(value * value, axis=0, keepdims=True))
    total = jnp.sum(jnp.concatenate(rows, 0), axis=1, keepdims=True)
    return total * (1.0 / (EXTENT * EXTENT))


def own_kernel(now_ref, table_ref, spectrum_ref, energy_ref):
    for pair in range(0, now_ref.shape[0], 2):
        for k, (real, imag) in enumerate(spectra([now_ref[pair], now_ref[pair + 1]], table_ref)):
            spectrum_ref[pair + k, :, :EXTENT] = real
            spectrum_ref[pair + k, :, EXTENT:] = imag
    energy_ref[...] = jnp.broadcast_to(energy(now_ref), energy_ref.shape)


def flow_kernel(peak_ref, low_ref, spectrum_ref, energy_ref, table_ref, last_ref, out_ref, inverse_ref, arrived):
    count = low_ref.shape[0]
    copy = pltpu.make_async_copy(last_ref, inverse_ref, arrived)
    copy.start()
    crosses = []
    for pair in range(0, count, 2):
        block = []
        for k, (lr, li) in enumerate(spectra([low_ref[pair], low_ref[pair + 1]], table_ref)):
            nr = spectrum_ref[pair + k, :, :EXTENT]
            ni = spectrum_ref[pair + k, :, EXTENT:]
            block.append(jnp.concatenate([nr * lr + ni * li, ni * lr - nr * li], 1))
        crosses.append(jnp.concatenate(block, 0))
    copy.wait()
    third = 6 * EXTENT
    fourth = jnp.concatenate(
        [
            inverse_ref[third : third + 2 * REACH],
            inverse_ref[third + 2 * REACH :, : 6 * HALF - 2 * EXTENT],
        ],
        1,
    )
    correlations = []
    for cross in crosses:
        high, low = split(cross)
        outer = dot(jnp.concatenate([high, low, high], 1), inverse_ref[:third])
        columns = []
        for k in range(2):
            block = outer[HALF * k : HALF * (k + 1)]
            columns.append(jnp.concatenate([block[:, :EXTENT], block[:, EXTENT:]], 0))
        high, low = split(jnp.concatenate(columns, 1))
        result = dot(fourth, jnp.concatenate([high, low, high], 0))
        correlations += [result[:, :EXTENT], result[:, EXTENT:]]

    scale = (SCORE_GAIN / EXTENT) / jnp.sqrt(energy_ref[:, :1] * energy(low_ref) + EPSILON)
    shape = (2 * REACH, EXTENT)
    row = lax.broadcasted_iota(jnp.int32, shape, 0) - REACH
    column = lax.broadcasted_iota(jnp.int32, shape, 1)
    scores, relatives, tops = [], [], []
    for n in range(count):
        rel_y = row - peak_ref[0, n]
        rel_x = ((column - peak_ref[1, n] + EXTENT // 2) & (EXTENT - 1)) - EXTENT // 2
        quarter = EXTENT // 4
        inside = (rel_y >= -quarter) & (rel_y < quarter) & (rel_x >= -quarter) & (rel_x < quarter)
        score = jnp.where(inside, correlations[n] * scale[n : n + 1], -1e30)
        scores.append(score)
        relatives.append((rel_y.astype(F32), rel_x[:1].astype(F32)))
        tops.append(jnp.max(score, axis=0, keepdims=True))
    top = jnp.max(jnp.concatenate(tops, 0), axis=1, keepdims=True)
    sums, sums_y, sums_x = [], [], []
    for n in range(count):
        weight = jnp.exp(scores[n] - top[n : n + 1])
        rel_y, rel_x = relatives[n]
        along = jnp.sum(weight, axis=0, keepdims=True)
        sums.append(along)
        sums_y.append(jnp.sum(weight * rel_y, axis=0, keepdims=True))
        sums_x.append(along * rel_x)
    total, total_y, total_x = (
        jnp.sum(jnp.concatenate(s, 0), axis=1, keepdims=True) for s in (sums, sums_y, sums_x)
    )
    node = lax.broadcasted_iota(jnp.int32, (count, EXTENT), 0)
    lane = lax.broadcasted_iota(jnp.int32, (count, EXTENT), 1)
    peak_y = jnp.zeros((count, EXTENT), jnp.int32)
    peak_x = jnp.zeros((count, EXTENT), jnp.int32)
    for n in range(count):
        peak_y = jnp.where(node == n, peak_ref[0, n], peak_y)
        peak_x = jnp.where(node == n, peak_ref[1, n], peak_x)
    flow_y = peak_y.astype(F32) + total_y / total
    flow_x = peak_x.astype(F32) + total_x / total
    flow = jnp.where(lane == node, flow_y, jnp.where(lane == node + count, flow_x, 0.0))
    flow = jnp.sum(flow, axis=0, keepdims=True)
    out_ref[...] = jnp.broadcast_to(flow[None], out_ref.shape)


def fill_band(target_ref, residual, offset, sub_sign):
    block = EXTENT
    lane = lax.broadcasted_iota(jnp.int32, (1, block), 1)
    tap = (lane - BAND).astype(F32) - residual
    raw = jnp.where(lane <= 2 * BAND, 1.0 / (1.0 + tap * tap), 0.0)
    norm = jnp.sum(raw, axis=1, keepdims=True)
    a = lax.broadcasted_iota(jnp.int32, (block, block), 0)
    b = lax.broadcasted_iota(jnp.int32, (block, block), 1)
    d = sub_sign * (a - b) - offset
    k = ((d + block // 2) & (block - 1)) - block // 2
    away = k.astype(F32) - residual
    value = (1.0 / (1.0 + away * away)) / norm
    blocks = {}
    for step in (-1, 0, 1):
        near = jnp.abs(d + sub_sign * step * block) <= BAND
        blocks[step] = jnp.where(near, value, 0.0).astype(BF)
    zero = jnp.zeros((block, block), BF)
    count = target_ref.shape[0] // block
    for i in range(count):
        for j in range(count):
            target_ref[i * block : (i + 1) * block, j * block : (j + 1) * block] = blocks.get(
                i - j, zero
            )


def render_kernel(map_ref, band_ref, flow_ref, route_ref, tile_ref, position_ref, send_ref, col_ref, row_ref, pass_ref):
    sections = flow_ref.shape[0]
    tile_count, edge, _ = tile_ref.shape
    slots = send_ref.shape[0]
    section, owner = lax.axis_index("gz"), lax.axis_index("xy")
    position = jnp.zeros(flow_ref.shape[1:], F32)
    for s in range(sections):
        position = position + map_ref[section, s] * flow_ref[s]
    position_ref[...] = position
    per_tile = NODES // tile_count
    lanes = lax.broadcasted_iota(jnp.int32, position.shape, 1)
    height = edge // slots
    columns = edge // EXTENT
    chunk = EXTENT
    for t in range(tile_count):
        offset_y, offset_x = band_ref[t, 0], band_ref[t, 1]
        shift_y, shift_x = (
            jnp.sum(jnp.where(lanes // per_tile == c * tile_count + t, position, 0.0), axis=1, keepdims=True)
            * (MIP_SCALE / per_tile)
            for c in range(2)
        )
        fill_band(col_ref, shift_x - offset_x.astype(F32), offset_x, 1)
        fill_band(row_ref, shift_y - offset_y.astype(F32), offset_y, -1)
        for c in range(edge // chunk):
            rows = slice(c * chunk, (c + 1) * chunk)
            pass_ref[rows, :] = dot(tile_ref[t, rows, :], col_ref[...]).astype(BF)
        for c in range(edge // chunk):
            rows = slice(c * chunk, (c + 1) * chunk)
            first, last = c * chunk // height, (c + 1) * chunk // height
            done = dot(row_ref[rows, :], pass_ref[...]).astype(BF)
            done = done.reshape(last - first, height, edge)
            for j in range(columns):
                at = (t * columns + j) * height
                send_ref[first:last, at : at + height, :] = done[:, :, j * EXTENT : (j + 1) * EXTENT]
    lane = lax.broadcasted_iota(jnp.int32, (slots, tile_count * slots), 1)
    slot = lax.broadcasted_iota(jnp.int32, (slots, tile_count * slots), 0)
    names = jnp.broadcast_to(route_ref[...], lane.shape).astype(F32)
    place = lax.broadcasted_iota(jnp.int32, (slots, EXTENT), 1)
    share = EXTENT // (tile_count * height)
    here = place // (tile_count * height) == owner % share
    info = jnp.zeros((slots, EXTENT), F32)
    for t in range(tile_count):
        own = jnp.sum(jnp.where(lane == slot + t * slots, names, 0.0), axis=1, keepdims=True)
        info = jnp.where(here & (place // height % tile_count == t), own, info)
    tail = tile_count * columns * height
    for p in range(slots):
        send_ref[p, tail:, :] = jnp.broadcast_to(info[p : p + 1], (8, EXTENT)).astype(BF)


def gather_kernel(piece_ref, out_ref, data_ref):
    owners, rows, _ = piece_ref.shape
    _, out_rows, edge = out_ref.shape
    height = edge // owners
    columns = edge // EXTENT
    tile_count = (rows - 8) // (columns * height)
    tail = rows - 8
    share = EXTENT // (tile_count * height)
    lane_row = lax.broadcasted_iota(jnp.int32, (EXTENT, EXTENT), 1) % height
    sub = lax.broadcasted_iota(jnp.int32, (EXTENT, EXTENT), 0)
    same = lane_row == sub % height
    for d in range(owners):
        for t in range(tile_count):
            at = (d * tile_count + t) * height
            for j in range(columns):
                source = (t * columns + j) * height
                data_ref[at : at + height, j * EXTENT : (j + 1) * EXTENT] = piece_ref[
                    d, source : source + height, :
                ]
    names = [
        sum(piece_ref[d, tail : tail + 8, :].astype(F32) for d in range(start, start + share))[0:1]
        for start in range(0, owners, share)
    ]
    for c in range(owners * out_rows // EXTENT):
        group = (sub // height + c * (EXTENT // height)).astype(F32)
        hits = [jnp.where(same & (name == group), 1.0, 0.0) for name in names]
        count = jnp.sum(sum(hits), axis=1, keepdims=True)
        total = dot(jnp.concatenate([hit.astype(BF) for hit in hits], 1), data_ref[...])
        total = total * (1.0 / jnp.maximum(count, 1.0))
        first, last = c * EXTENT // out_rows, (c + 1) * EXTENT // out_rows
        out_ref[first:last] = total.astype(BF).reshape(last - first, out_rows, edge)


def in_vmem():
    return pl.BlockSpec(memory_space=pltpu.VMEM)


def in_smem():
    return pl.BlockSpec(memory_space=pltpu.SMEM)


def params():
    return pltpu.CompilerParams(vmem_limit_bytes=40 * 1024 * 1024)


def exchange(value, axis):
    return lax.all_to_all(value, axis, split_axis=0, concat_axis=0, tiled=True)


def body(patches, peak_offsets, tiles, band_offsets, routes):
    sections = lax.axis_size("gz")
    owners = lax.axis_size("xy")
    tile_count, edge = tiles.shape[1], tiles.shape[-1]
    height = edge // PIECES
    share = 2
    count = patches.shape[1]

    below = lax.ppermute(patches, "gz", [(i, i + 1) for i in range(sections - 1)])
    early_table, late_table = (jnp.asarray(t) for t in dft_constants())
    spectrum, power = pl.pallas_call(
        own_kernel,
        out_shape=(
            jax.ShapeDtypeStruct((count, HALF, 2 * EXTENT), F32),
            jax.ShapeDtypeStruct((count, EXTENT), F32),
        ),
        in_specs=[in_vmem()] * 2,
        out_specs=(in_vmem(), in_vmem()),
        compiler_params=params(),
        cost_estimate=pl.CostEstimate(flops=10**9, bytes_accessed=2**20, transcendentals=0),
        name="own",
    )(patches[0], early_table)
    flow = pl.pallas_call(
        flow_kernel,
        out_shape=jax.ShapeDtypeStruct((sections, 1, EXTENT), F32),
        in_specs=[in_smem()] + [in_vmem()] * 4 + [pl.BlockSpec(memory_space=pl.ANY)],
        out_specs=in_vmem(),
        scratch_shapes=[pltpu.VMEM(late_table.shape, BF), pltpu.SemaphoreType.DMA],
        compiler_params=params(),
        name="flow",
    )(peak_offsets[0].T, below[0], spectrum, power, early_table, late_table)
    flow = exchange(flow, "gz")

    position, pieces = pl.pallas_call(
        render_kernel,
        out_shape=(
            jax.ShapeDtypeStruct((1, EXTENT), F32),
            jax.ShapeDtypeStruct((PIECES, tile_count * height * edge // EXTENT + 8, EXTENT), BF),
        ),
        in_specs=[in_smem(), in_smem()] + [in_vmem()] * 3,
        out_specs=(in_vmem(), in_vmem()),
        scratch_shapes=[pltpu.VMEM((edge, edge), BF)] * 3,
        compiler_params=params(),
        name="render",
    )(jnp.asarray(relaxation_map(sections)), band_offsets[0], flow, routes[0].T, tiles[0])
    pieces = exchange(pieces, "xy")

    cells = pl.pallas_call(
        gather_kernel,
        out_shape=jax.ShapeDtypeStruct((owners, share * height, edge), BF),
        in_specs=[in_vmem()],
        out_specs=in_vmem(),
        scratch_shapes=[pltpu.VMEM((owners * tile_count * height, edge), BF)],
        compiler_params=params(),
        name="gather",
    )(pieces)
    cells = exchange(cells, "xy")
    rendered = cells.reshape(PIECES, share, height, edge).transpose(1, 0, 2, 3)
    rendered = rendered.reshape(1, share, edge, edge)
    return position[:, : 2 * count].reshape(1, 2, count), rendered


def solution(mesh):
    placed = (
        P("gz", "xy", None, None),
        P("gz", "xy", None),
        P("gz", "xy", None, None),
        P("gz", "xy", None),
        P("gz", "xy", None),
    )
    return jax.shard_map(
        body,
        mesh=mesh,
        in_specs=placed,
        out_specs=(P("gz", None, "xy"), P("gz", "xy", None, None)),
        check_vma=False,
    )
```

```python
import jax
import jax.numpy as jnp
import numpy as np
from jax import lax
from jax.experimental import pallas as pl
from jax.experimental.pallas import tpu as pltpu
from jax.sharding import PartitionSpec as P

PIECES = 32
NODES = 8
WIDE = 4
BAND = 6
RELAX = 3
EPSILON = 1e-06
STEP_SIZE = 0.25
ANCHOR_WEIGHT = 0.5
MIP_SCALE = 0.0625
SCORE_GAIN = 6.0

EXTENT = 128
HALF = 72
REACH = 40
BF = jnp.bfloat16
F32 = jnp.float32


def high_low(table):
    high = table.astype(jnp.bfloat16)
    low = (table - high.astype(np.float64)).astype(jnp.bfloat16)
    return high, low


def dft_constants():
    line = np.arange(EXTENT)
    phase = 2.0 * np.pi * ((line[:, None] * line[None, :]) % EXTENT) / EXTENT
    cos, sin = np.cos(phase), np.sin(phase)
    first = np.concatenate([cos[:HALF], sin[:HALF]], 0)
    first = np.concatenate(high_low(first), 1)
    second_high, second_low = high_low(np.concatenate([cos, sin], 1))
    second = np.concatenate([second_high, second_high, second_low], 0)
    third_high, third_low = high_low(np.block([[cos, sin], [-sin, cos]]))
    third = np.concatenate([third_high, third_high, third_low], 0)
    weight = np.where(line[:HALF] <= EXTENT // 2, 2.0, 0.0)
    weight[0] = weight[EXTENT // 2] = 1.0
    rows = (np.arange(-REACH, REACH) % EXTENT)[:, None]
    angle = 2.0 * np.pi * ((rows * line[None, :HALF]) % EXTENT) / EXTENT
    fourth = np.concatenate([weight * np.cos(angle), -weight * np.sin(angle)], 1)
    fourth_high, fourth_low = high_low(fourth / float(EXTENT * EXTENT))
    fourth = np.concatenate([fourth_high, fourth_high, fourth_low], 1)
    fourth = np.pad(fourth, ((0, 0), (0, 4 * EXTENT - fourth.shape[1])))
    early = np.concatenate([first, second], 0)
    late = np.concatenate([third, fourth[:, : 2 * EXTENT], fourth[:, 2 * EXTENT :]], 0)
    return early, late


def relaxation_map(sections):
    flow = np.eye(sections)
    positions = np.tril(np.ones((sections, sections)))
    for _ in range(RELAX):
        lower = np.zeros_like(positions)
        upper = np.zeros_like(positions)
        lower[1:] = positions[:-1] + flow[1:] - positions[1:]
        upper[:-1] = positions[1:] - flow[1:] - positions[:-1]
        positions = positions + STEP_SIZE * (lower + upper - ANCHOR_WEIGHT * positions)
    return positions.astype(np.float32)


def split(value):
    high = value.astype(BF)
    return high, (value - high.astype(F32)).astype(BF)


def dot(a, b):
    return jnp.dot(a, b, preferred_element_type=F32)


def spectra(patches, table_ref):
    lines = []
    for pair in range(0, len(patches), 2):
        both = jnp.concatenate(patches[pair : pair + 2], 1)
        line = dot(table_ref[: 2 * HALF], jnp.concatenate([both, both], 0))
        lines += [line[:, :EXTENT], line[:, EXTENT:]]
    high, low = split(jnp.concatenate(lines, 0))
    product = dot(jnp.concatenate([high, low, high], 1), table_ref[2 * HALF :])
    result = []
    for k in range(len(patches)):
        a = product[2 * HALF * k : 2 * HALF * k + HALF]
        b = product[2 * HALF * k + HALF : 2 * HALF * (k + 1)]
        result.append((a[:, :EXTENT] - b[:, EXTENT:], -(a[:, EXTENT:] + b[:, :EXTENT])))
    return result


def energy(ref):
    rows = []
    for n in range(ref.shape[0]):
        value = ref[n].astype(F32)
        rows.append(jnp.sum(value * value, axis=0, keepdims=True))
    total = jnp.sum(jnp.concatenate(rows, 0), axis=1, keepdims=True)
    return total * (1.0 / (EXTENT * EXTENT))


def own_kernel(now_ref, table_ref, spectrum_ref, energy_ref):
    for pair in range(0, now_ref.shape[0], 2):
        for k, (real, imag) in enumerate(spectra([now_ref[pair], now_ref[pair + 1]], table_ref)):
            spectrum_ref[pair + k, :, :EXTENT] = real
            spectrum_ref[pair + k, :, EXTENT:] = imag
    energy_ref[...] = jnp.broadcast_to(energy(now_ref), energy_ref.shape)


def flow_kernel(peak_ref, low_ref, spectrum_ref, energy_ref, table_ref, last_ref, out_ref, inverse_ref, arrived):
    count = low_ref.shape[0]
    copy = pltpu.make_async_copy(last_ref, inverse_ref, arrived)
    copy.start()
    crosses = []
    for pair in range(0, count, 2):
        block = []
        for k, (lr, li) in enumerate(spectra([low_ref[pair], low_ref[pair + 1]], table_ref)):
            nr = spectrum_ref[pair + k, :, :EXTENT]
            ni = spectrum_ref[pair + k, :, EXTENT:]
            block.append(jnp.concatenate([nr * lr + ni * li, ni * lr - nr * li], 1))
        crosses.append(jnp.concatenate(block, 0))
    copy.wait()
    third = 6 * EXTENT
    fourth = jnp.concatenate(
        [
            inverse_ref[third : third + 2 * REACH],
            inverse_ref[third + 2 * REACH :, : 6 * HALF - 2 * EXTENT],
        ],
        1,
    )
    correlations = []
    for cross in crosses:
        high, low = split(cross)
        outer = dot(jnp.concatenate([high, low, high], 1), inverse_ref[:third])
        columns = []
        for k in range(2):
            block = outer[HALF * k : HALF * (k + 1)]
            columns.append(jnp.concatenate([block[:, :EXTENT], block[:, EXTENT:]], 0))
        high, low = split(jnp.concatenate(columns, 1))
        result = dot(fourth, jnp.concatenate([high, low, high], 0))
        correlations += [result[:, :EXTENT], result[:, EXTENT:]]

    scale = (SCORE_GAIN / EXTENT) / jnp.sqrt(energy_ref[:, :1] * energy(low_ref) + EPSILON)
    shape = (2 * REACH, EXTENT)
    row = lax.broadcasted_iota(jnp.int32, shape, 0) - REACH
    column = lax.broadcasted_iota(jnp.int32, shape, 1)
    scores, relatives, tops = [], [], []
    for n in range(count):
        rel_y = row - peak_ref[0, n]
        rel_x = ((column - peak_ref[1, n] + EXTENT // 2) & (EXTENT - 1)) - EXTENT // 2
        quarter = EXTENT // 4
        inside = (rel_y >= -quarter) & (rel_y < quarter) & (rel_x >= -quarter) & (rel_x < quarter)
        score = jnp.where(inside, correlations[n] * scale[n : n + 1], -1e30)
        scores.append(score)
        relatives.append((rel_y.astype(F32), rel_x[:1].astype(F32)))
        tops.append(jnp.max(score, axis=0, keepdims=True))
    top = jnp.max(jnp.concatenate(tops, 0), axis=1, keepdims=True)
    sums, sums_y, sums_x = [], [], []
    for n in range(count):
        weight = jnp.exp(scores[n] - top[n : n + 1])
        rel_y, rel_x = relatives[n]
        along = jnp.sum(weight, axis=0, keepdims=True)
        sums.append(along)
        sums_y.append(jnp.sum(weight * rel_y, axis=0, keepdims=True))
        sums_x.append(along * rel_x)
    total, total_y, total_x = (
        jnp.sum(jnp.concatenate(s, 0), axis=1, keepdims=True) for s in (sums, sums_y, sums_x)
    )
    node = lax.broadcasted_iota(jnp.int32, (count, EXTENT), 0)
    lane = lax.broadcasted_iota(jnp.int32, (count, EXTENT), 1)
    peak_y = jnp.zeros((count, EXTENT), jnp.int32)
    peak_x = jnp.zeros((count, EXTENT), jnp.int32)
    for n in range(count):
        peak_y = jnp.where(node == n, peak_ref[0, n], peak_y)
        peak_x = jnp.where(node == n, peak_ref[1, n], peak_x)
    flow_y = peak_y.astype(F32) + total_y / total
    flow_x = peak_x.astype(F32) + total_x / total
    flow = jnp.where(lane == node, flow_y, jnp.where(lane == node + count, flow_x, 0.0))
    flow = jnp.sum(flow, axis=0, keepdims=True)
    out_ref[...] = jnp.broadcast_to(flow[None], out_ref.shape)


def fill_band(target_ref, residual, offset, sub_sign):
    block = EXTENT
    lane = lax.broadcasted_iota(jnp.int32, (1, block), 1)
    tap = (lane - BAND).astype(F32) - residual
    raw = jnp.where(lane <= 2 * BAND, 1.0 / (1.0 + tap * tap), 0.0)
    norm = jnp.sum(raw, axis=1, keepdims=True)
    a = lax.broadcasted_iota(jnp.int32, (block, block), 0)
    b = lax.broadcasted_iota(jnp.int32, (block, block), 1)
    d = sub_sign * (a - b) - offset
    k = ((d + block // 2) & (block - 1)) - block // 2
    away = k.astype(F32) - residual
    value = (1.0 / (1.0 + away * away)) / norm
    blocks = {}
    for step in (-1, 0, 1):
        near = jnp.abs(d + sub_sign * step * block) <= BAND
        blocks[step] = jnp.where(near, value, 0.0).astype(BF)
    zero = jnp.zeros((block, block), BF)
    count = target_ref.shape[0] // block
    for i in range(count):
        for j in range(count):
            target_ref[i * block : (i + 1) * block, j * block : (j + 1) * block] = blocks.get(
                i - j, zero
            )


def render_kernel(map_ref, band_ref, flow_ref, route_ref, tile_ref, position_ref, send_ref, col_ref, row_ref, pass_ref):
    sections = flow_ref.shape[0]
    tile_count, edge, _ = tile_ref.shape
    slots = send_ref.shape[0]
    section, owner = lax.axis_index("gz"), lax.axis_index("xy")
    second_core = section % 2 == 1

    def slot_of(p):
        return jnp.where(second_core, p % WIDE * (slots // WIDE) + p // WIDE, p)

    position = jnp.zeros(flow_ref.shape[1:], F32)
    for s in range(sections):
        position = position + map_ref[section, s] * flow_ref[s]
    position_ref[...] = position
    per_tile = NODES // tile_count
    lanes = lax.broadcasted_iota(jnp.int32, position.shape, 1)
    height = edge // slots
    columns = edge // EXTENT
    chunk = EXTENT
    for t in range(tile_count):
        offset_y, offset_x = band_ref[t, 0], band_ref[t, 1]
        shift_y, shift_x = (
            jnp.sum(jnp.where(lanes // per_tile == c * tile_count + t, position, 0.0), axis=1, keepdims=True)
            * (MIP_SCALE / per_tile)
            for c in range(2)
        )
        fill_band(col_ref, shift_x - offset_x.astype(F32), offset_x, 1)
        fill_band(row_ref, shift_y - offset_y.astype(F32), offset_y, -1)
        for c in range(edge // chunk):
            rows = slice(c * chunk, (c + 1) * chunk)
            pass_ref[rows, :] = dot(tile_ref[t, rows, :], col_ref[...]).astype(BF)
        for c in range(edge // chunk):
            rows = slice(c * chunk, (c + 1) * chunk)
            first, last = c * chunk // height, (c + 1) * chunk // height
            done = dot(row_ref[rows, :], pass_ref[...]).astype(BF)
            done = done.reshape(last - first, height, edge)
            for p in range(first, last):
                for j in range(columns):
                    at = (t * columns + j) * height
                    send_ref[slot_of(p), at : at + height, :] = done[
                        p - first, :, j * EXTENT : (j + 1) * EXTENT
                    ]
    lane = lax.broadcasted_iota(jnp.int32, (slots, tile_count * slots), 1)
    slot = lax.broadcasted_iota(jnp.int32, (slots, tile_count * slots), 0)
    names = jnp.broadcast_to(route_ref[...], lane.shape).astype(F32)
    place = lax.broadcasted_iota(jnp.int32, (slots, EXTENT), 1)
    share = EXTENT // (tile_count * height)
    here = place // (tile_count * height) == owner % share
    info = jnp.zeros((slots, EXTENT), F32)
    for t in range(tile_count):
        own = jnp.sum(jnp.where(lane == slot + t * slots, names, 0.0), axis=1, keepdims=True)
        info = jnp.where(here & (place // height % tile_count == t), own, info)
    tail = tile_count * columns * height
    for p in range(slots):
        send_ref[slot_of(p), tail:, :] = jnp.broadcast_to(info[p : p + 1], (8, EXTENT)).astype(BF)


def gather_kernel(piece_ref, out_ref, data_ref):
    owners, rows, _ = piece_ref.shape
    _, out_rows, edge = out_ref.shape
    height = edge // owners
    columns = edge // EXTENT
    tile_count = (rows - 8) // (columns * height)
    tail = rows - 8
    share = EXTENT // (tile_count * height)
    lane_row = lax.broadcasted_iota(jnp.int32, (EXTENT, EXTENT), 1) % height
    sub = lax.broadcasted_iota(jnp.int32, (EXTENT, EXTENT), 0)
    same = lane_row == sub % height
    for d in range(owners):
        for t in range(tile_count):
            at = (d * tile_count + t) * height
            for j in range(columns):
                source = (t * columns + j) * height
                data_ref[at : at + height, j * EXTENT : (j + 1) * EXTENT] = piece_ref[
                    d, source : source + height, :
                ]
    names = [
        sum(piece_ref[d, tail : tail + 8, :].astype(F32) for d in range(start, start + share))[0:1]
        for start in range(0, owners, share)
    ]
    for c in range(owners * out_rows // EXTENT):
        group = (sub // height + c * (EXTENT // height)).astype(F32)
        hits = [jnp.where(same & (name == group), 1.0, 0.0) for name in names]
        count = jnp.sum(sum(hits), axis=1, keepdims=True)
        total = dot(jnp.concatenate([hit.astype(BF) for hit in hits], 1), data_ref[...])
        total = total * (1.0 / jnp.maximum(count, 1.0))
        first, last = c * EXTENT // out_rows, (c + 1) * EXTENT // out_rows
        out_ref[first:last] = total.astype(BF).reshape(last - first, out_rows, edge)


def in_vmem():
    return pl.BlockSpec(memory_space=pltpu.VMEM)


def in_smem():
    return pl.BlockSpec(memory_space=pltpu.SMEM)


def params():
    return pltpu.CompilerParams(vmem_limit_bytes=40 * 1024 * 1024)


def exchange(value, axis, groups=None):
    return lax.all_to_all(
        value, axis, split_axis=0, concat_axis=0, tiled=True, axis_index_groups=groups
    )


def exchange_x_then_z(value):
    owners, rows, lanes = value.shape
    high = owners // WIDE
    along_x = [[z * WIDE + x for x in range(WIDE)] for z in range(high)]
    along_z = [[z * WIDE + x for z in range(high)] for x in range(WIDE)]
    value = exchange(value.reshape(WIDE, high * rows, lanes), "xy", along_x)
    value = value.reshape(WIDE, high, rows, lanes).transpose(1, 0, 2, 3)
    value = exchange(value.reshape(high, WIDE * rows, lanes), "xy", along_z)
    return value.reshape(owners, rows, lanes)


def body(patches, peak_offsets, tiles, band_offsets, routes):
    sections = lax.axis_size("gz")
    owners = lax.axis_size("xy")
    tile_count, edge = tiles.shape[1], tiles.shape[-1]
    height = edge // PIECES
    share = 2
    count = patches.shape[1]

    below = lax.ppermute(patches, "gz", [(i, i + 1) for i in range(sections - 1)])
    early_table, late_table = (jnp.asarray(t) for t in dft_constants())
    spectrum, power = pl.pallas_call(
        own_kernel,
        out_shape=(
            jax.ShapeDtypeStruct((count, HALF, 2 * EXTENT), F32),
            jax.ShapeDtypeStruct((count, EXTENT), F32),
        ),
        in_specs=[in_vmem()] * 2,
        out_specs=(in_vmem(), in_vmem()),
        compiler_params=params(),
        cost_estimate=pl.CostEstimate(flops=10**9, bytes_accessed=2**20, transcendentals=0),
        name="own",
    )(patches[0], early_table)
    flow = pl.pallas_call(
        flow_kernel,
        out_shape=jax.ShapeDtypeStruct((sections, 1, EXTENT), F32),
        in_specs=[in_smem()] + [in_vmem()] * 4 + [pl.BlockSpec(memory_space=pl.ANY)],
        out_specs=in_vmem(),
        scratch_shapes=[pltpu.VMEM(late_table.shape, BF), pltpu.SemaphoreType.DMA],
        compiler_params=params(),
        name="flow",
    )(peak_offsets[0].T, below[0], spectrum, power, early_table, late_table)
    flow = exchange(flow, "gz")

    position, pieces = pl.pallas_call(
        render_kernel,
        out_shape=(
            jax.ShapeDtypeStruct((1, EXTENT), F32),
            jax.ShapeDtypeStruct((PIECES, tile_count * height * edge // EXTENT + 8, EXTENT), BF),
        ),
        in_specs=[in_smem(), in_smem()] + [in_vmem()] * 3,
        out_specs=(in_vmem(), in_vmem()),
        scratch_shapes=[pltpu.VMEM((edge, edge), BF)] * 3,
        compiler_params=params(),
        name="render",
    )(jnp.asarray(relaxation_map(sections)), band_offsets[0], flow, routes[0].T, tiles[0])
    pieces = lax.cond(
        lax.axis_index("gz") % 2 == 1,
        exchange_x_then_z,
        lambda value: exchange(value, "xy"),
        pieces,
    )

    cells = pl.pallas_call(
        gather_kernel,
        out_shape=jax.ShapeDtypeStruct((owners, share * height, edge), BF),
        in_specs=[in_vmem()],
        out_specs=in_vmem(),
        scratch_shapes=[pltpu.VMEM((owners * tile_count * height, edge), BF)],
        compiler_params=params(),
        name="gather",
    )(pieces)
    cells = exchange(cells, "xy")
    rendered = cells.reshape(PIECES, share, height, edge).transpose(1, 0, 2, 3)
    rendered = rendered.reshape(1, share, edge, edge)
    return position[:, : 2 * count].reshape(1, 2, count), rendered


def solution(mesh):
    placed = (
        P("gz", "xy", None, None),
        P("gz", "xy", None),
        P("gz", "xy", None, None),
        P("gz", "xy", None),
        P("gz", "xy", None),
    )
    return jax.shard_map(
        body,
        mesh=mesh,
        in_specs=placed,
        out_specs=(P("gz", None, "xy"), P("gz", "xy", None, None)),
        check_vma=False,
    )
```

```python
import jax
import jax.numpy as jnp
import numpy as np
from jax import lax
from jax.experimental import pallas as pl
from jax.experimental.pallas import tpu as pltpu
from jax.sharding import PartitionSpec as P

PIECES = 32
NODES = 8
WIDE = 4
BAND = 6
RELAX = 3
EPSILON = 1e-06
STEP_SIZE = 0.25
ANCHOR_WEIGHT = 0.5
MIP_SCALE = 0.0625
SCORE_GAIN = 6.0

EXTENT = 128
HALF = 72
REACH = 40
BF = jnp.bfloat16
F32 = jnp.float32


def high_low(table):
    high = table.astype(jnp.bfloat16)
    low = (table - high.astype(np.float64)).astype(jnp.bfloat16)
    return high, low


def dft_constants():
    line = np.arange(EXTENT)
    phase = 2.0 * np.pi * ((line[:, None] * line[None, :]) % EXTENT) / EXTENT
    cos, sin = np.cos(phase), np.sin(phase)
    first = np.concatenate([cos[:HALF], sin[:HALF]], 0)
    first = np.concatenate(high_low(first), 1)
    second_high, second_low = high_low(np.concatenate([cos, sin], 1))
    second = np.concatenate([second_high, second_high, second_low], 0)
    third_high, third_low = high_low(np.block([[cos, sin], [-sin, cos]]))
    third = np.concatenate([third_high, third_high, third_low], 0)
    weight = np.where(line[:HALF] <= EXTENT // 2, 2.0, 0.0)
    weight[0] = weight[EXTENT // 2] = 1.0
    rows = (np.arange(-REACH, REACH) % EXTENT)[:, None]
    angle = 2.0 * np.pi * ((rows * line[None, :HALF]) % EXTENT) / EXTENT
    fourth = np.concatenate([weight * np.cos(angle), -weight * np.sin(angle)], 1)
    fourth_high, fourth_low = high_low(fourth / float(EXTENT * EXTENT))
    fourth = np.concatenate([fourth_high, fourth_high, fourth_low], 1)
    fourth = np.pad(fourth, ((0, 0), (0, 4 * EXTENT - fourth.shape[1])))
    early = np.concatenate([first, second], 0)
    late = np.concatenate([third, fourth[:, : 2 * EXTENT], fourth[:, 2 * EXTENT :]], 0)
    return early, late


def relaxation_map(sections):
    flow = np.eye(sections)
    positions = np.tril(np.ones((sections, sections)))
    for _ in range(RELAX):
        lower = np.zeros_like(positions)
        upper = np.zeros_like(positions)
        lower[1:] = positions[:-1] + flow[1:] - positions[1:]
        upper[:-1] = positions[1:] - flow[1:] - positions[:-1]
        positions = positions + STEP_SIZE * (lower + upper - ANCHOR_WEIGHT * positions)
    return positions.astype(np.float32)


def split(value):
    high = value.astype(BF)
    return high, (value - high.astype(F32)).astype(BF)


def dot(a, b):
    return jnp.dot(a, b, preferred_element_type=F32)


def spectra(patches, table_ref):
    lines = []
    for pair in range(0, len(patches), 2):
        both = jnp.concatenate(patches[pair : pair + 2], 1)
        line = dot(table_ref[: 2 * HALF], jnp.concatenate([both, both], 0))
        lines += [line[:, :EXTENT], line[:, EXTENT:]]
    high, low = split(jnp.concatenate(lines, 0))
    product = dot(jnp.concatenate([high, low, high], 1), table_ref[2 * HALF :])
    result = []
    for k in range(len(patches)):
        a = product[2 * HALF * k : 2 * HALF * k + HALF]
        b = product[2 * HALF * k + HALF : 2 * HALF * (k + 1)]
        result.append((a[:, :EXTENT] - b[:, EXTENT:], -(a[:, EXTENT:] + b[:, :EXTENT])))
    return result


def energy(ref):
    rows = []
    for n in range(ref.shape[0]):
        value = ref[n].astype(F32)
        rows.append(jnp.sum(value * value, axis=0, keepdims=True))
    total = jnp.sum(jnp.concatenate(rows, 0), axis=1, keepdims=True)
    return total * (1.0 / (EXTENT * EXTENT))


def own_kernel(route_ref, now_ref, table_ref, spectrum_ref, energy_ref, name_ref):
    slots = name_ref.shape[0]
    tile_count = route_ref.shape[1] // slots
    height = EXTENT // WIDE // tile_count
    owner = lax.axis_index("xy")
    lane = lax.broadcasted_iota(jnp.int32, (slots, tile_count * slots), 1)
    slot = lax.broadcasted_iota(jnp.int32, (slots, tile_count * slots), 0)
    names = jnp.broadcast_to(route_ref[...], lane.shape).astype(F32)
    place = lax.broadcasted_iota(jnp.int32, (slots, EXTENT), 1)
    here = place // (tile_count * height) == owner % WIDE
    row = jnp.zeros((slots, EXTENT), F32)
    for t in range(tile_count):
        own = jnp.sum(jnp.where(lane == slot + t * slots, names, 0.0), axis=1, keepdims=True)
        row = jnp.where(here & (place // height % tile_count == t), own, row)
    for p in range(slots):
        name_ref[p] = jnp.broadcast_to(row[p : p + 1], (8, EXTENT)).astype(BF)
    for pair in range(0, now_ref.shape[0], 2):
        for k, (real, imag) in enumerate(spectra([now_ref[pair], now_ref[pair + 1]], table_ref)):
            spectrum_ref[pair + k, :, :EXTENT] = real
            spectrum_ref[pair + k, :, EXTENT:] = imag
    energy_ref[...] = jnp.broadcast_to(energy(now_ref), energy_ref.shape)


def flow_kernel(peak_ref, low_ref, spectrum_ref, energy_ref, table_ref, last_ref, out_ref, inverse_ref, arrived):
    count = low_ref.shape[0]
    copy = pltpu.make_async_copy(last_ref, inverse_ref, arrived)
    copy.start()
    crosses = []
    for pair in range(0, count, 2):
        block = []
        for k, (lr, li) in enumerate(spectra([low_ref[pair], low_ref[pair + 1]], table_ref)):
            nr = spectrum_ref[pair + k, :, :EXTENT]
            ni = spectrum_ref[pair + k, :, EXTENT:]
            block.append(jnp.concatenate([nr * lr + ni * li, ni * lr - nr * li], 1))
        crosses.append(jnp.concatenate(block, 0))
    copy.wait()
    third = 6 * EXTENT
    fourth = jnp.concatenate(
        [
            inverse_ref[third : third + 2 * REACH],
            inverse_ref[third + 2 * REACH :, : 6 * HALF - 2 * EXTENT],
        ],
        1,
    )
    correlations = []
    for cross in crosses:
        high, low = split(cross)
        outer = dot(jnp.concatenate([high, low, high], 1), inverse_ref[:third])
        columns = []
        for k in range(2):
            block = outer[HALF * k : HALF * (k + 1)]
            columns.append(jnp.concatenate([block[:, :EXTENT], block[:, EXTENT:]], 0))
        high, low = split(jnp.concatenate(columns, 1))
        result = dot(fourth, jnp.concatenate([high, low, high], 0))
        correlations += [result[:, :EXTENT], result[:, EXTENT:]]

    scale = (SCORE_GAIN / EXTENT) / jnp.sqrt(energy_ref[:, :1] * energy(low_ref) + EPSILON)
    shape = (2 * REACH, EXTENT)
    row = lax.broadcasted_iota(jnp.int32, shape, 0) - REACH
    column = lax.broadcasted_iota(jnp.int32, shape, 1)
    scores, relatives, tops = [], [], []
    for n in range(count):
        rel_y = row - peak_ref[0, n]
        rel_x = ((column - peak_ref[1, n] + EXTENT // 2) & (EXTENT - 1)) - EXTENT // 2
        quarter = EXTENT // 4
        inside = (rel_y >= -quarter) & (rel_y < quarter) & (rel_x >= -quarter) & (rel_x < quarter)
        score = jnp.where(inside, correlations[n] * scale[n : n + 1], -1e30)
        scores.append(score)
        relatives.append((rel_y.astype(F32), rel_x[:1].astype(F32)))
        tops.append(jnp.max(score, axis=0, keepdims=True))
    top = jnp.max(jnp.concatenate(tops, 0), axis=1, keepdims=True)
    sums, sums_y, sums_x = [], [], []
    for n in range(count):
        weight = jnp.exp(scores[n] - top[n : n + 1])
        rel_y, rel_x = relatives[n]
        along = jnp.sum(weight, axis=0, keepdims=True)
        sums.append(along)
        sums_y.append(jnp.sum(weight * rel_y, axis=0, keepdims=True))
        sums_x.append(along * rel_x)
    total, total_y, total_x = (
        jnp.sum(jnp.concatenate(s, 0), axis=1, keepdims=True) for s in (sums, sums_y, sums_x)
    )
    node = lax.broadcasted_iota(jnp.int32, (count, EXTENT), 0)
    lane = lax.broadcasted_iota(jnp.int32, (count, EXTENT), 1)
    peak_y = jnp.zeros((count, EXTENT), jnp.int32)
    peak_x = jnp.zeros((count, EXTENT), jnp.int32)
    for n in range(count):
        peak_y = jnp.where(node == n, peak_ref[0, n], peak_y)
        peak_x = jnp.where(node == n, peak_ref[1, n], peak_x)
    flow_y = peak_y.astype(F32) + total_y / total
    flow_x = peak_x.astype(F32) + total_x / total
    flow = jnp.where(lane == node, flow_y, jnp.where(lane == node + count, flow_x, 0.0))
    flow = jnp.sum(flow, axis=0, keepdims=True)
    out_ref[...] = jnp.broadcast_to(flow[None], out_ref.shape)


def fill_band(target_ref, residual, offset, sub_sign):
    block = EXTENT
    lane = lax.broadcasted_iota(jnp.int32, (1, block), 1)
    tap = (lane - BAND).astype(F32) - residual
    raw = jnp.where(lane <= 2 * BAND, 1.0 / (1.0 + tap * tap), 0.0)
    norm = jnp.sum(raw, axis=1, keepdims=True)
    a = lax.broadcasted_iota(jnp.int32, (block, block), 0)
    b = lax.broadcasted_iota(jnp.int32, (block, block), 1)
    d = sub_sign * (a - b) - offset
    k = ((d + block // 2) & (block - 1)) - block // 2
    away = k.astype(F32) - residual
    value = (1.0 / (1.0 + away * away)) / norm
    blocks = {}
    for step in (-1, 0, 1):
        near = jnp.abs(d + sub_sign * step * block) <= BAND
        blocks[step] = jnp.where(near, value, 0.0).astype(BF)
    zero = jnp.zeros((block, block), BF)
    count = target_ref.shape[0] // block
    for i in range(count):
        for j in range(count):
            target_ref[i * block : (i + 1) * block, j * block : (j + 1) * block] = blocks.get(
                i - j, zero
            )


def render_kernel(map_ref, band_ref, flow_ref, tile_ref, *refs):
    *name_refs, position_ref, send_ref, col_ref, row_ref, pass_ref = refs
    sections = flow_ref.shape[0]
    tile_count, edge, _ = tile_ref.shape
    slots = send_ref.shape[0]
    section = lax.axis_index("gz")
    position = jnp.zeros(flow_ref.shape[1:], F32)
    for s in range(sections):
        position = position + map_ref[section, s] * flow_ref[s]
    position_ref[...] = position
    per_tile = NODES // tile_count
    lanes = lax.broadcasted_iota(jnp.int32, position.shape, 1)
    height = edge // slots
    columns = edge // EXTENT
    chunk = EXTENT
    for t in range(tile_count):
        offset_y, offset_x = band_ref[t, 0], band_ref[t, 1]
        shift_y, shift_x = (
            jnp.sum(jnp.where(lanes // per_tile == c * tile_count + t, position, 0.0), axis=1, keepdims=True)
            * (MIP_SCALE / per_tile)
            for c in range(2)
        )
        fill_band(col_ref, shift_x - offset_x.astype(F32), offset_x, 1)
        fill_band(row_ref, shift_y - offset_y.astype(F32), offset_y, -1)
        for c in range(edge // chunk):
            rows = slice(c * chunk, (c + 1) * chunk)
            pass_ref[rows, :] = dot(tile_ref[t, rows, :], col_ref[...]).astype(BF)
        for c in range(edge // chunk):
            rows = slice(c * chunk, (c + 1) * chunk)
            first, last = c * chunk // height, (c + 1) * chunk // height
            done = dot(row_ref[rows, :], pass_ref[...]).astype(BF)
            done = done.reshape(last - first, height, edge)
            for j in range(columns):
                at = (t * columns + j) * height
                send_ref[first:last, at : at + height, :] = done[:, :, j * EXTENT : (j + 1) * EXTENT]
    for name_ref in name_refs:
        send_ref[:, tile_count * columns * height :, :] = name_ref[...]


def gather_kernel(piece_ref, *refs):
    *name_refs, out_ref, data_ref = refs
    owners = piece_ref.shape[0]
    _, out_rows, edge = out_ref.shape
    height = edge // owners
    columns = edge // EXTENT
    tile_count = EXTENT // WIDE // height
    tail = tile_count * columns * height
    name_ref = name_refs[0] if name_refs else piece_ref.at[:, tail:]
    lane_row = lax.broadcasted_iota(jnp.int32, (EXTENT, EXTENT), 1) % height
    sub = lax.broadcasted_iota(jnp.int32, (EXTENT, EXTENT), 0)
    same = lane_row == sub % height
    for d in range(owners):
        for t in range(tile_count):
            at = (d * tile_count + t) * height
            for j in range(columns):
                source = (t * columns + j) * height
                data_ref[at : at + height, j * EXTENT : (j + 1) * EXTENT] = piece_ref[
                    d, source : source + height, :
                ]
    names = [
        sum(name_ref[d].astype(F32) for d in range(start, start + WIDE))[0:1]
        for start in range(0, owners, WIDE)
    ]
    for c in range(owners * out_rows // EXTENT):
        group = (sub // height + c * (EXTENT // height)).astype(F32)
        hits = [jnp.where(same & (name == group), 1.0, 0.0) for name in names]
        count = jnp.sum(sum(hits), axis=1, keepdims=True)
        total = dot(jnp.concatenate([hit.astype(BF) for hit in hits], 1), data_ref[...])
        total = total * (1.0 / jnp.maximum(count, 1.0))
        first, last = c * EXTENT // out_rows, (c + 1) * EXTENT // out_rows
        out_ref[first:last] = total.astype(BF).reshape(last - first, out_rows, edge)


def in_vmem():
    return pl.BlockSpec(memory_space=pltpu.VMEM)


def in_smem():
    return pl.BlockSpec(memory_space=pltpu.SMEM)


def params():
    return pltpu.CompilerParams(vmem_limit_bytes=40 * 1024 * 1024)


def exchange(value, axis):
    return lax.all_to_all(value, axis, split_axis=0, concat_axis=0, tiled=True)


def body(patches, peak_offsets, tiles, band_offsets, routes):
    sections = lax.axis_size("gz")
    owners = lax.axis_size("xy")
    tile_count, edge = tiles.shape[1], tiles.shape[-1]
    height = edge // PIECES
    share = 2
    count = patches.shape[1]

    below = lax.ppermute(patches, "gz", [(i, i + 1) for i in range(sections - 1)])
    early_table, late_table = (jnp.asarray(t) for t in dft_constants())
    spectrum, power, names = pl.pallas_call(
        own_kernel,
        out_shape=(
            jax.ShapeDtypeStruct((count, HALF, 2 * EXTENT), F32),
            jax.ShapeDtypeStruct((count, EXTENT), F32),
            jax.ShapeDtypeStruct((PIECES, 8, EXTENT), BF),
        ),
        in_specs=[in_vmem()] * 3,
        out_specs=(in_vmem(),) * 3,
        compiler_params=params(),
        cost_estimate=pl.CostEstimate(flops=10**9, bytes_accessed=2**20, transcendentals=0),
        name="own",
    )(routes[0].T, patches[0], early_table)
    flow = pl.pallas_call(
        flow_kernel,
        out_shape=jax.ShapeDtypeStruct((sections, 1, EXTENT), F32),
        in_specs=[in_smem()] + [in_vmem()] * 4 + [pl.BlockSpec(memory_space=pl.ANY)],
        out_specs=in_vmem(),
        scratch_shapes=[pltpu.VMEM(late_table.shape, BF), pltpu.SemaphoreType.DMA],
        compiler_params=params(),
        name="flow",
    )(peak_offsets[0].T, below[0], spectrum, power, early_table, late_table)
    flow = exchange(flow, "gz")

    linear = jnp.asarray(relaxation_map(sections))
    piece_rows = tile_count * height * edge // EXTENT

    def render(flow, image, *names):
        return pl.pallas_call(
            render_kernel,
            out_shape=(
                jax.ShapeDtypeStruct((1, EXTENT), F32),
                jax.ShapeDtypeStruct((PIECES, piece_rows + 8 * len(names), EXTENT), BF),
            ),
            in_specs=[in_smem(), in_smem()] + [in_vmem()] * (2 + len(names)),
            out_specs=(in_vmem(), in_vmem()),
            scratch_shapes=[pltpu.VMEM((edge, edge), BF)] * 3,
            compiler_params=params(),
            cost_estimate=pl.CostEstimate(flops=4 * 10**9, bytes_accessed=2**21, transcendentals=0),
            name="render",
        )(linear, band_offsets[0], flow, image, *names)

    def gather(*received):
        return pl.pallas_call(
            gather_kernel,
            out_shape=jax.ShapeDtypeStruct((owners, share * height, edge), BF),
            in_specs=[in_vmem()] * len(received),
            out_specs=in_vmem(),
            scratch_shapes=[pltpu.VMEM((owners * tile_count * height, edge), BF)],
            compiler_params=params(),
            name="gather",
        )(*received)

    def together(flow, image, names):
        position, whole = render(flow, image, names)
        return position, gather(exchange(whole, "xy"))

    def names_ahead(flow, image, names):
        names = exchange(names, "xy")
        position, pieces = render(flow, image)
        return position, gather(exchange(pieces, "xy"), names)

    second_core = lax.axis_index("gz") % 2 == 1
    position, cells = lax.cond(second_core, names_ahead, together, flow, tiles[0], names)
    cells = exchange(cells, "xy")
    rendered = cells.reshape(PIECES, share, height, edge).transpose(1, 0, 2, 3)
    rendered = rendered.reshape(1, share, edge, edge)
    return position[:, : 2 * count].reshape(1, 2, count), rendered


def solution(mesh):
    placed = (
        P("gz", "xy", None, None),
        P("gz", "xy", None),
        P("gz", "xy", None, None),
        P("gz", "xy", None),
        P("gz", "xy", None),
    )
    return jax.shard_map(
        body,
        mesh=mesh,
        in_specs=placed,
        out_specs=(P("gz", None, "xy"), P("gz", "xy", None, None)),
        check_vma=False,
    )
```

```python
import jax
import jax.numpy as jnp
import numpy as np
from jax import lax
from jax.experimental import pallas as pl
from jax.experimental.pallas import tpu as pltpu
from jax.sharding import PartitionSpec as P

PIECES = 32
NODES = 8
WIDE = 4
BAND = 6
RELAX = 3
EPSILON = 1e-06
STEP_SIZE = 0.25
ANCHOR_WEIGHT = 0.5
MIP_SCALE = 0.0625
SCORE_GAIN = 6.0

EXTENT = 128
HALF = 72
REACH = 40
BF = jnp.bfloat16
F32 = jnp.float32


def high_low(table):
    high = table.astype(jnp.bfloat16)
    low = (table - high.astype(np.float64)).astype(jnp.bfloat16)
    return high, low


def dft_constants():
    line = np.arange(EXTENT)
    phase = 2.0 * np.pi * ((line[:, None] * line[None, :]) % EXTENT) / EXTENT
    cos, sin = np.cos(phase), np.sin(phase)
    first = np.concatenate([cos[:HALF], sin[:HALF]], 0)
    first = np.concatenate(high_low(first), 1)
    second_high, second_low = high_low(np.concatenate([cos, sin], 1))
    second = np.concatenate([second_high, second_high, second_low], 0)
    third_high, third_low = high_low(np.block([[cos, sin], [-sin, cos]]))
    third = np.concatenate([third_high, third_high, third_low], 0)
    weight = np.where(line[:HALF] <= EXTENT // 2, 2.0, 0.0)
    weight[0] = weight[EXTENT // 2] = 1.0
    rows = (np.arange(-REACH, REACH) % EXTENT)[:, None]
    angle = 2.0 * np.pi * ((rows * line[None, :HALF]) % EXTENT) / EXTENT
    fourth = np.concatenate([weight * np.cos(angle), -weight * np.sin(angle)], 1)
    fourth_high, fourth_low = high_low(fourth / float(EXTENT * EXTENT))
    fourth = np.concatenate([fourth_high, fourth_high, fourth_low], 1)
    fourth = np.pad(fourth, ((0, 0), (0, 4 * EXTENT - fourth.shape[1])))
    early = np.concatenate([first, second], 0)
    late = np.concatenate([third, fourth[:, : 2 * EXTENT], fourth[:, 2 * EXTENT :]], 0)
    return early, late


def relaxation_map(sections):
    flow = np.eye(sections)
    positions = np.tril(np.ones((sections, sections)))
    for _ in range(RELAX):
        lower = np.zeros_like(positions)
        upper = np.zeros_like(positions)
        lower[1:] = positions[:-1] + flow[1:] - positions[1:]
        upper[:-1] = positions[1:] - flow[1:] - positions[:-1]
        positions = positions + STEP_SIZE * (lower + upper - ANCHOR_WEIGHT * positions)
    return positions.astype(np.float32)


def split(value):
    high = value.astype(BF)
    return high, (value - high.astype(F32)).astype(BF)


def dot(a, b):
    return jnp.dot(a, b, preferred_element_type=F32)


def spectra(patches, table_ref):
    lines = []
    for pair in range(0, len(patches), 2):
        both = jnp.concatenate(patches[pair : pair + 2], 1)
        line = dot(table_ref[: 2 * HALF], jnp.concatenate([both, both], 0))
        lines += [line[:, :EXTENT], line[:, EXTENT:]]
    high, low = split(jnp.concatenate(lines, 0))
    product = dot(jnp.concatenate([high, low, high], 1), table_ref[2 * HALF :])
    result = []
    for k in range(len(patches)):
        a = product[2 * HALF * k : 2 * HALF * k + HALF]
        b = product[2 * HALF * k + HALF : 2 * HALF * (k + 1)]
        result.append((a[:, :EXTENT] - b[:, EXTENT:], -(a[:, EXTENT:] + b[:, :EXTENT])))
    return result


def energy(ref):
    rows = []
    for n in range(ref.shape[0]):
        value = ref[n].astype(F32)
        rows.append(jnp.sum(value * value, axis=0, keepdims=True))
    total = jnp.sum(jnp.concatenate(rows, 0), axis=1, keepdims=True)
    return total * (1.0 / (EXTENT * EXTENT))


def own_kernel(route_ref, now_ref, table_ref, spectrum_ref, energy_ref, name_ref):
    slots = name_ref.shape[0]
    tile_count = route_ref.shape[1] // slots
    height = EXTENT // WIDE // tile_count
    owner = lax.axis_index("xy")
    lane = lax.broadcasted_iota(jnp.int32, (slots, tile_count * slots), 1)
    slot = lax.broadcasted_iota(jnp.int32, (slots, tile_count * slots), 0)
    names = jnp.broadcast_to(route_ref[...], lane.shape).astype(F32)
    place = lax.broadcasted_iota(jnp.int32, (slots, EXTENT), 1)
    here = place // (tile_count * height) == owner % WIDE
    row = jnp.zeros((slots, EXTENT), F32)
    for t in range(tile_count):
        own = jnp.sum(jnp.where(lane == slot + t * slots, names, 0.0), axis=1, keepdims=True)
        row = jnp.where(here & (place // height % tile_count == t), own, row)
    for p in range(slots):
        name_ref[p] = jnp.broadcast_to(row[p : p + 1], (8, EXTENT)).astype(BF)
    for pair in range(0, now_ref.shape[0], 2):
        for k, (real, imag) in enumerate(spectra([now_ref[pair], now_ref[pair + 1]], table_ref)):
            spectrum_ref[pair + k, :, :EXTENT] = real
            spectrum_ref[pair + k, :, EXTENT:] = imag
    energy_ref[...] = jnp.broadcast_to(energy(now_ref), energy_ref.shape)


def flow_kernel(peak_ref, low_ref, spectrum_ref, energy_ref, table_ref, last_ref, out_ref, inverse_ref, arrived):
    count = low_ref.shape[0]
    copy = pltpu.make_async_copy(last_ref, inverse_ref, arrived)
    copy.start()
    crosses = []
    for pair in range(0, count, 2):
        block = []
        for k, (lr, li) in enumerate(spectra([low_ref[pair], low_ref[pair + 1]], table_ref)):
            nr = spectrum_ref[pair + k, :, :EXTENT]
            ni = spectrum_ref[pair + k, :, EXTENT:]
            block.append(jnp.concatenate([nr * lr + ni * li, ni * lr - nr * li], 1))
        crosses.append(jnp.concatenate(block, 0))
    copy.wait()
    third = 6 * EXTENT
    fourth = jnp.concatenate(
        [
            inverse_ref[third : third + 2 * REACH],
            inverse_ref[third + 2 * REACH :, : 6 * HALF - 2 * EXTENT],
        ],
        1,
    )
    correlations = []
    for cross in crosses:
        high, low = split(cross)
        outer = dot(jnp.concatenate([high, low, high], 1), inverse_ref[:third])
        columns = []
        for k in range(2):
            block = outer[HALF * k : HALF * (k + 1)]
            columns.append(jnp.concatenate([block[:, :EXTENT], block[:, EXTENT:]], 0))
        high, low = split(jnp.concatenate(columns, 1))
        result = dot(fourth, jnp.concatenate([high, low, high], 0))
        correlations += [result[:, :EXTENT], result[:, EXTENT:]]

    scale = (SCORE_GAIN / EXTENT) / jnp.sqrt(energy_ref[:, :1] * energy(low_ref) + EPSILON)
    shape = (2 * REACH, EXTENT)
    row = lax.broadcasted_iota(jnp.int32, shape, 0) - REACH
    column = lax.broadcasted_iota(jnp.int32, shape, 1)
    scores, relatives, tops = [], [], []
    for n in range(count):
        rel_y = row - peak_ref[0, n]
        rel_x = ((column - peak_ref[1, n] + EXTENT // 2) & (EXTENT - 1)) - EXTENT // 2
        quarter = EXTENT // 4
        inside = (rel_y >= -quarter) & (rel_y < quarter) & (rel_x >= -quarter) & (rel_x < quarter)
        score = jnp.where(inside, correlations[n] * scale[n : n + 1], -1e30)
        scores.append(score)
        relatives.append((rel_y.astype(F32), rel_x[:1].astype(F32)))
        tops.append(jnp.max(score, axis=0, keepdims=True))
    top = jnp.max(jnp.concatenate(tops, 0), axis=1, keepdims=True)
    sums, sums_y, sums_x = [], [], []
    for n in range(count):
        weight = jnp.exp(scores[n] - top[n : n + 1])
        rel_y, rel_x = relatives[n]
        along = jnp.sum(weight, axis=0, keepdims=True)
        sums.append(along)
        sums_y.append(jnp.sum(weight * rel_y, axis=0, keepdims=True))
        sums_x.append(along * rel_x)
    total, total_y, total_x = (
        jnp.sum(jnp.concatenate(s, 0), axis=1, keepdims=True) for s in (sums, sums_y, sums_x)
    )
    node = lax.broadcasted_iota(jnp.int32, (count, EXTENT), 0)
    lane = lax.broadcasted_iota(jnp.int32, (count, EXTENT), 1)
    peak_y = jnp.zeros((count, EXTENT), jnp.int32)
    peak_x = jnp.zeros((count, EXTENT), jnp.int32)
    for n in range(count):
        peak_y = jnp.where(node == n, peak_ref[0, n], peak_y)
        peak_x = jnp.where(node == n, peak_ref[1, n], peak_x)
    flow_y = peak_y.astype(F32) + total_y / total
    flow_x = peak_x.astype(F32) + total_x / total
    flow = jnp.where(lane == node, flow_y, jnp.where(lane == node + count, flow_x, 0.0))
    flow = jnp.sum(flow, axis=0, keepdims=True)
    out_ref[...] = jnp.broadcast_to(flow[None], out_ref.shape)


def fill_band(target_ref, residual, offset, sub_sign):
    block = EXTENT
    lane = lax.broadcasted_iota(jnp.int32, (1, block), 1)
    tap = (lane - BAND).astype(F32) - residual
    raw = jnp.where(lane <= 2 * BAND, 1.0 / (1.0 + tap * tap), 0.0)
    norm = jnp.sum(raw, axis=1, keepdims=True)
    a = lax.broadcasted_iota(jnp.int32, (block, block), 0)
    b = lax.broadcasted_iota(jnp.int32, (block, block), 1)
    d = sub_sign * (a - b) - offset
    k = ((d + block // 2) & (block - 1)) - block // 2
    away = k.astype(F32) - residual
    value = (1.0 / (1.0 + away * away)) / norm
    blocks = {}
    for step in (-1, 0, 1):
        near = jnp.abs(d + sub_sign * step * block) <= BAND
        blocks[step] = jnp.where(near, value, 0.0).astype(BF)
    zero = jnp.zeros((block, block), BF)
    count = target_ref.shape[0] // block
    for i in range(count):
        for j in range(count):
            target_ref[i * block : (i + 1) * block, j * block : (j + 1) * block] = blocks.get(
                i - j, zero
            )


def render_kernel(map_ref, band_ref, flow_ref, tile_ref, *refs):
    name_ref, position_ref, send_ref, *name_outs, col_ref, row_ref, pass_ref = refs
    sections = flow_ref.shape[0]
    tile_count, edge, _ = tile_ref.shape
    slots = send_ref.shape[0]
    section = lax.axis_index("gz")
    position = jnp.zeros(flow_ref.shape[1:], F32)
    for s in range(sections):
        position = position + map_ref[section, s] * flow_ref[s]
    position_ref[...] = position
    per_tile = NODES // tile_count
    lanes = lax.broadcasted_iota(jnp.int32, position.shape, 1)
    height = edge // slots
    columns = edge // EXTENT
    chunk = EXTENT
    for t in range(tile_count):
        offset_y, offset_x = band_ref[t, 0], band_ref[t, 1]
        shift_y, shift_x = (
            jnp.sum(jnp.where(lanes // per_tile == c * tile_count + t, position, 0.0), axis=1, keepdims=True)
            * (MIP_SCALE / per_tile)
            for c in range(2)
        )
        fill_band(col_ref, shift_x - offset_x.astype(F32), offset_x, 1)
        fill_band(row_ref, shift_y - offset_y.astype(F32), offset_y, -1)
        for c in range(edge // chunk):
            rows = slice(c * chunk, (c + 1) * chunk)
            pass_ref[rows, :] = dot(tile_ref[t, rows, :], col_ref[...]).astype(BF)
        for c in range(edge // chunk):
            rows = slice(c * chunk, (c + 1) * chunk)
            first, last = c * chunk // height, (c + 1) * chunk // height
            done = dot(row_ref[rows, :], pass_ref[...]).astype(BF)
            done = done.reshape(last - first, height, edge)
            for j in range(columns):
                at = (t * columns + j) * height
                send_ref[first:last, at : at + height, :] = done[:, :, j * EXTENT : (j + 1) * EXTENT]
    if name_outs:
        name_outs[0][...] = name_ref[...]
    else:
        send_ref[:, tile_count * columns * height :, :] = name_ref[...]


def gather_kernel(piece_ref, *refs):
    *name_refs, out_ref, data_ref = refs
    owners = piece_ref.shape[0]
    _, out_rows, edge = out_ref.shape
    height = edge // owners
    columns = edge // EXTENT
    tile_count = EXTENT // WIDE // height
    tail = tile_count * columns * height
    name_ref = name_refs[0] if name_refs else piece_ref.at[:, tail:]
    lane_row = lax.broadcasted_iota(jnp.int32, (EXTENT, EXTENT), 1) % height
    sub = lax.broadcasted_iota(jnp.int32, (EXTENT, EXTENT), 0)
    same = lane_row == sub % height
    for d in range(owners):
        for t in range(tile_count):
            at = (d * tile_count + t) * height
            for j in range(columns):
                source = (t * columns + j) * height
                data_ref[at : at + height, j * EXTENT : (j + 1) * EXTENT] = piece_ref[
                    d, source : source + height, :
                ]
    names = [
        sum(name_ref[d].astype(F32) for d in range(start, start + WIDE))[0:1]
        for start in range(0, owners, WIDE)
    ]
    for c in range(owners * out_rows // EXTENT):
        group = (sub // height + c * (EXTENT // height)).astype(F32)
        hits = [jnp.where(same & (name == group), 1.0, 0.0) for name in names]
        count = jnp.sum(sum(hits), axis=1, keepdims=True)
        total = dot(jnp.concatenate([hit.astype(BF) for hit in hits], 1), data_ref[...])
        total = total * (1.0 / jnp.maximum(count, 1.0))
        first, last = c * EXTENT // out_rows, (c + 1) * EXTENT // out_rows
        out_ref[first:last] = total.astype(BF).reshape(last - first, out_rows, edge)


def in_vmem():
    return pl.BlockSpec(memory_space=pltpu.VMEM)


def in_smem():
    return pl.BlockSpec(memory_space=pltpu.SMEM)


def params():
    return pltpu.CompilerParams(vmem_limit_bytes=40 * 1024 * 1024)


def exchange(value, axis):
    return lax.all_to_all(value, axis, split_axis=0, concat_axis=0, tiled=True)


def body(patches, peak_offsets, tiles, band_offsets, routes):
    sections = lax.axis_size("gz")
    owners = lax.axis_size("xy")
    tile_count, edge = tiles.shape[1], tiles.shape[-1]
    height = edge // PIECES
    share = 2
    count = patches.shape[1]

    below = lax.ppermute(patches, "gz", [(i, i + 1) for i in range(sections - 1)])
    early_table, late_table = (jnp.asarray(t) for t in dft_constants())
    spectrum, power, names = pl.pallas_call(
        own_kernel,
        out_shape=(
            jax.ShapeDtypeStruct((count, HALF, 2 * EXTENT), F32),
            jax.ShapeDtypeStruct((count, EXTENT), F32),
            jax.ShapeDtypeStruct((PIECES, 8, EXTENT), BF),
        ),
        in_specs=[in_vmem()] * 3,
        out_specs=(in_vmem(),) * 3,
        compiler_params=params(),
        cost_estimate=pl.CostEstimate(flops=10**9, bytes_accessed=2**20, transcendentals=0),
        name="own",
    )(routes[0].T, patches[0], early_table)
    flow = pl.pallas_call(
        flow_kernel,
        out_shape=jax.ShapeDtypeStruct((sections, 1, EXTENT), F32),
        in_specs=[in_smem()] + [in_vmem()] * 4 + [pl.BlockSpec(memory_space=pl.ANY)],
        out_specs=in_vmem(),
        scratch_shapes=[pltpu.VMEM(late_table.shape, BF), pltpu.SemaphoreType.DMA],
        compiler_params=params(),
        name="flow",
    )(peak_offsets[0].T, below[0], spectrum, power, early_table, late_table)
    flow = exchange(flow, "gz")

    linear = jnp.asarray(relaxation_map(sections))
    piece_rows = tile_count * height * edge // EXTENT

    def render(flow, image, names, apart):
        rows = (piece_rows, names.shape[1]) if apart else (piece_rows + names.shape[1],)
        shapes = tuple(jax.ShapeDtypeStruct((PIECES, r, EXTENT), BF) for r in rows)
        return pl.pallas_call(
            render_kernel,
            out_shape=(jax.ShapeDtypeStruct((1, EXTENT), F32),) + shapes,
            in_specs=[in_smem(), in_smem()] + [in_vmem()] * 3,
            out_specs=(in_vmem(),) * (1 + len(rows)),
            scratch_shapes=[pltpu.VMEM((edge, edge), BF)] * 3,
            compiler_params=params(),
            name="render",
        )(linear, band_offsets[0], flow, image, names)

    def gather(*received):
        return pl.pallas_call(
            gather_kernel,
            out_shape=jax.ShapeDtypeStruct((owners, share * height, edge), BF),
            in_specs=[in_vmem()] * len(received),
            out_specs=in_vmem(),
            scratch_shapes=[pltpu.VMEM((owners * tile_count * height, edge), BF)],
            compiler_params=params(),
            name="gather",
        )(*received)

    def together(flow, image, names):
        position, whole = render(flow, image, names, False)
        return position, gather(exchange(whole, "xy"))

    def names_ahead(flow, image, names):
        position, pieces, names = render(flow, image, names, True)
        names = exchange(names, "xy")
        pieces, names = lax.optimization_barrier((pieces, names))
        return position, gather(exchange(pieces, "xy"), names)

    second_core = lax.axis_index("gz") % 2 == 1
    position, cells = lax.cond(second_core, names_ahead, together, flow, tiles[0], names)
    cells = exchange(cells, "xy")
    rendered = cells.reshape(PIECES, share, height, edge).transpose(1, 0, 2, 3)
    rendered = rendered.reshape(1, share, edge, edge)
    return position[:, : 2 * count].reshape(1, 2, count), rendered


def solution(mesh):
    placed = (
        P("gz", "xy", None, None),
        P("gz", "xy", None),
        P("gz", "xy", None, None),
        P("gz", "xy", None),
        P("gz", "xy", None),
    )
    return jax.shard_map(
        body,
        mesh=mesh,
        in_specs=placed,
        out_specs=(P("gz", None, "xy"), P("gz", "xy", None, None)),
        check_vma=False,
    )
```

```python
import jax
import jax.numpy as jnp
import numpy as np
from jax import lax
from jax.experimental import pallas as pl
from jax.experimental.pallas import tpu as pltpu
from jax.sharding import PartitionSpec as P

PIECES = 32
WIDE = 4
BAND = 6
RELAX = 3
EPSILON = 1e-06
STEP_SIZE = 0.25
ANCHOR_WEIGHT = 0.5
MIP_SCALE = 0.0625
SCORE_GAIN = 6.0

EXTENT = 128
HALF = 72
REACH = 40
BF = jnp.bfloat16
F32 = jnp.float32


def high_low(table):
    high = table.astype(jnp.bfloat16)
    low = (table - high.astype(np.float64)).astype(jnp.bfloat16)
    return high, low


def dft_constants():
    line = np.arange(EXTENT)
    phase = 2.0 * np.pi * ((line[:, None] * line[None, :]) % EXTENT) / EXTENT
    cos, sin = np.cos(phase), np.sin(phase)
    first = np.concatenate([cos[:HALF], sin[:HALF]], 0)
    first = np.concatenate(high_low(first), 1)
    second_high, second_low = high_low(np.concatenate([cos, sin], 1))
    second = np.concatenate([second_high, second_high, second_low], 0)
    third_high, third_low = high_low(np.block([[cos, sin], [-sin, cos]]))
    third = np.concatenate([third_high, third_high, third_low], 0)
    weight = np.where(line[:HALF] <= EXTENT // 2, 2.0, 0.0)
    weight[0] = weight[EXTENT // 2] = 1.0
    rows = (np.arange(-REACH, REACH) % EXTENT)[:, None]
    angle = 2.0 * np.pi * ((rows * line[None, :HALF]) % EXTENT) / EXTENT
    fourth = np.concatenate([weight * np.cos(angle), -weight * np.sin(angle)], 1)
    fourth_high, fourth_low = high_low(fourth / float(EXTENT * EXTENT))
    fourth = np.concatenate([fourth_high, fourth_high, fourth_low], 1)
    fourth = np.pad(fourth, ((0, 0), (0, 4 * EXTENT - fourth.shape[1])))
    early = np.concatenate([first, second], 0)
    late = np.concatenate([third, fourth[:, : 2 * EXTENT], fourth[:, 2 * EXTENT :]], 0)
    return early, late


def relaxation_map(sections):
    flow = np.eye(sections)
    positions = np.tril(np.ones((sections, sections)))
    for _ in range(RELAX):
        lower = np.zeros_like(positions)
        upper = np.zeros_like(positions)
        lower[1:] = positions[:-1] + flow[1:] - positions[1:]
        upper[:-1] = positions[1:] - flow[1:] - positions[:-1]
        positions = positions + STEP_SIZE * (lower + upper - ANCHOR_WEIGHT * positions)
    return positions.astype(np.float32)


def split(value):
    high = value.astype(BF)
    return high, (value - high.astype(F32)).astype(BF)


def dot(a, b):
    return jnp.dot(a, b, preferred_element_type=F32)


def spectra(patches, table_ref):
    lines = []
    for pair in range(0, len(patches), 2):
        both = jnp.concatenate(patches[pair : pair + 2], 1)
        line = dot(table_ref[: 2 * HALF], jnp.concatenate([both, both], 0))
        lines += [line[:, :EXTENT], line[:, EXTENT:]]
    high, low = split(jnp.concatenate(lines, 0))
    product = dot(jnp.concatenate([high, low, high], 1), table_ref[2 * HALF :])
    result = []
    for k in range(len(patches)):
        a = product[2 * HALF * k : 2 * HALF * k + HALF]
        b = product[2 * HALF * k + HALF : 2 * HALF * (k + 1)]
        result.append((a[:, :EXTENT] - b[:, EXTENT:], -(a[:, EXTENT:] + b[:, :EXTENT])))
    return result


def energy(ref):
    rows = []
    for n in range(ref.shape[0]):
        value = ref[n].astype(F32)
        rows.append(jnp.sum(value * value, axis=0, keepdims=True))
    total = jnp.sum(jnp.concatenate(rows, 0), axis=1, keepdims=True)
    return total * (1.0 / (EXTENT * EXTENT))


def own_kernel(now_ref, table_ref, spectrum_ref, energy_ref):
    for pair in range(0, now_ref.shape[0], 2):
        for k, (real, imag) in enumerate(spectra([now_ref[pair], now_ref[pair + 1]], table_ref)):
            spectrum_ref[pair + k, :, :EXTENT] = real
            spectrum_ref[pair + k, :, EXTENT:] = imag
    energy_ref[...] = jnp.broadcast_to(energy(now_ref), energy_ref.shape)


def write_names(owner, route_ref, name_ref):
    slots = name_ref.shape[0]
    tile_count = route_ref.shape[1] // slots
    height = EXTENT // WIDE // tile_count
    lane = lax.broadcasted_iota(jnp.int32, (slots, tile_count * slots), 1)
    slot = lax.broadcasted_iota(jnp.int32, (slots, tile_count * slots), 0)
    names = jnp.broadcast_to(route_ref[...], lane.shape).astype(F32)
    place = lax.broadcasted_iota(jnp.int32, (slots, EXTENT), 1)
    here = place // (tile_count * height) == owner % WIDE
    row = jnp.zeros((slots, EXTENT), F32)
    for t in range(tile_count):
        own = jnp.sum(jnp.where(lane == slot + t * slots, names, 0.0), axis=1, keepdims=True)
        row = jnp.where(here & (place // height % tile_count == t), own, row)
    for p in range(slots):
        name_ref[p] = jnp.broadcast_to(row[p : p + 1], (8, EXTENT)).astype(BF)


def flow_kernel(place_ref, peak_ref, route_ref, low_ref, spectrum_ref, energy_ref, table_ref, inverse_ref, out_ref, name_ref):
    count = low_ref.shape[0]
    write_names(place_ref[0], route_ref, name_ref)
    crosses = []
    for pair in range(0, count, 2):
        block = []
        for k, (lr, li) in enumerate(spectra([low_ref[pair], low_ref[pair + 1]], table_ref)):
            nr = spectrum_ref[pair + k, :, :EXTENT]
            ni = spectrum_ref[pair + k, :, EXTENT:]
            block.append(jnp.concatenate([nr * lr + ni * li, ni * lr - nr * li], 1))
        crosses.append(jnp.concatenate(block, 0))
    third = 6 * EXTENT
    fourth = jnp.concatenate(
        [
            inverse_ref[third : third + 2 * REACH],
            inverse_ref[third + 2 * REACH :, : 6 * HALF - 2 * EXTENT],
        ],
        1,
    )
    correlations = []
    for cross in crosses:
        high, low = split(cross)
        outer = dot(jnp.concatenate([high, low, high], 1), inverse_ref[:third])
        columns = []
        for k in range(2):
            block = outer[HALF * k : HALF * (k + 1)]
            columns.append(jnp.concatenate([block[:, :EXTENT], block[:, EXTENT:]], 0))
        high, low = split(jnp.concatenate(columns, 1))
        result = dot(fourth, jnp.concatenate([high, low, high], 0))
        correlations += [result[:, :EXTENT], result[:, EXTENT:]]

    scale = (SCORE_GAIN / EXTENT) / jnp.sqrt(energy_ref[:, :1] * energy(low_ref) + EPSILON)
    shape = (2 * REACH, EXTENT)
    row = lax.broadcasted_iota(jnp.int32, shape, 0) - REACH
    column = lax.broadcasted_iota(jnp.int32, shape, 1)
    scores, relatives, tops = [], [], []
    for n in range(count):
        rel_y = row - peak_ref[0, n]
        rel_x = ((column - peak_ref[1, n] + EXTENT // 2) & (EXTENT - 1)) - EXTENT // 2
        quarter = EXTENT // 4
        inside = (rel_y >= -quarter) & (rel_y < quarter) & (rel_x >= -quarter) & (rel_x < quarter)
        score = jnp.where(inside, correlations[n] * scale[n : n + 1], -1e30)
        scores.append(score)
        relatives.append((rel_y.astype(F32), rel_x[:1].astype(F32)))
        tops.append(jnp.max(score, axis=0, keepdims=True))
    top = jnp.max(jnp.concatenate(tops, 0), axis=1, keepdims=True)
    sums, sums_y, sums_x = [], [], []
    for n in range(count):
        weight = jnp.exp(scores[n] - top[n : n + 1])
        rel_y, rel_x = relatives[n]
        along = jnp.sum(weight, axis=0, keepdims=True)
        sums.append(along)
        sums_y.append(jnp.sum(weight * rel_y, axis=0, keepdims=True))
        sums_x.append(along * rel_x)
    total, total_y, total_x = (
        jnp.sum(jnp.concatenate(s, 0), axis=1, keepdims=True) for s in (sums, sums_y, sums_x)
    )
    node = lax.broadcasted_iota(jnp.int32, (count, EXTENT), 0)
    lane = lax.broadcasted_iota(jnp.int32, (count, EXTENT), 1)
    peak_y = jnp.zeros((count, EXTENT), jnp.int32)
    peak_x = jnp.zeros((count, EXTENT), jnp.int32)
    for n in range(count):
        peak_y = jnp.where(node == n, peak_ref[0, n], peak_y)
        peak_x = jnp.where(node == n, peak_ref[1, n], peak_x)
    flow_y = peak_y.astype(F32) + total_y / total
    flow_x = peak_x.astype(F32) + total_x / total
    flow = jnp.where(lane == node, flow_y, jnp.where(lane == node + count, flow_x, 0.0))
    flow = jnp.sum(flow, axis=0, keepdims=True)
    out_ref[...] = jnp.broadcast_to(flow[None], out_ref.shape)


def fill_band(target_ref, residual, offset, sub_sign):
    block = EXTENT
    lane = lax.broadcasted_iota(jnp.int32, (1, block), 1)
    tap = (lane - BAND).astype(F32) - residual
    raw = jnp.where(lane <= 2 * BAND, 1.0 / (1.0 + tap * tap), 0.0)
    norm = jnp.sum(raw, axis=1, keepdims=True)
    a = lax.broadcasted_iota(jnp.int32, (block, block), 0)
    b = lax.broadcasted_iota(jnp.int32, (block, block), 1)
    d = sub_sign * (a - b) - offset
    k = ((d + block // 2) & (block - 1)) - block // 2
    away = k.astype(F32) - residual
    value = (1.0 / (1.0 + away * away)) / norm
    blocks = {}
    for step in (-1, 0, 1):
        near = jnp.abs(d + sub_sign * step * block) <= BAND
        blocks[step] = jnp.where(near, value, 0.0).astype(BF)
    zero = jnp.zeros((block, block), BF)
    count = target_ref.shape[0] // block
    for i in range(count):
        for j in range(count):
            target_ref[i * block : (i + 1) * block, j * block : (j + 1) * block] = blocks.get(
                i - j, zero
            )


def render_kernel(place_ref, map_ref, band_ref, flow_ref, name_ref, tile_ref, position_ref, send_ref, *scratch):
    sections = flow_ref.shape[0]
    tile_count, edge, _ = tile_ref.shape
    slots = send_ref.shape[0]
    section = place_ref[1]
    second_core = place_ref[2] == 1

    def slot_of(p):
        return jnp.where(second_core, p % WIDE * (slots // WIDE) + p // WIDE, p)

    position = jnp.zeros(flow_ref.shape[1:], F32)
    for s in range(sections):
        position = position + map_ref[section, s] * flow_ref[s]
    nodes = position_ref.shape[1]
    for c in range(2):
        position_ref[c : c + 1, :] = position[:, c * nodes : (c + 1) * nodes]
    per_tile = nodes // tile_count
    lanes = lax.broadcasted_iota(jnp.int32, position.shape, 1)
    height = edge // slots
    columns = edge // EXTENT
    chunk = EXTENT
    for t in range(tile_count):
        col_ref, row_ref, pass_ref = scratch[3 * t : 3 * t + 3]
        offset_y, offset_x = band_ref[t, 0], band_ref[t, 1]
        shift_y, shift_x = (
            jnp.sum(jnp.where(lanes // per_tile == c * tile_count + t, position, 0.0), axis=1, keepdims=True)
            * (MIP_SCALE / per_tile)
            for c in range(2)
        )
        fill_band(col_ref, shift_x - offset_x.astype(F32), offset_x, 1)
        fill_band(row_ref, shift_y - offset_y.astype(F32), offset_y, -1)
        for c in range(edge // chunk):
            rows = slice(c * chunk, (c + 1) * chunk)
            pass_ref[rows, :] = dot(tile_ref[t, rows, :], col_ref[...]).astype(BF)
        for c in range(edge // chunk):
            rows = slice(c * chunk, (c + 1) * chunk)
            first, last = c * chunk // height, (c + 1) * chunk // height
            done = dot(row_ref[rows, :], pass_ref[...]).astype(BF)
            done = done.reshape(last - first, height, edge)
            for p in range(first, last):
                for j in range(columns):
                    at = (t * columns + j) * height
                    send_ref[slot_of(p), at : at + height, :] = done[
                        p - first, :, j * EXTENT : (j + 1) * EXTENT
                    ]
    tail = tile_count * columns * height
    for p in range(slots):
        send_ref[slot_of(p), tail:, :] = name_ref[p]


def gather_kernel(piece_ref, out_ref, data_ref):
    owners, rows, _ = piece_ref.shape
    _, out_rows, edge = out_ref.shape
    height = edge // owners
    columns = edge // EXTENT
    tile_count = (rows - 8) // (columns * height)
    tail = rows - 8
    share = EXTENT // (tile_count * height)
    lane_row = lax.broadcasted_iota(jnp.int32, (EXTENT, EXTENT), 1) % height
    sub = lax.broadcasted_iota(jnp.int32, (EXTENT, EXTENT), 0)
    same = lane_row == sub % height
    for d in range(owners):
        for t in range(tile_count):
            at = (d * tile_count + t) * height
            for j in range(columns):
                source = (t * columns + j) * height
                data_ref[at : at + height, j * EXTENT : (j + 1) * EXTENT] = piece_ref[
                    d, source : source + height, :
                ]
    names = [
        sum(piece_ref[d, tail : tail + 8, :].astype(F32) for d in range(start, start + share))[0:1]
        for start in range(0, owners, share)
    ]
    for c in range(owners * out_rows // EXTENT):
        group = (sub // height + c * (EXTENT // height)).astype(F32)
        hits = [jnp.where(same & (name == group), 1.0, 0.0) for name in names]
        count = jnp.sum(sum(hits), axis=1, keepdims=True)
        total = dot(jnp.concatenate([hit.astype(BF) for hit in hits], 1), data_ref[...])
        total = total * (1.0 / jnp.maximum(count, 1.0))
        first, last = c * EXTENT // out_rows, (c + 1) * EXTENT // out_rows
        out_ref[first:last] = total.astype(BF).reshape(last - first, out_rows, edge)


def in_vmem():
    return pl.BlockSpec(memory_space=pltpu.VMEM)


def in_smem():
    return pl.BlockSpec(memory_space=pltpu.SMEM)


def params():
    return pltpu.CompilerParams(vmem_limit_bytes=40 * 1024 * 1024)


def exchange(value, axis, groups=None):
    return lax.all_to_all(
        value, axis, split_axis=0, concat_axis=0, tiled=True, axis_index_groups=groups
    )


def exchange_x_then_z(value):
    owners, rows, lanes = value.shape
    high = owners // WIDE
    along_x = [[z * WIDE + x for x in range(WIDE)] for z in range(high)]
    along_z = [[z * WIDE + x for z in range(high)] for x in range(WIDE)]
    value = exchange(value.reshape(WIDE, high * rows, lanes), "xy", along_x)
    value = value.reshape(WIDE, high, rows, lanes).transpose(1, 0, 2, 3)
    value = exchange(value.reshape(high, WIDE * rows, lanes), "xy", along_z)
    return value.reshape(owners, rows, lanes)


def body(patches, peak_offsets, tiles, band_offsets, routes):
    sections = lax.axis_size("gz")
    owners = lax.axis_size("xy")
    tile_count, edge = tiles.shape[1], tiles.shape[-1]
    height = edge // PIECES
    share = 2
    count = patches.shape[1]

    section = lax.axis_index("gz")
    below = lax.ppermute(patches, "gz", [(i, i + 1) for i in range(sections - 1)])
    early_table, late_table = (jnp.asarray(t) for t in dft_constants())
    second_core = section % 2 == 1
    place = jnp.stack([lax.axis_index("xy"), section, second_core.astype(jnp.int32)])
    spectrum, power = pl.pallas_call(
        own_kernel,
        out_shape=(
            jax.ShapeDtypeStruct((count, HALF, 2 * EXTENT), F32),
            jax.ShapeDtypeStruct((count, EXTENT), F32),
        ),
        in_specs=[in_vmem()] * 2,
        out_specs=(in_vmem(),) * 2,
        compiler_params=params(),
        cost_estimate=pl.CostEstimate(flops=10**9, bytes_accessed=2**20, transcendentals=0),
        name="own",
    )(patches[0], early_table)
    flow, names = pl.pallas_call(
        flow_kernel,
        out_shape=(
            jax.ShapeDtypeStruct((sections, 1, EXTENT), F32),
            jax.ShapeDtypeStruct((PIECES, 8, EXTENT), BF),
        ),
        in_specs=[in_smem()] * 2 + [in_vmem()] * 6,
        out_specs=(in_vmem(),) * 2,
        compiler_params=params(),
        name="flow",
    )(place, peak_offsets[0].T, routes[0].T, below[0], spectrum, power, early_table, late_table)
    flow = exchange(flow, "gz")

    position, pieces = pl.pallas_call(
        render_kernel,
        out_shape=(
            jax.ShapeDtypeStruct((2, count), F32),
            jax.ShapeDtypeStruct((PIECES, tile_count * height * edge // EXTENT + 8, EXTENT), BF),
        ),
        in_specs=[in_smem()] * 3 + [in_vmem()] * 3,
        out_specs=(in_vmem(), in_vmem()),
        scratch_shapes=[pltpu.VMEM((edge, edge), BF)] * (3 * tile_count),
        compiler_params=params(),
        name="render",
    )(place, jnp.asarray(relaxation_map(sections)), band_offsets[0], flow, names, tiles[0])
    pieces = lax.cond(
        second_core,
        exchange_x_then_z,
        lambda value: exchange(value, "xy"),
        pieces,
    )

    cells = pl.pallas_call(
        gather_kernel,
        out_shape=jax.ShapeDtypeStruct((owners, share * height, edge), BF),
        in_specs=[in_vmem()],
        out_specs=in_vmem(),
        scratch_shapes=[pltpu.VMEM((owners * tile_count * height, edge), BF)],
        compiler_params=params(),
        name="gather",
    )(pieces)
    cells = exchange(cells, "xy")
    rendered = cells.reshape(PIECES, share, height, edge).transpose(1, 0, 2, 3)
    rendered = rendered.reshape(1, share, edge, edge)
    return position[None], rendered


def solution(mesh):
    placed = (
        P("gz", "xy", None, None),
        P("gz", "xy", None),
        P("gz", "xy", None, None),
        P("gz", "xy", None),
        P("gz", "xy", None),
    )
    return jax.shard_map(
        body,
        mesh=mesh,
        in_specs=placed,
        out_specs=(P("gz", None, "xy"), P("gz", "xy", None, None)),
        check_vma=False,
    )
```

```python
import jax
import jax.numpy as jnp
import numpy as np
from jax import lax
from jax.experimental import pallas as pl
from jax.experimental.pallas import tpu as pltpu
from jax.sharding import PartitionSpec as P

PIECES = 32
WIDE = 4
BAND = 6
RELAX = 3
EPSILON = 1e-06
STEP_SIZE = 0.25
ANCHOR_WEIGHT = 0.5
MIP_SCALE = 0.0625
SCORE_GAIN = 6.0

EXTENT = 128
HALF = 72
REACH = 40
BF = jnp.bfloat16
F32 = jnp.float32


def high_low(table):
    high = table.astype(jnp.bfloat16)
    low = (table - high.astype(np.float64)).astype(jnp.bfloat16)
    return high, low


def dft_constants():
    line = np.arange(EXTENT)
    phase = 2.0 * np.pi * ((line[:, None] * line[None, :]) % EXTENT) / EXTENT
    cos, sin = np.cos(phase), np.sin(phase)
    first = np.concatenate([cos[:HALF], sin[:HALF]], 0)
    first = np.concatenate(high_low(first), 1)
    second_high, second_low = high_low(np.concatenate([cos, sin], 1))
    second = np.concatenate([second_high, second_high, second_low], 0)
    third_high, third_low = high_low(np.block([[cos, sin], [-sin, cos]]))
    third = np.concatenate([third_high, third_high, third_low], 0)
    weight = np.where(line[:HALF] <= EXTENT // 2, 2.0, 0.0)
    weight[0] = weight[EXTENT // 2] = 1.0
    rows = (np.arange(-REACH, REACH) % EXTENT)[:, None]
    angle = 2.0 * np.pi * ((rows * line[None, :HALF]) % EXTENT) / EXTENT
    fourth = np.concatenate([weight * np.cos(angle), -weight * np.sin(angle)], 1)
    fourth_high, fourth_low = high_low(fourth / float(EXTENT * EXTENT))
    fourth = np.concatenate([fourth_high, fourth_high, fourth_low], 1)
    fourth = np.pad(fourth, ((0, 0), (0, 4 * EXTENT - fourth.shape[1])))
    early = np.concatenate([first, second], 0)
    late = np.concatenate([third, fourth[:, : 2 * EXTENT], fourth[:, 2 * EXTENT :]], 0)
    return early, late


def relaxation_map(sections):
    flow = np.eye(sections)
    positions = np.tril(np.ones((sections, sections)))
    for _ in range(RELAX):
        lower = np.zeros_like(positions)
        upper = np.zeros_like(positions)
        lower[1:] = positions[:-1] + flow[1:] - positions[1:]
        upper[:-1] = positions[1:] - flow[1:] - positions[:-1]
        positions = positions + STEP_SIZE * (lower + upper - ANCHOR_WEIGHT * positions)
    return positions.astype(np.float32)


def split(value):
    high = value.astype(BF)
    return high, (value - high.astype(F32)).astype(BF)


def dot(a, b):
    return jnp.dot(a, b, preferred_element_type=F32)


def spectra(patches, table_ref):
    lines = []
    for pair in range(0, len(patches), 2):
        both = jnp.concatenate(patches[pair : pair + 2], 1)
        line = dot(table_ref[: 2 * HALF], jnp.concatenate([both, both], 0))
        lines += [line[:, :EXTENT], line[:, EXTENT:]]
    high, low = split(jnp.concatenate(lines, 0))
    product = dot(jnp.concatenate([high, low, high], 1), table_ref[2 * HALF :])
    result = []
    for k in range(len(patches)):
        a = product[2 * HALF * k : 2 * HALF * k + HALF]
        b = product[2 * HALF * k + HALF : 2 * HALF * (k + 1)]
        result.append((a[:, :EXTENT] - b[:, EXTENT:], -(a[:, EXTENT:] + b[:, :EXTENT])))
    return result


def energy(ref):
    rows = []
    for n in range(ref.shape[0]):
        value = ref[n].astype(F32)
        rows.append(jnp.sum(value * value, axis=0, keepdims=True))
    total = jnp.sum(jnp.concatenate(rows, 0), axis=1, keepdims=True)
    return total * (1.0 / (EXTENT * EXTENT))


def own_kernel(now_ref, table_ref, spectrum_ref, energy_ref):
    for pair in range(0, now_ref.shape[0], 2):
        for k, (real, imag) in enumerate(spectra([now_ref[pair], now_ref[pair + 1]], table_ref)):
            spectrum_ref[pair + k, :, :EXTENT] = real
            spectrum_ref[pair + k, :, EXTENT:] = imag
    energy_ref[...] = jnp.broadcast_to(energy(now_ref), energy_ref.shape)


def write_names(owner, route_ref, name_ref):
    slots = name_ref.shape[0]
    tile_count = route_ref.shape[1] // slots
    height = EXTENT // WIDE // tile_count
    lane = lax.broadcasted_iota(jnp.int32, (slots, tile_count * slots), 1)
    slot = lax.broadcasted_iota(jnp.int32, (slots, tile_count * slots), 0)
    names = jnp.broadcast_to(route_ref[...], lane.shape).astype(F32)
    place = lax.broadcasted_iota(jnp.int32, (slots, EXTENT), 1)
    here = place // (tile_count * height) == owner % WIDE
    row = jnp.zeros((slots, EXTENT), F32)
    for t in range(tile_count):
        own = jnp.sum(jnp.where(lane == slot + t * slots, names, 0.0), axis=1, keepdims=True)
        row = jnp.where(here & (place // height % tile_count == t), own, row)
    for p in range(slots):
        name_ref[p] = jnp.broadcast_to(row[p : p + 1], (8, EXTENT)).astype(BF)


def flow_kernel(place_ref, peak_ref, route_ref, low_ref, spectrum_ref, energy_ref, table_ref, inverse_ref, out_ref, name_ref):
    count = low_ref.shape[0]
    write_names(place_ref[0], route_ref, name_ref)
    crosses = []
    for pair in range(0, count, 2):
        block = []
        for k, (lr, li) in enumerate(spectra([low_ref[pair], low_ref[pair + 1]], table_ref)):
            nr = spectrum_ref[pair + k, :, :EXTENT]
            ni = spectrum_ref[pair + k, :, EXTENT:]
            block.append(jnp.concatenate([nr * lr + ni * li, ni * lr - nr * li], 1))
        crosses.append(jnp.concatenate(block, 0))
    third = 6 * EXTENT
    fourth = jnp.concatenate(
        [
            inverse_ref[third : third + 2 * REACH],
            inverse_ref[third + 2 * REACH :, : 6 * HALF - 2 * EXTENT],
        ],
        1,
    )
    correlations = []
    for cross in crosses:
        high, low = split(cross)
        outer = dot(jnp.concatenate([high, low, high], 1), inverse_ref[:third])
        columns = []
        for k in range(2):
            block = outer[HALF * k : HALF * (k + 1)]
            columns.append(jnp.concatenate([block[:, :EXTENT], block[:, EXTENT:]], 0))
        high, low = split(jnp.concatenate(columns, 1))
        result = dot(fourth, jnp.concatenate([high, low, high], 0))
        correlations += [result[:, :EXTENT], result[:, EXTENT:]]

    scale = (SCORE_GAIN / EXTENT) / jnp.sqrt(energy_ref[:, :1] * energy(low_ref) + EPSILON)
    shape = (2 * REACH, EXTENT)
    row = lax.broadcasted_iota(jnp.int32, shape, 0) - REACH
    column = lax.broadcasted_iota(jnp.int32, shape, 1)
    scores, relatives, tops = [], [], []
    for n in range(count):
        rel_y = row - peak_ref[0, n]
        rel_x = ((column - peak_ref[1, n] + EXTENT // 2) & (EXTENT - 1)) - EXTENT // 2
        quarter = EXTENT // 4
        inside = (rel_y >= -quarter) & (rel_y < quarter) & (rel_x >= -quarter) & (rel_x < quarter)
        score = jnp.where(inside, correlations[n] * scale[n : n + 1], -1e30)
        scores.append(score)
        relatives.append((rel_y.astype(F32), rel_x[:1].astype(F32)))
        tops.append(jnp.max(score, axis=0, keepdims=True))
    top = jnp.max(jnp.concatenate(tops, 0), axis=1, keepdims=True)
    sums, sums_y, sums_x = [], [], []
    for n in range(count):
        weight = jnp.exp(scores[n] - top[n : n + 1])
        rel_y, rel_x = relatives[n]
        along = jnp.sum(weight, axis=0, keepdims=True)
        sums.append(along)
        sums_y.append(jnp.sum(weight * rel_y, axis=0, keepdims=True))
        sums_x.append(along * rel_x)
    total, total_y, total_x = (
        jnp.sum(jnp.concatenate(s, 0), axis=1, keepdims=True) for s in (sums, sums_y, sums_x)
    )
    node = lax.broadcasted_iota(jnp.int32, (count, EXTENT), 0)
    lane = lax.broadcasted_iota(jnp.int32, (count, EXTENT), 1)
    peak_y = jnp.zeros((count, EXTENT), jnp.int32)
    peak_x = jnp.zeros((count, EXTENT), jnp.int32)
    for n in range(count):
        peak_y = jnp.where(node == n, peak_ref[0, n], peak_y)
        peak_x = jnp.where(node == n, peak_ref[1, n], peak_x)
    flow_y = peak_y.astype(F32) + total_y / total
    flow_x = peak_x.astype(F32) + total_x / total
    flow = jnp.where(lane == node, flow_y, jnp.where(lane == node + count, flow_x, 0.0))
    flow = jnp.sum(flow, axis=0, keepdims=True)
    out_ref[...] = jnp.broadcast_to(flow[None], out_ref.shape)


def fill_band(target_ref, residual, offset, sub_sign):
    block = EXTENT
    lane = lax.broadcasted_iota(jnp.int32, (1, block), 1)
    tap = (lane - BAND).astype(F32) - residual
    raw = jnp.where(lane <= 2 * BAND, 1.0 / (1.0 + tap * tap), 0.0)
    norm = jnp.sum(raw, axis=1, keepdims=True)
    a = lax.broadcasted_iota(jnp.int32, (block, block), 0)
    b = lax.broadcasted_iota(jnp.int32, (block, block), 1)
    d = sub_sign * (a - b) - offset
    k = ((d + block // 2) & (block - 1)) - block // 2
    away = k.astype(F32) - residual
    value = (1.0 / (1.0 + away * away)) / norm
    blocks = {}
    for step in (-1, 0, 1):
        near = jnp.abs(d + sub_sign * step * block) <= BAND
        blocks[step] = jnp.where(near, value, 0.0).astype(BF)
    zero = jnp.zeros((block, block), BF)
    count = target_ref.shape[0] // block
    for i in range(count):
        for j in range(count):
            target_ref[i * block : (i + 1) * block, j * block : (j + 1) * block] = blocks.get(
                i - j, zero
            )


def render_kernel(place_ref, map_ref, band_ref, flow_ref, name_ref, tile_ref, position_ref, send_ref, *scratch):
    sections = flow_ref.shape[0]
    tile_count, edge, _ = tile_ref.shape
    slots = send_ref.shape[0]
    section = place_ref[1]
    second_core = place_ref[2] == 1

    def slot_of(p):
        return jnp.where(second_core, p % WIDE * (slots // WIDE) + p // WIDE, p)

    position = jnp.zeros(flow_ref.shape[1:], F32)
    for s in range(sections):
        position = position + map_ref[section, s] * flow_ref[s]
    *scratch, moved_ref, moved = scratch
    nodes = position_ref.shape[1]
    for c in range(2):
        moved_ref[c : c + 1, :] = position[:, c * nodes : (c + 1) * nodes]
    leaving = pltpu.make_async_copy(moved_ref, position_ref, moved)
    leaving.start()
    per_tile = nodes // tile_count
    lanes = lax.broadcasted_iota(jnp.int32, position.shape, 1)
    height = edge // slots
    columns = edge // EXTENT
    chunk = EXTENT
    for t in range(tile_count):
        col_ref, row_ref, pass_ref = scratch[3 * t : 3 * t + 3]
        offset_y, offset_x = band_ref[t, 0], band_ref[t, 1]
        shift_y, shift_x = (
            jnp.sum(jnp.where(lanes // per_tile == c * tile_count + t, position, 0.0), axis=1, keepdims=True)
            * (MIP_SCALE / per_tile)
            for c in range(2)
        )
        fill_band(col_ref, shift_x - offset_x.astype(F32), offset_x, 1)
        fill_band(row_ref, shift_y - offset_y.astype(F32), offset_y, -1)
        for c in range(edge // chunk):
            rows = slice(c * chunk, (c + 1) * chunk)
            pass_ref[rows, :] = dot(tile_ref[t, rows, :], col_ref[...]).astype(BF)
        for c in range(edge // chunk):
            rows = slice(c * chunk, (c + 1) * chunk)
            first, last = c * chunk // height, (c + 1) * chunk // height
            near = range(max(c - 1, 0), min(c + 2, edge // chunk))
            from_row = near[0] * chunk // (edge // 2) * (edge // 2)
            to_row = edge // 2 if near[-1] * chunk < edge // 2 else edge
            done = dot(row_ref[rows, from_row:to_row], pass_ref[from_row:to_row, :]).astype(BF)
            done = done.reshape(last - first, height, edge)
            for p in range(first, last):
                for j in range(columns):
                    at = (t * columns + j) * height
                    send_ref[slot_of(p), at : at + height, :] = done[
                        p - first, :, j * EXTENT : (j + 1) * EXTENT
                    ]
    tail = tile_count * columns * height
    for p in range(slots):
        send_ref[slot_of(p), tail:, :] = name_ref[p]
    leaving.wait()


def gather_kernel(piece_ref, out_ref, data_ref):
    owners, rows, _ = piece_ref.shape
    _, out_rows, edge = out_ref.shape
    height = edge // owners
    columns = edge // EXTENT
    tile_count = (rows - 8) // (columns * height)
    tail = rows - 8
    share = EXTENT // (tile_count * height)
    lane_row = lax.broadcasted_iota(jnp.int32, (EXTENT, EXTENT), 1) % height
    sub = lax.broadcasted_iota(jnp.int32, (EXTENT, EXTENT), 0)
    same = lane_row == sub % height
    for d in range(owners):
        for t in range(tile_count):
            at = (d * tile_count + t) * height
            for j in range(columns):
                source = (t * columns + j) * height
                data_ref[at : at + height, j * EXTENT : (j + 1) * EXTENT] = piece_ref[
                    d, source : source + height, :
                ]
    names = [
        sum(piece_ref[d, tail : tail + 8, :].astype(F32) for d in range(start, start + share))[0:1]
        for start in range(0, owners, share)
    ]
    for c in range(owners * out_rows // EXTENT):
        group = (sub // height + c * (EXTENT // height)).astype(F32)
        hits = [jnp.where(same & (name == group), 1.0, 0.0) for name in names]
        count = jnp.sum(sum(hits), axis=1, keepdims=True)
        total = dot(jnp.concatenate([hit.astype(BF) for hit in hits], 1), data_ref[...])
        total = total * (1.0 / jnp.maximum(count, 1.0))
        first, last = c * EXTENT // out_rows, (c + 1) * EXTENT // out_rows
        out_ref[first:last] = total.astype(BF).reshape(last - first, out_rows, edge)


def place_kernel(cell_ref, out_ref, arrived):
    height = out_ref.shape[2]
    copies = [
        pltpu.make_async_copy(
            cell_ref.at[:, g * height : (g + 1) * height, :], out_ref.at[g], arrived.at[g]
        )
        for g in range(out_ref.shape[0])
    ]
    for copy in copies:
        copy.start()
    for copy in copies:
        copy.wait()


def in_vmem():
    return pl.BlockSpec(memory_space=pltpu.VMEM)


def in_smem():
    return pl.BlockSpec(memory_space=pltpu.SMEM)


def params():
    return pltpu.CompilerParams(vmem_limit_bytes=40 * 1024 * 1024)


def exchange(value, axis, groups=None):
    return lax.all_to_all(
        value, axis, split_axis=0, concat_axis=0, tiled=True, axis_index_groups=groups
    )


def exchange_x_then_z(value):
    owners, rows, lanes = value.shape
    high = owners // WIDE
    along_x = [[z * WIDE + x for x in range(WIDE)] for z in range(high)]
    along_z = [[z * WIDE + x for z in range(high)] for x in range(WIDE)]
    value = exchange(value.reshape(WIDE, high * rows, lanes), "xy", along_x)
    value = value.reshape(WIDE, high, rows, lanes).transpose(1, 0, 2, 3)
    value = exchange(value.reshape(high, WIDE * rows, lanes), "xy", along_z)
    return value.reshape(owners, rows, lanes)


def body(patches, peak_offsets, tiles, band_offsets, routes):
    sections = lax.axis_size("gz")
    owners = lax.axis_size("xy")
    tile_count, edge = tiles.shape[1], tiles.shape[-1]
    height = edge // PIECES
    share = 2
    count = patches.shape[1]

    section = lax.axis_index("gz")
    below = lax.ppermute(patches, "gz", [(i, i + 1) for i in range(sections - 1)])
    early_table, late_table = (jnp.asarray(t) for t in dft_constants())
    second_core = section % 2 == 1
    place = jnp.stack([lax.axis_index("xy"), section, second_core.astype(jnp.int32)])
    spectrum, power = pl.pallas_call(
        own_kernel,
        out_shape=(
            jax.ShapeDtypeStruct((count, HALF, 2 * EXTENT), F32),
            jax.ShapeDtypeStruct((count, EXTENT), F32),
        ),
        in_specs=[in_vmem()] * 2,
        out_specs=(in_vmem(),) * 2,
        compiler_params=params(),
        cost_estimate=pl.CostEstimate(flops=10**9, bytes_accessed=2**20, transcendentals=0),
        name="own",
    )(patches[0], early_table)
    flow, names = pl.pallas_call(
        flow_kernel,
        out_shape=(
            jax.ShapeDtypeStruct((sections, 1, EXTENT), F32),
            jax.ShapeDtypeStruct((PIECES, 8, EXTENT), BF),
        ),
        in_specs=[in_smem()] * 2 + [in_vmem()] * 6,
        out_specs=(in_vmem(),) * 2,
        compiler_params=params(),
        name="flow",
    )(place, peak_offsets[0].T, routes[0].T, below[0], spectrum, power, early_table, late_table)
    flow = exchange(flow, "gz")

    position, pieces = pl.pallas_call(
        render_kernel,
        out_shape=(
            jax.ShapeDtypeStruct((2, count), F32),
            jax.ShapeDtypeStruct((PIECES, tile_count * height * edge // EXTENT + 8, EXTENT), BF),
        ),
        in_specs=[in_smem()] * 3 + [in_vmem()] * 3,
        out_specs=(pl.BlockSpec(memory_space=pl.ANY), in_vmem()),
        scratch_shapes=[pltpu.VMEM((edge, edge), BF)] * (3 * tile_count)
        + [pltpu.VMEM((2, count), F32), pltpu.SemaphoreType.DMA],
        compiler_params=params(),
        name="render",
    )(place, jnp.asarray(relaxation_map(sections)), band_offsets[0], flow, names, tiles[0])
    pieces = lax.cond(
        second_core,
        exchange_x_then_z,
        lambda value: exchange(value, "xy"),
        pieces,
    )

    cells = pl.pallas_call(
        gather_kernel,
        out_shape=jax.ShapeDtypeStruct((owners, share * height, edge), BF),
        in_specs=[in_vmem()],
        out_specs=in_vmem(),
        scratch_shapes=[pltpu.VMEM((owners * tile_count * height, edge), BF)],
        compiler_params=params(),
        name="gather",
    )(pieces)
    cells = exchange(cells, "xy")
    rendered = pl.pallas_call(
        place_kernel,
        out_shape=jax.ShapeDtypeStruct((share, PIECES, height, edge), BF),
        in_specs=[in_vmem()],
        out_specs=pl.BlockSpec(memory_space=pl.ANY),
        scratch_shapes=[pltpu.SemaphoreType.DMA((share,))],
        compiler_params=params(),
        name="place",
    )(cells)
    rendered = rendered.reshape(1, share, edge, edge)
    return position[None], rendered


def solution(mesh):
    placed = (
        P("gz", "xy", None, None),
        P("gz", "xy", None),
        P("gz", "xy", None, None),
        P("gz", "xy", None),
        P("gz", "xy", None),
    )
    return jax.shard_map(
        body,
        mesh=mesh,
        in_specs=placed,
        out_specs=(P("gz", None, "xy"), P("gz", "xy", None, None)),
        check_vma=False,
    )
```

```python
import jax
import jax.numpy as jnp
import numpy as np
from jax import lax
from jax.experimental import pallas as pl
from jax.experimental.pallas import tpu as pltpu
from jax.sharding import PartitionSpec as P

PIECES = 32
WIDE = 4
BAND = 6
RELAX = 3
EPSILON = 1e-06
STEP_SIZE = 0.25
ANCHOR_WEIGHT = 0.5
MIP_SCALE = 0.0625
SCORE_GAIN = 6.0

EXTENT = 128
HALF = 72
REACH = 40
BF = jnp.bfloat16
F32 = jnp.float32


def high_low(table):
    high = table.astype(jnp.bfloat16)
    low = (table - high.astype(np.float64)).astype(jnp.bfloat16)
    return high, low


def dft_constants():
    line = np.arange(EXTENT)
    phase = 2.0 * np.pi * ((line[:, None] * line[None, :]) % EXTENT) / EXTENT
    cos, sin = np.cos(phase), np.sin(phase)
    first = np.concatenate([cos[:HALF], sin[:HALF]], 0)
    first = np.concatenate(high_low(first), 1)
    second_high, second_low = high_low(np.concatenate([cos, sin], 1))
    second = np.concatenate([second_high, second_high, second_low], 0)
    third_high, third_low = high_low(np.block([[cos, sin], [-sin, cos]]))
    third = np.concatenate([third_high, third_high, third_low], 0)
    weight = np.where(line[:HALF] <= EXTENT // 2, 2.0, 0.0)
    weight[0] = weight[EXTENT // 2] = 1.0
    rows = (np.arange(-REACH, REACH) % EXTENT)[:, None]
    angle = 2.0 * np.pi * ((rows * line[None, :HALF]) % EXTENT) / EXTENT
    fourth = np.concatenate([weight * np.cos(angle), -weight * np.sin(angle)], 1)
    fourth_high, fourth_low = high_low(fourth / float(EXTENT * EXTENT))
    fourth = np.concatenate([fourth_high, fourth_high, fourth_low], 1)
    fourth = np.pad(fourth, ((0, 0), (0, 4 * EXTENT - fourth.shape[1])))
    early = np.concatenate([first, second], 0)
    late = np.concatenate([third, fourth[:, : 2 * EXTENT], fourth[:, 2 * EXTENT :]], 0)
    return early, late


def relaxation_map(sections):
    flow = np.eye(sections)
    positions = np.tril(np.ones((sections, sections)))
    for _ in range(RELAX):
        lower = np.zeros_like(positions)
        upper = np.zeros_like(positions)
        lower[1:] = positions[:-1] + flow[1:] - positions[1:]
        upper[:-1] = positions[1:] - flow[1:] - positions[:-1]
        positions = positions + STEP_SIZE * (lower + upper - ANCHOR_WEIGHT * positions)
    return positions.astype(np.float32)


def split(value):
    high = value.astype(BF)
    return high, (value - high.astype(F32)).astype(BF)


def dot(a, b):
    return jnp.dot(a, b, preferred_element_type=F32)


def spectra(patches, table_ref):
    lines = []
    for pair in range(0, len(patches), 2):
        both = jnp.concatenate(patches[pair : pair + 2], 1)
        line = dot(table_ref[: 2 * HALF], jnp.concatenate([both, both], 0))
        lines += [line[:, :EXTENT], line[:, EXTENT:]]
    high, low = split(jnp.concatenate(lines, 0))
    product = dot(jnp.concatenate([high, low, high], 1), table_ref[2 * HALF :])
    result = []
    for k in range(len(patches)):
        a = product[2 * HALF * k : 2 * HALF * k + HALF]
        b = product[2 * HALF * k + HALF : 2 * HALF * (k + 1)]
        result.append((a[:, :EXTENT] - b[:, EXTENT:], -(a[:, EXTENT:] + b[:, :EXTENT])))
    return result


def energy(ref):
    rows = []
    for n in range(ref.shape[0]):
        value = ref[n].astype(F32)
        rows.append(jnp.sum(value * value, axis=0, keepdims=True))
    total = jnp.sum(jnp.concatenate(rows, 0), axis=1, keepdims=True)
    return total * (1.0 / (EXTENT * EXTENT))


def own_kernel(now_ref, table_ref, spectrum_ref, energy_ref):
    for pair in range(0, now_ref.shape[0], 2):
        for k, (real, imag) in enumerate(spectra([now_ref[pair], now_ref[pair + 1]], table_ref)):
            spectrum_ref[pair + k, :, :EXTENT] = real
            spectrum_ref[pair + k, :, EXTENT:] = imag
    energy_ref[...] = jnp.broadcast_to(energy(now_ref), energy_ref.shape)


def write_names(owner, route_ref, name_ref):
    slots = name_ref.shape[0]
    tile_count = route_ref.shape[1] // slots
    height = EXTENT // WIDE // tile_count
    lane = lax.broadcasted_iota(jnp.int32, (slots, tile_count * slots), 1)
    slot = lax.broadcasted_iota(jnp.int32, (slots, tile_count * slots), 0)
    names = jnp.broadcast_to(route_ref[...], lane.shape).astype(F32)
    place = lax.broadcasted_iota(jnp.int32, (slots, EXTENT), 1)
    here = place // (tile_count * height) == owner % WIDE
    row = jnp.zeros((slots, EXTENT), F32)
    for t in range(tile_count):
        own = jnp.sum(jnp.where(lane == slot + t * slots, names, 0.0), axis=1, keepdims=True)
        row = jnp.where(here & (place // height % tile_count == t), own, row)
    for p in range(slots):
        name_ref[p] = row[p : p + 1]


def flow_kernel(place_ref, peak_ref, route_ref, low_ref, spectrum_ref, energy_ref, table_ref, inverse_ref, out_ref, name_ref):
    count = low_ref.shape[0]
    write_names(place_ref[0], route_ref, name_ref)
    crosses = []
    for n, (lr, li) in enumerate(spectra([low_ref[n] for n in range(count)], table_ref)):
        nr = spectrum_ref[n, :, :EXTENT]
        ni = spectrum_ref[n, :, EXTENT:]
        crosses.append(jnp.concatenate([nr * lr + ni * li, ni * lr - nr * li], 1))
    third = 6 * EXTENT
    fourth = jnp.concatenate(
        [
            inverse_ref[third : third + 2 * REACH],
            inverse_ref[third + 2 * REACH :, : 6 * HALF - 2 * EXTENT],
        ],
        1,
    )
    high, low = split(jnp.concatenate(crosses, 0))
    outer = dot(jnp.concatenate([high, low, high], 1), inverse_ref[:third])
    correlations = []
    for pair in range(0, count, 2):
        columns = []
        for n in (pair, pair + 1):
            block = outer[HALF * n : HALF * (n + 1)]
            columns.append(jnp.concatenate([block[:, :EXTENT], block[:, EXTENT:]], 0))
        high, low = split(jnp.concatenate(columns, 1))
        result = dot(fourth, jnp.concatenate([high, low, high], 0))
        correlations += [result[:, :EXTENT], result[:, EXTENT:]]

    scale = (SCORE_GAIN / EXTENT) / jnp.sqrt(energy_ref[:, :1] * energy(low_ref) + EPSILON)
    shape = (2 * REACH, EXTENT)
    row = lax.broadcasted_iota(jnp.int32, shape, 0) - REACH
    column = lax.broadcasted_iota(jnp.int32, shape, 1)
    scores, relatives, tops = [], [], []
    for n in range(count):
        rel_y = row - peak_ref[0, n]
        rel_x = ((column - peak_ref[1, n] + EXTENT // 2) & (EXTENT - 1)) - EXTENT // 2
        quarter = EXTENT // 4
        inside = (rel_y >= -quarter) & (rel_y < quarter) & (rel_x >= -quarter) & (rel_x < quarter)
        score = jnp.where(inside, correlations[n] * scale[n : n + 1], -1e30)
        scores.append(score)
        relatives.append((rel_y.astype(F32), rel_x[:1].astype(F32)))
        tops.append(jnp.max(score, axis=0, keepdims=True))
    top = jnp.max(jnp.concatenate(tops, 0), axis=1, keepdims=True)
    sums, sums_y, sums_x = [], [], []
    for n in range(count):
        weight = jnp.exp(scores[n] - top[n : n + 1])
        rel_y, rel_x = relatives[n]
        along = jnp.sum(weight, axis=0, keepdims=True)
        sums.append(along)
        sums_y.append(jnp.sum(weight * rel_y, axis=0, keepdims=True))
        sums_x.append(along * rel_x)
    total, total_y, total_x = (
        jnp.sum(jnp.concatenate(s, 0), axis=1, keepdims=True) for s in (sums, sums_y, sums_x)
    )
    node = lax.broadcasted_iota(jnp.int32, (count, EXTENT), 0)
    lane = lax.broadcasted_iota(jnp.int32, (count, EXTENT), 1)
    peak_y = jnp.zeros((count, EXTENT), jnp.int32)
    peak_x = jnp.zeros((count, EXTENT), jnp.int32)
    for n in range(count):
        peak_y = jnp.where(node == n, peak_ref[0, n], peak_y)
        peak_x = jnp.where(node == n, peak_ref[1, n], peak_x)
    flow_y = peak_y.astype(F32) + total_y / total
    flow_x = peak_x.astype(F32) + total_x / total
    flow = jnp.where(lane == node, flow_y, jnp.where(lane == node + count, flow_x, 0.0))
    flow = jnp.sum(flow, axis=0, keepdims=True)
    out_ref[...] = jnp.broadcast_to(flow[None], out_ref.shape)


def fill_band(target_ref, residual, offset, sub_sign):
    block = EXTENT
    lane = lax.broadcasted_iota(jnp.int32, (1, block), 1)
    tap = (lane - BAND).astype(F32) - residual
    raw = jnp.where(lane <= 2 * BAND, 1.0 / (1.0 + tap * tap), 0.0)
    norm = jnp.sum(raw, axis=1, keepdims=True)
    a = lax.broadcasted_iota(jnp.int32, (block, block), 0)
    b = lax.broadcasted_iota(jnp.int32, (block, block), 1)
    d = sub_sign * (a - b) - offset
    k = ((d + block // 2) & (block - 1)) - block // 2
    away = k.astype(F32) - residual
    value = (1.0 / (1.0 + away * away)) / norm
    blocks = {}
    for step in (-1, 0, 1):
        near = jnp.abs(d + sub_sign * step * block) <= BAND
        blocks[step] = jnp.where(near, value, 0.0).astype(BF)
    zero = jnp.zeros((block, block), BF)
    count = target_ref.shape[0] // block
    for i in range(count):
        for j in range(count):
            target_ref[i * block : (i + 1) * block, j * block : (j + 1) * block] = blocks.get(
                i - j, zero
            )


def render_kernel(place_ref, map_ref, band_ref, flow_ref, name_ref, tile_ref, position_ref, send_ref, *scratch):
    sections = flow_ref.shape[0]
    tile_count, edge, _ = tile_ref.shape
    slots = send_ref.shape[0]
    section = place_ref[1]
    position = jnp.zeros(flow_ref.shape[1:], F32)
    for s in range(sections):
        position = position + map_ref[section, s] * flow_ref[s]
    *scratch, moved_ref, moved = scratch
    nodes = position_ref.shape[1]
    for c in range(2):
        moved_ref[c : c + 1, :] = position[:, c * nodes : (c + 1) * nodes]
    leaving = pltpu.make_async_copy(moved_ref, position_ref, moved)
    leaving.start()
    per_tile = nodes // tile_count
    lanes = lax.broadcasted_iota(jnp.int32, position.shape, 1)
    height = edge // slots
    columns = edge // EXTENT
    chunk = EXTENT
    for t in range(tile_count):
        col_ref, row_ref, pass_ref = scratch[3 * t : 3 * t + 3]
        offset_y, offset_x = band_ref[t, 0], band_ref[t, 1]
        shift_y, shift_x = (
            jnp.sum(jnp.where(lanes // per_tile == c * tile_count + t, position, 0.0), axis=1, keepdims=True)
            * (MIP_SCALE / per_tile)
            for c in range(2)
        )
        fill_band(col_ref, shift_x - offset_x.astype(F32), offset_x, 1)
        fill_band(row_ref, shift_y - offset_y.astype(F32), offset_y, -1)
        for c in range(edge // chunk):
            rows = slice(c * chunk, (c + 1) * chunk)
            pass_ref[rows, :] = dot(tile_ref[t, rows, :], col_ref[...]).astype(BF)
        for c in range(edge // chunk):
            rows = slice(c * chunk, (c + 1) * chunk)
            first, last = c * chunk // height, (c + 1) * chunk // height
            near = range(max(c - 1, 0), min(c + 2, edge // chunk))
            from_row = near[0] * chunk // (edge // 2) * (edge // 2)
            to_row = edge // 2 if near[-1] * chunk < edge // 2 else edge
            done = dot(row_ref[rows, from_row:to_row], pass_ref[from_row:to_row, :]).astype(BF)
            done = done.reshape(last - first, height, edge)
            for j in range(columns):
                at = (t * columns + j) * height
                send_ref[first:last, at : at + height, :] = done[:, :, j * EXTENT : (j + 1) * EXTENT]
    tail = tile_count * columns * height
    if send_ref.shape[1] > tail:
        for p in range(slots):
            send_ref[p, tail:, :] = jnp.broadcast_to(name_ref[p], (8, EXTENT)).astype(BF)
    leaving.wait()


def gather_kernel(piece_ref, *refs):
    *name_refs, out_ref, data_ref = refs
    owners = piece_ref.shape[0]
    _, out_rows, edge = out_ref.shape
    height = edge // owners
    columns = edge // EXTENT
    tile_count = EXTENT // WIDE // height
    tail = tile_count * columns * height
    name_ref = name_refs[0] if name_refs else piece_ref.at[:, tail:]
    lane_row = lax.broadcasted_iota(jnp.int32, (EXTENT, EXTENT), 1) % height
    sub = lax.broadcasted_iota(jnp.int32, (EXTENT, EXTENT), 0)
    same = lane_row == sub % height
    for d in range(owners):
        for t in range(tile_count):
            at = (d * tile_count + t) * height
            for j in range(columns):
                source = (t * columns + j) * height
                data_ref[at : at + height, j * EXTENT : (j + 1) * EXTENT] = piece_ref[
                    d, source : source + height, :
                ]
    names = [
        sum(name_ref[d].astype(F32) for d in range(start, start + WIDE))[0:1]
        for start in range(0, owners, WIDE)
    ]
    for c in range(owners * out_rows // EXTENT):
        group = (sub // height + c * (EXTENT // height)).astype(F32)
        hits = [jnp.where(same & (name == group), 1.0, 0.0) for name in names]
        count = jnp.sum(sum(hits), axis=1, keepdims=True)
        total = dot(jnp.concatenate([hit.astype(BF) for hit in hits], 1), data_ref[...])
        total = total * (1.0 / jnp.maximum(count, 1.0))
        first, last = c * EXTENT // out_rows, (c + 1) * EXTENT // out_rows
        out_ref[first:last] = total.astype(BF).reshape(last - first, out_rows, edge)


def place_kernel(cell_ref, out_ref, arrived):
    height = out_ref.shape[2]
    copies = [
        pltpu.make_async_copy(
            cell_ref.at[:, g * height : (g + 1) * height, :], out_ref.at[g], arrived.at[g]
        )
        for g in range(out_ref.shape[0])
    ]
    for copy in copies:
        copy.start()
    for copy in copies:
        copy.wait()


def in_vmem():
    return pl.BlockSpec(memory_space=pltpu.VMEM)


def in_smem():
    return pl.BlockSpec(memory_space=pltpu.SMEM)


def params():
    return pltpu.CompilerParams(vmem_limit_bytes=40 * 1024 * 1024)


def exchange(value, axis):
    return lax.all_to_all(value, axis, split_axis=0, concat_axis=0, tiled=True)


def body(patches, peak_offsets, tiles, band_offsets, routes):
    sections = lax.axis_size("gz")
    owners = lax.axis_size("xy")
    tile_count, edge = tiles.shape[1], tiles.shape[-1]
    height = edge // PIECES
    share = 2
    count = patches.shape[1]

    section = lax.axis_index("gz")
    below = lax.ppermute(patches, "gz", [(i, i + 1) for i in range(sections - 1)])
    early_table, late_table = (jnp.asarray(t) for t in dft_constants())
    second_core = section % 2 == 1
    place = jnp.stack([lax.axis_index("xy"), section, second_core.astype(jnp.int32)])
    spectrum, power = pl.pallas_call(
        own_kernel,
        out_shape=(
            jax.ShapeDtypeStruct((count, HALF, 2 * EXTENT), F32),
            jax.ShapeDtypeStruct((count, EXTENT), F32),
        ),
        in_specs=[in_vmem()] * 2,
        out_specs=(in_vmem(),) * 2,
        compiler_params=params(),
        cost_estimate=pl.CostEstimate(flops=10**9, bytes_accessed=2**20, transcendentals=0),
        name="own",
    )(patches[0], early_table)
    flow, names = pl.pallas_call(
        flow_kernel,
        out_shape=(
            jax.ShapeDtypeStruct((sections, 1, EXTENT), F32),
            jax.ShapeDtypeStruct((PIECES, 1, EXTENT), F32),
        ),
        in_specs=[in_smem()] * 2 + [in_vmem()] * 6,
        out_specs=(in_vmem(),) * 2,
        compiler_params=params(),
        name="flow",
    )(place, peak_offsets[0].T, routes[0].T, below[0], spectrum, power, early_table, late_table)
    flow = exchange(flow, "gz")

    linear = jnp.asarray(relaxation_map(sections))
    piece_rows = tile_count * height * edge // EXTENT

    def render(flow, image, names, rows):
        return pl.pallas_call(
            render_kernel,
            out_shape=(
                jax.ShapeDtypeStruct((2, count), F32),
                jax.ShapeDtypeStruct((PIECES, rows, EXTENT), BF),
            ),
            in_specs=[in_smem()] * 3 + [in_vmem()] * 3,
            out_specs=(pl.BlockSpec(memory_space=pl.ANY), in_vmem()),
            scratch_shapes=[pltpu.VMEM((edge, edge), BF)] * (3 * tile_count)
            + [pltpu.VMEM((2, count), F32), pltpu.SemaphoreType.DMA],
            compiler_params=params(),
            name="render",
        )(place, linear, band_offsets[0], flow, names, image)

    def gather(*received):
        return pl.pallas_call(
            gather_kernel,
            out_shape=jax.ShapeDtypeStruct((owners, share * height, edge), BF),
            in_specs=[in_vmem()] * len(received),
            out_specs=in_vmem(),
            scratch_shapes=[pltpu.VMEM((owners * tile_count * height, edge), BF)],
            compiler_params=params(),
            name="gather",
        )(*received)

    def together(flow, image, names):
        position, whole = render(flow, image, names, piece_rows + 8)
        return position, gather(exchange(whole, "xy"))

    def names_ahead(flow, image, names):
        position, pieces = render(flow, image, names, piece_rows)
        names, pieces = lax.optimization_barrier((names, pieces))
        names, pieces = lax.optimization_barrier((exchange(names, "xy"), pieces))
        return position, gather(exchange(pieces, "xy"), names)

    position, cells = lax.cond(second_core, names_ahead, together, flow, tiles[0], names)
    cells = exchange(cells, "xy")
    rendered = pl.pallas_call(
        place_kernel,
        out_shape=jax.ShapeDtypeStruct((share, PIECES, height, edge), BF),
        in_specs=[in_vmem()],
        out_specs=pl.BlockSpec(memory_space=pl.ANY),
        scratch_shapes=[pltpu.SemaphoreType.DMA((share,))],
        compiler_params=params(),
        name="place",
    )(cells)
    rendered = rendered.reshape(1, share, edge, edge)
    return position[None], rendered


def solution(mesh):
    placed = (
        P("gz", "xy", None, None),
        P("gz", "xy", None),
        P("gz", "xy", None, None),
        P("gz", "xy", None),
        P("gz", "xy", None),
    )
    return jax.shard_map(
        body,
        mesh=mesh,
        in_specs=placed,
        out_specs=(P("gz", None, "xy"), P("gz", "xy", None, None)),
        check_vma=False,
    )
```

```python
import jax
import jax.numpy as jnp
import numpy as np
from jax import lax
from jax.experimental import pallas as pl
from jax.experimental.pallas import tpu as pltpu
from jax.sharding import PartitionSpec as P

PIECES = 32
WIDE = 4
SHARE = 8
BAND = 6
RELAX = 3
EPSILON = 1e-06
STEP_SIZE = 0.25
ANCHOR_WEIGHT = 0.5
MIP_SCALE = 0.0625
SCORE_GAIN = 6.0

EXTENT = 128
HALF = 72
REACH = 40
BF = jnp.bfloat16
F32 = jnp.float32


def high_low(table):
    high = table.astype(jnp.bfloat16)
    low = (table - high.astype(np.float64)).astype(jnp.bfloat16)
    return high, low


def dft_constants():
    line = np.arange(EXTENT)
    phase = 2.0 * np.pi * ((line[:, None] * line[None, :]) % EXTENT) / EXTENT
    cos, sin = np.cos(phase), np.sin(phase)
    first = np.concatenate([cos[:HALF], sin[:HALF]], 0)
    first = np.concatenate(high_low(first), 1)
    second_high, second_low = high_low(np.concatenate([cos, sin], 1))
    second = np.concatenate([second_high, second_high, second_low], 0)
    third_high, third_low = high_low(np.block([[cos, sin], [-sin, cos]]))
    third = np.concatenate([third_high, third_high, third_low], 0)
    weight = np.where(line[:HALF] <= EXTENT // 2, 2.0, 0.0)
    weight[0] = weight[EXTENT // 2] = 1.0
    rows = (np.arange(-REACH, REACH) % EXTENT)[:, None]
    angle = 2.0 * np.pi * ((rows * line[None, :HALF]) % EXTENT) / EXTENT
    fourth = np.concatenate([weight * np.cos(angle), -weight * np.sin(angle)], 1)
    fourth_high, fourth_low = high_low(fourth / float(EXTENT * EXTENT))
    fourth = np.concatenate([fourth_high, fourth_high, fourth_low], 1)
    fourth = np.pad(fourth, ((0, 0), (0, 4 * EXTENT - fourth.shape[1])))
    early = np.concatenate([first, second], 0)
    late = np.concatenate([third, fourth[:, : 2 * EXTENT], fourth[:, 2 * EXTENT :]], 0)
    return early, late


def relaxation_map(sections):
    flow = np.eye(sections)
    positions = np.tril(np.ones((sections, sections)))
    for _ in range(RELAX):
        lower = np.zeros_like(positions)
        upper = np.zeros_like(positions)
        lower[1:] = positions[:-1] + flow[1:] - positions[1:]
        upper[:-1] = positions[1:] - flow[1:] - positions[:-1]
        positions = positions + STEP_SIZE * (lower + upper - ANCHOR_WEIGHT * positions)
    return positions.astype(np.float32)


def split(value):
    high = value.astype(BF)
    return high, (value - high.astype(F32)).astype(BF)


def dot(a, b):
    return jnp.dot(a, b, preferred_element_type=F32)


def spectra(patches, table_ref):
    lines = []
    for pair in range(0, len(patches), 2):
        both = jnp.concatenate(patches[pair : pair + 2], 1)
        line = dot(table_ref[: 2 * HALF], jnp.concatenate([both, both], 0))
        lines += [line[:, :EXTENT], line[:, EXTENT:]]
    high, low = split(jnp.concatenate(lines, 0))
    product = dot(jnp.concatenate([high, low, high], 1), table_ref[2 * HALF :])
    result = []
    for k in range(len(patches)):
        a = product[2 * HALF * k : 2 * HALF * k + HALF]
        b = product[2 * HALF * k + HALF : 2 * HALF * (k + 1)]
        result.append((a[:, :EXTENT] - b[:, EXTENT:], -(a[:, EXTENT:] + b[:, :EXTENT])))
    return result


def energy(ref):
    rows = []
    for n in range(ref.shape[0]):
        value = ref[n].astype(F32)
        rows.append(jnp.sum(value * value, axis=0, keepdims=True))
    total = jnp.sum(jnp.concatenate(rows, 0), axis=1, keepdims=True)
    return total * (1.0 / (EXTENT * EXTENT))


def own_kernel(now_ref, table_ref, spectrum_ref, energy_ref):
    for pair in range(0, now_ref.shape[0], 2):
        for k, (real, imag) in enumerate(spectra([now_ref[pair], now_ref[pair + 1]], table_ref)):
            spectrum_ref[pair + k, :, :EXTENT] = real
            spectrum_ref[pair + k, :, EXTENT:] = imag
    energy_ref[...] = jnp.broadcast_to(energy(now_ref), energy_ref.shape)


def write_names(owner, route_ref, name_ref):
    slots = name_ref.shape[0]
    tile_count = route_ref.shape[1] // slots
    height = EXTENT // SHARE // tile_count
    lane = lax.broadcasted_iota(jnp.int32, (slots, tile_count * slots), 1)
    slot = lax.broadcasted_iota(jnp.int32, (slots, tile_count * slots), 0)
    names = jnp.broadcast_to(route_ref[...], lane.shape).astype(F32)
    place = lax.broadcasted_iota(jnp.int32, (slots, EXTENT), 1)
    here = place // (tile_count * height) == (owner & (SHARE - 1))
    row = jnp.zeros((slots, EXTENT), F32)
    for t in range(tile_count):
        own = jnp.sum(jnp.where(lane == slot + t * slots, names, 0.0), axis=1, keepdims=True)
        row = jnp.where(here & (place // height % tile_count == t), own, row)
    for p in range(slots):
        name_ref[p] = jnp.broadcast_to(row[p : p + 1], (8, EXTENT)).astype(BF)


def flow_kernel(place_ref, peak_ref, route_ref, low_ref, spectrum_ref, energy_ref, table_ref, inverse_ref, out_ref, name_ref):
    count = low_ref.shape[0]
    write_names(place_ref[:, :1], route_ref, name_ref)
    crosses = []
    for n, (lr, li) in enumerate(spectra([low_ref[n] for n in range(count)], table_ref)):
        nr = spectrum_ref[n, :, :EXTENT]
        ni = spectrum_ref[n, :, EXTENT:]
        crosses.append(jnp.concatenate([nr * lr + ni * li, ni * lr - nr * li], 1))
    third = 6 * EXTENT
    fourth = jnp.concatenate(
        [
            inverse_ref[third : third + 2 * REACH],
            inverse_ref[third + 2 * REACH :, : 6 * HALF - 2 * EXTENT],
        ],
        1,
    )
    high, low = split(jnp.concatenate(crosses, 0))
    outer = dot(jnp.concatenate([high, low, high], 1), inverse_ref[:third])
    correlations = []
    for pair in range(0, count, 2):
        columns = []
        for n in (pair, pair + 1):
            block = outer[HALF * n : HALF * (n + 1)]
            columns.append(jnp.concatenate([block[:, :EXTENT], block[:, EXTENT:]], 0))
        high, low = split(jnp.concatenate(columns, 1))
        result = dot(fourth, jnp.concatenate([high, low, high], 0))
        correlations += [result[:, :EXTENT], result[:, EXTENT:]]

    scale = (SCORE_GAIN / EXTENT) / jnp.sqrt(energy_ref[:, :1] * energy(low_ref) + EPSILON)
    shape = (2 * REACH, EXTENT)
    row = lax.broadcasted_iota(jnp.int32, shape, 0) - REACH
    column = lax.broadcasted_iota(jnp.int32, shape, 1)
    scores, relatives, tops = [], [], []
    for n in range(count):
        rel_y = row - peak_ref[0:1, n : n + 1]
        rel_x = ((column - peak_ref[1:2, n : n + 1] + EXTENT // 2) & (EXTENT - 1)) - EXTENT // 2
        quarter = EXTENT // 4
        inside = (rel_y >= -quarter) & (rel_y < quarter) & (rel_x >= -quarter) & (rel_x < quarter)
        score = jnp.where(inside, correlations[n] * scale[n : n + 1], -1e30)
        scores.append(score)
        relatives.append((rel_y.astype(F32), rel_x[:1].astype(F32)))
        tops.append(jnp.max(score, axis=0, keepdims=True))
    top = jnp.max(jnp.concatenate(tops, 0), axis=1, keepdims=True)
    sums, sums_y, sums_x = [], [], []
    for n in range(count):
        weight = jnp.exp(scores[n] - top[n : n + 1])
        rel_y, rel_x = relatives[n]
        along = jnp.sum(weight, axis=0, keepdims=True)
        sums.append(along)
        sums_y.append(jnp.sum(weight * rel_y, axis=0, keepdims=True))
        sums_x.append(along * rel_x)
    total, total_y, total_x = (
        jnp.sum(jnp.concatenate(s, 0), axis=1, keepdims=True) for s in (sums, sums_y, sums_x)
    )
    node = lax.broadcasted_iota(jnp.int32, (count, EXTENT), 0)
    lane = lax.broadcasted_iota(jnp.int32, (count, EXTENT), 1)
    peak_y = jnp.zeros((count, EXTENT), jnp.int32)
    peak_x = jnp.zeros((count, EXTENT), jnp.int32)
    for n in range(count):
        peak_y = jnp.where(node == n, peak_ref[0:1, n : n + 1], peak_y)
        peak_x = jnp.where(node == n, peak_ref[1:2, n : n + 1], peak_x)
    flow_y = peak_y.astype(F32) + total_y / total
    flow_x = peak_x.astype(F32) + total_x / total
    flow = jnp.where(lane == node, flow_y, jnp.where(lane == node + count, flow_x, 0.0))
    flow = jnp.sum(flow, axis=0, keepdims=True)
    out_ref[...] = jnp.broadcast_to(flow[None], out_ref.shape)


def fill_band(target_ref, residual, offset, sub_sign):
    block = EXTENT
    lane = lax.broadcasted_iota(jnp.int32, (1, block), 1)
    tap = (lane - BAND).astype(F32) - residual
    raw = jnp.where(lane <= 2 * BAND, 1.0 / (1.0 + tap * tap), 0.0)
    norm = jnp.sum(raw, axis=1, keepdims=True)
    a = lax.broadcasted_iota(jnp.int32, (block, block), 0)
    b = lax.broadcasted_iota(jnp.int32, (block, block), 1)
    d = sub_sign * (a - b) - offset
    k = ((d + block // 2) & (block - 1)) - block // 2
    away = k.astype(F32) - residual
    value = (1.0 / (1.0 + away * away)) / norm
    blocks = {}
    for step in (-1, 0, 1):
        near = jnp.abs(d + sub_sign * step * block) <= BAND
        blocks[step] = jnp.where(near, value, 0.0).astype(BF)
    zero = jnp.zeros((block, block), BF)
    count = target_ref.shape[0] // block
    for i in range(count):
        for j in range(count):
            target_ref[i * block : (i + 1) * block, j * block : (j + 1) * block] = blocks.get(
                i - j, zero
            )


def render_kernel(band_ref, map_ref, flow_ref, name_ref, tile_ref, position_ref, send_ref, *scratch):
    tile_count, edge, _ = tile_ref.shape
    slots = send_ref.shape[0]
    section = lax.axis_index("gz")
    second_core = section % 2 == 1

    def slot_of(p):
        return jnp.where(second_core, p % WIDE * (slots // WIDE) + p // WIDE, p)

    lanes = lax.broadcasted_iota(jnp.int32, map_ref.shape, 1)
    weights = jnp.sum(jnp.where(lanes == section, map_ref[...], 0.0), axis=1, keepdims=True)
    position = jnp.sum(weights * flow_ref[:, 0, :], axis=0, keepdims=True)
    nodes = position_ref.shape[1]
    for c in range(2):
        position_ref[c : c + 1, :] = position[:, c * nodes : (c + 1) * nodes]
    per_tile = nodes // tile_count
    lanes = lax.broadcasted_iota(jnp.int32, position.shape, 1)
    height = edge // slots
    columns = edge // EXTENT
    chunk = EXTENT
    chunks = edge // chunk

    def fill(t, c, target_ref, sub_sign):
        offset = band_ref[t : t + 1, c : c + 1]
        here = lanes // per_tile == c * tile_count + t
        total = jnp.sum(jnp.where(here, position, 0.0), axis=1, keepdims=True)
        shift = total * (MIP_SCALE / per_tile)
        fill_band(target_ref, shift - offset.astype(F32), offset, sub_sign)

    def first(t, c):
        col_ref, _, pass_ref = scratch[3 * t : 3 * t + 3]
        rows = slice(c * chunk, (c + 1) * chunk)
        pass_ref[rows, :] = dot(tile_ref[t, rows, :], col_ref[...]).astype(BF)

    def second(t, c):
        _, row_ref, pass_ref = scratch[3 * t : 3 * t + 3]
        near = range(max(c - 1, 0), min(c + 2, chunks))
        from_row = near[0] * chunk // (edge // 2) * (edge // 2)
        to_row = edge // 2 if near[-1] * chunk < edge // 2 else edge
        rows = slice(c * chunk, (c + 1) * chunk)
        done = dot(row_ref[rows, from_row:to_row], pass_ref[from_row:to_row, :]).astype(BF)
        each = chunk // height
        done = done.reshape(each, height, edge)
        for p in range(each):
            for j in range(columns):
                at = (t * columns + j) * height
                send_ref[slot_of(c * each + p), at : at + height, :] = done[
                    p, :, j * EXTENT : (j + 1) * EXTENT
                ]

    tail = tile_count * columns * height
    fill(0, 1, scratch[0], 1)
    for t in range(tile_count):
        for c in range(chunks):
            first(t, c)
            if c == 0:
                fill(t, 0, scratch[3 * t + 1], -1)
            if c == 1 and t + 1 < tile_count:
                fill(t + 1, 1, scratch[3 * t + 3], 1)
            if t > 0:
                second(t - 1, c)
    for c in range(chunks):
        second(tile_count - 1, c)
        for p in range(c * slots // chunks, (c + 1) * slots // chunks):
            send_ref[slot_of(p), tail:, :] = name_ref[p]


def gather_kernel(piece_ref, out_ref, data_ref):
    owners, rows, _ = piece_ref.shape
    _, out_rows, edge = out_ref.shape
    height = edge // owners
    columns = edge // EXTENT
    tail = rows - 8
    tile_count = tail // (columns * height)
    part = EXTENT // SHARE // tile_count
    parts = height // part
    depth = owners * tile_count * part
    for d in range(owners):
        for j in range(columns):
            pieces = []
            for t in range(tile_count):
                at = (t * columns + j) * height
                pieces.append(piece_ref[d, at : at + height, :].astype(F32))
            for k in range(parts):
                at = k * depth + d * tile_count * part
                data_ref[at : at + tile_count * part, j * EXTENT : (j + 1) * EXTENT] = (
                    jnp.concatenate([p[k * part : (k + 1) * part] for p in pieces], 0).astype(BF)
                )
    lane = lax.broadcasted_iota(jnp.int32, (EXTENT, EXTENT), 1)
    sub = lax.broadcasted_iota(jnp.int32, (EXTENT, EXTENT), 0)
    same = lane % part == sub % part
    names = [
        sum(piece_ref[d, tail : tail + 8, :].astype(F32) for d in range(start, start + SHARE))[0:1]
        for start in range(0, owners, SHARE)
    ]
    each = EXTENT // part
    for c in range(owners * out_rows // height // each):
        group = (sub // part + c * each).astype(F32)
        hits = [jnp.where(same & (name == group), 1.0, 0.0) for name in names]
        count = jnp.sum(sum(hits), axis=1, keepdims=True)
        scale = 1.0 / jnp.maximum(count, 1.0)
        pick = jnp.concatenate([hit.astype(BF) for hit in hits], 1)
        totals = [
            (dot(pick, data_ref[k * depth : (k + 1) * depth]) * scale).reshape(each, part, edge)
            for k in range(parts)
        ]
        total = jnp.concatenate(totals, 1).astype(BF)
        first, last = c * each * height // out_rows, (c + 1) * each * height // out_rows
        out_ref[first:last] = total.reshape(last - first, out_rows, edge)


def place_kernel(position_ref, cell_ref, moved_ref, out_ref, arrived):
    height = out_ref.shape[2]
    copies = [
        pltpu.make_async_copy(
            cell_ref.at[:, g * height : (g + 1) * height, :], out_ref.at[g], arrived.at[g]
        )
        for g in range(out_ref.shape[0])
    ]
    copies.append(pltpu.make_async_copy(position_ref, moved_ref, arrived.at[len(copies)]))
    for copy in copies:
        copy.start()
    for copy in copies:
        copy.wait()


def in_vmem():
    return pl.BlockSpec(memory_space=pltpu.VMEM)


def in_smem():
    return pl.BlockSpec(memory_space=pltpu.SMEM)


def params():
    return pltpu.CompilerParams(vmem_limit_bytes=40 * 1024 * 1024)


def exchange(value, axis, groups=None):
    return lax.all_to_all(
        value, axis, split_axis=0, concat_axis=0, tiled=True, axis_index_groups=groups
    )


def exchange_x_then_z(value):
    owners, rows, lanes = value.shape
    high = owners // WIDE
    along_x = [[z * WIDE + x for x in range(WIDE)] for z in range(high)]
    along_z = [[z * WIDE + x for z in range(high)] for x in range(WIDE)]
    value = exchange(value.reshape(WIDE, high * rows, lanes), "xy", along_x)
    value = value.reshape(WIDE, high, rows, lanes).transpose(1, 0, 2, 3)
    value = exchange(value.reshape(high, WIDE * rows, lanes), "xy", along_z)
    return value.reshape(owners, rows, lanes)


def body(patches, peak_offsets, tiles, band_offsets, routes):
    sections = lax.axis_size("gz")
    owners = lax.axis_size("xy")
    tile_count, edge = tiles.shape[1], tiles.shape[-1]
    height = edge // PIECES
    share = 2
    count = patches.shape[1]

    section = lax.axis_index("gz")
    below = lax.ppermute(patches, "gz", [(i, i + 1) for i in range(sections - 1)])
    early_table, late_table = (jnp.asarray(t) for t in dft_constants())
    second_core = section % 2 == 1
    place = jnp.stack([lax.axis_index("xy"), second_core.astype(jnp.int32)])[None]
    spectrum, power = pl.pallas_call(
        own_kernel,
        out_shape=(
            jax.ShapeDtypeStruct((count, HALF, 2 * EXTENT), F32),
            jax.ShapeDtypeStruct((count, EXTENT), F32),
        ),
        in_specs=[in_vmem()] * 2,
        out_specs=(in_vmem(),) * 2,
        compiler_params=params(),
        cost_estimate=pl.CostEstimate(flops=10**9, bytes_accessed=2**20, transcendentals=0),
        name="own",
    )(patches[0], early_table)
    flow, names = pl.pallas_call(
        flow_kernel,
        out_shape=(
            jax.ShapeDtypeStruct((sections, 1, EXTENT), F32),
            jax.ShapeDtypeStruct((PIECES, 8, EXTENT), BF),
        ),
        in_specs=[in_vmem()] * 8,
        out_specs=(in_vmem(),) * 2,
        compiler_params=params(),
        name="flow",
    )(place, peak_offsets[0].T, routes[0].T, below[0], spectrum, power, early_table, late_table)
    flow = exchange(flow, "gz")

    position, pieces = pl.pallas_call(
        render_kernel,
        out_shape=(
            jax.ShapeDtypeStruct((2, count), F32),
            jax.ShapeDtypeStruct((PIECES, tile_count * height * edge // EXTENT + 8, EXTENT), BF),
        ),
        in_specs=[in_vmem()] * 5,
        out_specs=(in_vmem(), in_vmem()),
        scratch_shapes=[pltpu.VMEM((edge, edge), BF)] * (3 * tile_count),
        compiler_params=params(),
        name="render",
    )(band_offsets[0], jnp.asarray(relaxation_map(sections).T), flow, names, tiles[0])
    pieces = lax.cond(
        second_core,
        exchange_x_then_z,
        lambda value: exchange(value, "xy"),
        pieces,
    )

    cells = pl.pallas_call(
        gather_kernel,
        out_shape=jax.ShapeDtypeStruct((owners, share * height, edge), BF),
        in_specs=[in_vmem()],
        out_specs=in_vmem(),
        scratch_shapes=[pltpu.VMEM((owners * tile_count * height, edge), BF)],
        compiler_params=params(),
        name="gather",
    )(pieces)
    cells = exchange(cells, "xy")
    position, rendered = pl.pallas_call(
        place_kernel,
        out_shape=(
            jax.ShapeDtypeStruct(position.shape, F32),
            jax.ShapeDtypeStruct((share, PIECES, height, edge), BF),
        ),
        in_specs=[in_vmem()] * 2,
        out_specs=(pl.BlockSpec(memory_space=pl.ANY),) * 2,
        scratch_shapes=[pltpu.SemaphoreType.DMA((share + 1,))],
        compiler_params=params(),
        name="place",
    )(position, cells)
    rendered = rendered.reshape(1, share, edge, edge)
    return position[None], rendered


def solution(mesh):
    placed = (
        P("gz", "xy", None, None),
        P("gz", "xy", None),
        P("gz", "xy", None, None),
        P("gz", "xy", None),
        P("gz", "xy", None),
    )
    return jax.shard_map(
        body,
        mesh=mesh,
        in_specs=placed,
        out_specs=(P("gz", None, "xy"), P("gz", "xy", None, None)),
        check_vma=False,
    )
```

```python
import jax
import jax.numpy as jnp
import numpy as np
from jax import lax
from jax.experimental import pallas as pl
from jax.experimental.pallas import tpu as pltpu
from jax.sharding import PartitionSpec as P

PIECES = 32
SHARE = 8
BAND = 6
RELAX = 3
EPSILON = 1e-06
STEP_SIZE = 0.25
ANCHOR_WEIGHT = 0.5
MIP_SCALE = 0.0625
SCORE_GAIN = 6.0

EXTENT = 128
HALF = 72
REACH = 40
BF = jnp.bfloat16
F32 = jnp.float32


def high_low(table):
    high = table.astype(jnp.bfloat16)
    low = (table - high.astype(np.float64)).astype(jnp.bfloat16)
    return high, low


def dft_constants():
    line = np.arange(EXTENT)
    phase = 2.0 * np.pi * ((line[:, None] * line[None, :]) % EXTENT) / EXTENT
    cos, sin = np.cos(phase), np.sin(phase)
    first = np.concatenate([cos[:HALF], sin[:HALF]], 0)
    first = np.concatenate(high_low(first), 1)
    second_high, second_low = high_low(np.concatenate([cos, sin], 1))
    second = np.concatenate([second_high, second_high, second_low], 0)
    third_high, third_low = high_low(np.block([[cos, sin], [-sin, cos]]))
    third = np.concatenate([third_high, third_high, third_low], 0)
    weight = np.where(line[:HALF] <= EXTENT // 2, 2.0, 0.0)
    weight[0] = weight[EXTENT // 2] = 1.0
    rows = (np.arange(-REACH, REACH) % EXTENT)[:, None]
    angle = 2.0 * np.pi * ((rows * line[None, :HALF]) % EXTENT) / EXTENT
    fourth = np.concatenate([weight * np.cos(angle), -weight * np.sin(angle)], 1)
    fourth_high, fourth_low = high_low(fourth / float(EXTENT * EXTENT))
    fourth = np.concatenate([fourth_high, fourth_high, fourth_low], 1)
    fourth = np.pad(fourth, ((0, 0), (0, 4 * EXTENT - fourth.shape[1])))
    early = np.concatenate([first, second], 0)
    late = np.concatenate([third, fourth[:, : 2 * EXTENT], fourth[:, 2 * EXTENT :]], 0)
    return early, late


def relaxation_map(sections):
    flow = np.eye(sections)
    positions = np.tril(np.ones((sections, sections)))
    for _ in range(RELAX):
        lower = np.zeros_like(positions)
        upper = np.zeros_like(positions)
        lower[1:] = positions[:-1] + flow[1:] - positions[1:]
        upper[:-1] = positions[1:] - flow[1:] - positions[:-1]
        positions = positions + STEP_SIZE * (lower + upper - ANCHOR_WEIGHT * positions)
    return positions.astype(np.float32)


def split(value):
    high = value.astype(BF)
    return high, (value - high.astype(F32)).astype(BF)


def dot(a, b):
    return jnp.dot(a, b, preferred_element_type=F32)


def spectra(patches, table_ref):
    lines = []
    for pair in range(0, len(patches), 2):
        both = jnp.concatenate(patches[pair : pair + 2], 1)
        line = dot(table_ref[: 2 * HALF], jnp.concatenate([both, both], 0))
        lines += [line[:, :EXTENT], line[:, EXTENT:]]
    high, low = split(jnp.concatenate(lines, 0))
    product = dot(jnp.concatenate([high, low, high], 1), table_ref[2 * HALF :])
    result = []
    for k in range(len(patches)):
        a = product[2 * HALF * k : 2 * HALF * k + HALF]
        b = product[2 * HALF * k + HALF : 2 * HALF * (k + 1)]
        result.append((a[:, :EXTENT] - b[:, EXTENT:], -(a[:, EXTENT:] + b[:, :EXTENT])))
    return result


def energy(ref):
    rows = []
    for n in range(ref.shape[0]):
        value = ref[n].astype(F32)
        rows.append(jnp.sum(value * value, axis=0, keepdims=True))
    total = jnp.sum(jnp.concatenate(rows, 0), axis=1, keepdims=True)
    return total * (1.0 / (EXTENT * EXTENT))


def own_kernel(now_ref, table_ref, spectrum_ref, energy_ref):
    shape = (HALF, EXTENT)
    row = lax.broadcasted_iota(jnp.int32, shape, 0)
    mean = (row == 0) & (lax.broadcasted_iota(jnp.int32, shape, 1) == 0)
    for pair in range(0, now_ref.shape[0], 2):
        for k, (real, imag) in enumerate(spectra([now_ref[pair], now_ref[pair + 1]], table_ref)):
            real, imag = jnp.where(mean, 0.0, real), jnp.where(mean, 0.0, imag)
            spectrum_ref[pair + k, :, :EXTENT] = real
            spectrum_ref[pair + k, :, EXTENT:] = imag
    energy_ref[...] = jnp.broadcast_to(energy(now_ref), energy_ref.shape)


def write_names(owner, second_core, route_ref, name_ref):
    slots = name_ref.shape[0]
    tile_count = route_ref.shape[1] // slots
    height = EXTENT // SHARE // tile_count
    lane = lax.broadcasted_iota(jnp.int32, (slots, tile_count * slots), 1)
    slot = lax.broadcasted_iota(jnp.int32, (slots, tile_count * slots), 0)
    names = jnp.broadcast_to(route_ref[...], lane.shape).astype(F32)
    place = lax.broadcasted_iota(jnp.int32, (slots, EXTENT), 1)
    own_place = owner & (SHARE - 1)
    slot_column = lax.broadcasted_iota(jnp.int32, (slots, 1), 0)
    pair_place = (own_place & (SHARE - 2)) | ((owner ^ slot_column) & 1)
    here = place // (tile_count * height) == jnp.where(second_core == 1, pair_place, own_place)
    row = jnp.zeros((slots, EXTENT), F32)
    for t in range(tile_count):
        own = jnp.sum(jnp.where(lane == slot + t * slots, names, 0.0), axis=1, keepdims=True)
        row = jnp.where(here & (place // height % tile_count == t), own, row)
    for p in range(slots):
        name_ref[p] = jnp.broadcast_to(row[p : p + 1], (8, EXTENT)).astype(BF)


def flow_kernel(place_ref, peak_ref, route_ref, low_ref, spectrum_ref, energy_ref, table_ref, inverse_ref, out_ref, name_ref):
    count = low_ref.shape[0]
    write_names(place_ref[:, :1], place_ref[:, 1:], route_ref, name_ref)
    crosses = []
    for n, (lr, li) in enumerate(spectra([low_ref[n] for n in range(count)], table_ref)):
        nr = spectrum_ref[n, :, :EXTENT]
        ni = spectrum_ref[n, :, EXTENT:]
        crosses.append(jnp.concatenate([nr * lr + ni * li, ni * lr - nr * li], 1))
    third = 6 * EXTENT
    fourth = jnp.concatenate(
        [
            inverse_ref[third : third + 2 * REACH],
            inverse_ref[third + 2 * REACH :, : 6 * HALF - 2 * EXTENT],
        ],
        1,
    )
    high, low = split(jnp.concatenate(crosses, 0))
    outer = dot(jnp.concatenate([high, low, high], 1), inverse_ref[:third])
    correlations = []
    for pair in range(0, count, 2):
        columns = []
        for n in (pair, pair + 1):
            block = outer[HALF * n : HALF * (n + 1)]
            columns.append(jnp.concatenate([block[:, :EXTENT], block[:, EXTENT:]], 0))
        high, low = split(jnp.concatenate(columns, 1))
        result = dot(fourth, jnp.concatenate([high, low, high], 0))
        correlations += [result[:, :EXTENT], result[:, EXTENT:]]

    scale = (SCORE_GAIN / EXTENT) / jnp.sqrt(energy_ref[:, :1] * energy(low_ref) + EPSILON)
    shape = (2 * REACH, EXTENT)
    row = lax.broadcasted_iota(jnp.int32, shape, 0) - REACH
    column = lax.broadcasted_iota(jnp.int32, shape, 1)
    scores, relatives, tops = [], [], []
    for n in range(count):
        rel_y = row - peak_ref[0:1, n : n + 1]
        rel_x = ((column - peak_ref[1:2, n : n + 1] + EXTENT // 2) & (EXTENT - 1)) - EXTENT // 2
        quarter = EXTENT // 4
        inside = (rel_y >= -quarter) & (rel_y < quarter) & (rel_x >= -quarter) & (rel_x < quarter)
        score = jnp.where(inside, correlations[n] * scale[n : n + 1], -1e30)
        scores.append(score)
        relatives.append((rel_y.astype(F32), rel_x[:1].astype(F32)))
        tops.append(jnp.max(score, axis=0, keepdims=True))
    top = jnp.max(jnp.concatenate(tops, 0), axis=1, keepdims=True)
    sums, sums_y, sums_x = [], [], []
    for n in range(count):
        weight = jnp.exp(scores[n] - top[n : n + 1])
        rel_y, rel_x = relatives[n]
        along = jnp.sum(weight, axis=0, keepdims=True)
        sums.append(along)
        sums_y.append(jnp.sum(weight * rel_y, axis=0, keepdims=True))
        sums_x.append(along * rel_x)
    total, total_y, total_x = (
        jnp.sum(jnp.concatenate(s, 0), axis=1, keepdims=True) for s in (sums, sums_y, sums_x)
    )
    node = lax.broadcasted_iota(jnp.int32, (count, EXTENT), 0)
    lane = lax.broadcasted_iota(jnp.int32, (count, EXTENT), 1)
    peak_y = jnp.zeros((count, EXTENT), jnp.int32)
    peak_x = jnp.zeros((count, EXTENT), jnp.int32)
    for n in range(count):
        peak_y = jnp.where(node == n, peak_ref[0:1, n : n + 1], peak_y)
        peak_x = jnp.where(node == n, peak_ref[1:2, n : n + 1], peak_x)
    flow_y = peak_y.astype(F32) + total_y / total
    flow_x = peak_x.astype(F32) + total_x / total
    flow = jnp.where(lane == node, flow_y, jnp.where(lane == node + count, flow_x, 0.0))
    flow = jnp.sum(flow, axis=0, keepdims=True)
    out_ref[...] = jnp.broadcast_to(flow[None], out_ref.shape)


def fill_band(target_ref, residual, offset, sub_sign):
    block = EXTENT
    lane = lax.broadcasted_iota(jnp.int32, (1, block), 1)
    tap = (lane - BAND).astype(F32) - residual
    raw = jnp.where(lane <= 2 * BAND, 1.0 / (1.0 + tap * tap), 0.0)
    norm = jnp.sum(raw, axis=1, keepdims=True)
    a = lax.broadcasted_iota(jnp.int32, (block, block), 0)
    b = lax.broadcasted_iota(jnp.int32, (block, block), 1)
    d = sub_sign * (a - b) - offset
    k = ((d + block // 2) & (block - 1)) - block // 2
    away = k.astype(F32) - residual
    value = (1.0 / (1.0 + away * away)) / norm
    blocks = {}
    for step in (-1, 0, 1):
        near = jnp.abs(d + sub_sign * step * block) <= BAND
        blocks[step] = jnp.where(near, value, 0.0).astype(BF)
    zero = jnp.zeros((block, block), BF)
    count = target_ref.shape[0] // block
    for i in range(count):
        for j in range(count):
            target_ref[i * block : (i + 1) * block, j * block : (j + 1) * block] = blocks.get(
                i - j, zero
            )


def render_kernel(band_ref, map_ref, flow_ref, name_ref, tile_ref, position_ref, send_ref, *scratch):
    tile_count, edge, _ = tile_ref.shape
    slots = send_ref.shape[0]
    section, owner = lax.axis_index("gz"), lax.axis_index("xy")
    second_core = section % 2 == 1

    def slot_of(p):
        return jnp.where(second_core, ((owner + p) % 2) * (slots // 2) + p // 2, p)

    lanes = lax.broadcasted_iota(jnp.int32, map_ref.shape, 1)
    weights = jnp.sum(jnp.where(lanes == section, map_ref[...], 0.0), axis=1, keepdims=True)
    position = jnp.sum(weights * flow_ref[:, 0, :], axis=0, keepdims=True)
    nodes = position_ref.shape[1]
    for c in range(2):
        position_ref[c : c + 1, :] = position[:, c * nodes : (c + 1) * nodes]
    per_tile = nodes // tile_count
    lanes = lax.broadcasted_iota(jnp.int32, position.shape, 1)
    height = edge // slots
    columns = edge // EXTENT
    chunk = EXTENT
    chunks = edge // chunk

    def fill(t, c, target_ref, sub_sign):
        offset = band_ref[t : t + 1, c : c + 1]
        here = lanes // per_tile == c * tile_count + t
        total = jnp.sum(jnp.where(here, position, 0.0), axis=1, keepdims=True)
        shift = total * (MIP_SCALE / per_tile)
        fill_band(target_ref, shift - offset.astype(F32), offset, sub_sign)

    def first(t, c):
        col_ref, _, pass_ref = scratch[3 * t : 3 * t + 3]
        rows = slice(c * chunk, (c + 1) * chunk)
        pass_ref[rows, :] = dot(tile_ref[t, rows, :], col_ref[...]).astype(BF)

    def second(t, c):
        _, row_ref, pass_ref = scratch[3 * t : 3 * t + 3]
        near = range(max(c - 1, 0), min(c + 2, chunks))
        from_row = near[0] * chunk // (edge // 2) * (edge // 2)
        to_row = edge // 2 if near[-1] * chunk < edge // 2 else edge
        rows = slice(c * chunk, (c + 1) * chunk)
        done = dot(row_ref[rows, from_row:to_row], pass_ref[from_row:to_row, :]).astype(BF)
        each = chunk // height
        done = done.reshape(each, height, edge)
        for p in range(each):
            for j in range(columns):
                at = (t * columns + j) * height
                send_ref[slot_of(c * each + p), at : at + height, :] = done[
                    p, :, j * EXTENT : (j + 1) * EXTENT
                ]

    tail = tile_count * columns * height
    fill(0, 1, scratch[0], 1)
    for t in range(tile_count):
        for c in range(chunks):
            first(t, c)
            if c == 0:
                fill(t, 0, scratch[3 * t + 1], -1)
            if c == 1 and t + 1 < tile_count:
                fill(t + 1, 1, scratch[3 * t + 3], 1)
            if t > 0:
                second(t - 1, c)
    for c in range(chunks):
        second(tile_count - 1, c)
        for p in range(c * slots // chunks, (c + 1) * slots // chunks):
            send_ref[slot_of(p), tail:, :] = name_ref[p]


def gather_kernel(piece_ref, out_ref, data_ref):
    owners, rows, _ = piece_ref.shape
    _, out_rows, edge = out_ref.shape
    height = edge // owners
    columns = edge // EXTENT
    tail = rows - 8
    tile_count = tail // (columns * height)
    part = EXTENT // SHARE // tile_count
    parts = height // part
    depth = owners * tile_count * part
    for d in range(owners):
        for j in range(columns):
            pieces = []
            for t in range(tile_count):
                at = (t * columns + j) * height
                pieces.append(piece_ref[d, at : at + height, :].astype(F32))
            for k in range(parts):
                at = k * depth + d * tile_count * part
                data_ref[at : at + tile_count * part, j * EXTENT : (j + 1) * EXTENT] = (
                    jnp.concatenate([p[k * part : (k + 1) * part] for p in pieces], 0).astype(BF)
                )
    lane = lax.broadcasted_iota(jnp.int32, (EXTENT, EXTENT), 1)
    sub = lax.broadcasted_iota(jnp.int32, (EXTENT, EXTENT), 0)
    same = lane % part == sub % part
    names = [
        sum(piece_ref[d, tail : tail + 8, :].astype(F32) for d in range(start, start + SHARE))[0:1]
        for start in range(0, owners, SHARE)
    ]
    each = EXTENT // part
    for c in range(owners * out_rows // height // each):
        group = (sub // part + c * each).astype(F32)
        hits = [jnp.where(same & (name == group), 1.0, 0.0) for name in names]
        count = jnp.sum(sum(hits), axis=1, keepdims=True)
        scale = 1.0 / jnp.maximum(count, 1.0)
        pick = jnp.concatenate([hit.astype(BF) for hit in hits], 1)
        totals = [
            (dot(pick, data_ref[k * depth : (k + 1) * depth]) * scale).reshape(each, part, edge)
            for k in range(parts)
        ]
        total = jnp.concatenate(totals, 1).astype(BF)
        first, last = c * each * height // out_rows, (c + 1) * each * height // out_rows
        out_ref[first:last] = total.reshape(last - first, out_rows, edge)


def place_kernel(position_ref, cell_ref, moved_ref, out_ref, arrived):
    height = out_ref.shape[2]
    copies = [
        pltpu.make_async_copy(
            cell_ref.at[:, g * height : (g + 1) * height, :], out_ref.at[g], arrived.at[g]
        )
        for g in range(out_ref.shape[0])
    ]
    copies.append(pltpu.make_async_copy(position_ref, moved_ref, arrived.at[len(copies)]))
    for copy in copies:
        copy.start()
    for copy in copies:
        copy.wait()


def in_vmem():
    return pl.BlockSpec(memory_space=pltpu.VMEM)


def in_smem():
    return pl.BlockSpec(memory_space=pltpu.SMEM)


def params():
    return pltpu.CompilerParams(vmem_limit_bytes=40 * 1024 * 1024)


def exchange(value, axis, groups=None):
    return lax.all_to_all(
        value, axis, split_axis=0, concat_axis=0, tiled=True, axis_index_groups=groups
    )


def exchange_pair_first(value):
    owners, rows, lanes = value.shape
    half = owners // 2
    kept, given = value[:half], value[half:]
    taken = lax.ppermute(given, "xy", [(i, i ^ 1) for i in range(owners)])
    value = jnp.concatenate([kept, taken], 1)
    parity = [[2 * i + q for i in range(half)] for q in range(2)]
    return exchange(value, "xy", parity).reshape(owners, rows, lanes)


def body(patches, peak_offsets, tiles, band_offsets, routes):
    sections = lax.axis_size("gz")
    owners = lax.axis_size("xy")
    tile_count, edge = tiles.shape[1], tiles.shape[-1]
    height = edge // PIECES
    share = 2
    count = patches.shape[1]

    section = lax.axis_index("gz")
    below = lax.ppermute(patches, "gz", [(i, i + 1) for i in range(sections - 1)])
    early_table, late_table = (jnp.asarray(t) for t in dft_constants())
    second_core = section % 2 == 1
    place = jnp.stack([lax.axis_index("xy"), second_core.astype(jnp.int32)])[None]
    spectrum, power = pl.pallas_call(
        own_kernel,
        out_shape=(
            jax.ShapeDtypeStruct((count, HALF, 2 * EXTENT), F32),
            jax.ShapeDtypeStruct((count, EXTENT), F32),
        ),
        in_specs=[in_vmem()] * 2,
        out_specs=(in_vmem(),) * 2,
        compiler_params=params(),
        cost_estimate=pl.CostEstimate(flops=10**9, bytes_accessed=2**20, transcendentals=0),
        name="own",
    )(patches[0], early_table)
    flow, names = pl.pallas_call(
        flow_kernel,
        out_shape=(
            jax.ShapeDtypeStruct((sections, 1, EXTENT), F32),
            jax.ShapeDtypeStruct((PIECES, 8, EXTENT), BF),
        ),
        in_specs=[in_vmem()] * 8,
        out_specs=(in_vmem(),) * 2,
        compiler_params=params(),
        name="flow",
    )(place, peak_offsets[0].T, routes[0].T, below[0], spectrum, power, early_table, late_table)
    flow = exchange(flow, "gz")

    position, pieces = pl.pallas_call(
        render_kernel,
        out_shape=(
            jax.ShapeDtypeStruct((2, count), F32),
            jax.ShapeDtypeStruct((PIECES, tile_count * height * edge // EXTENT + 8, EXTENT), BF),
        ),
        in_specs=[in_vmem()] * 5,
        out_specs=(in_vmem(), in_vmem()),
        scratch_shapes=[pltpu.VMEM((edge, edge), BF)] * (3 * tile_count),
        compiler_params=params(),
        name="render",
    )(band_offsets[0], jnp.asarray(relaxation_map(sections).T), flow, names, tiles[0])
    pieces = lax.cond(
        second_core,
        exchange_pair_first,
        lambda value: exchange(value, "xy"),
        pieces,
    )

    cells = pl.pallas_call(
        gather_kernel,
        out_shape=jax.ShapeDtypeStruct((owners, share * height, edge), BF),
        in_specs=[in_vmem()],
        out_specs=in_vmem(),
        scratch_shapes=[pltpu.VMEM((owners * tile_count * height, edge), BF)],
        compiler_params=params(),
        name="gather",
    )(pieces)
    cells = exchange(cells, "xy")
    position, rendered = pl.pallas_call(
        place_kernel,
        out_shape=(
            jax.ShapeDtypeStruct(position.shape, F32),
            jax.ShapeDtypeStruct((share, PIECES, height, edge), BF),
        ),
        in_specs=[in_vmem()] * 2,
        out_specs=(pl.BlockSpec(memory_space=pl.ANY),) * 2,
        scratch_shapes=[pltpu.SemaphoreType.DMA((share + 1,))],
        compiler_params=params(),
        name="place",
    )(position, cells)
    rendered = rendered.reshape(1, share, edge, edge)
    return position[None], rendered


def solution(mesh):
    placed = (
        P("gz", "xy", None, None),
        P("gz", "xy", None),
        P("gz", "xy", None, None),
        P("gz", "xy", None),
        P("gz", "xy", None),
    )
    return jax.shard_map(
        body,
        mesh=mesh,
        in_specs=placed,
        out_specs=(P("gz", None, "xy"), P("gz", "xy", None, None)),
        check_vma=False,
    )
```

```python
import jax
import jax.numpy as jnp
import numpy as np
from jax import lax
from jax.experimental import pallas as pl
from jax.experimental.pallas import tpu as pltpu
from jax.sharding import PartitionSpec as P

PIECES = 32
WIDE = 4
SHARE = 8
BAND = 6
RELAX = 3
EPSILON = 1e-06
STEP_SIZE = 0.25
ANCHOR_WEIGHT = 0.5
MIP_SCALE = 0.0625
SCORE_GAIN = 6.0

EXTENT = 128
HALF = 72
REACH = 40
BF = jnp.bfloat16
F32 = jnp.float32


def high_low(table):
    high = table.astype(jnp.bfloat16)
    low = (table - high.astype(np.float64)).astype(jnp.bfloat16)
    return high, low


def dft_constants():
    line = np.arange(EXTENT)
    phase = 2.0 * np.pi * ((line[:, None] * line[None, :]) % EXTENT) / EXTENT
    cos, sin = np.cos(phase), np.sin(phase)
    first = np.concatenate([cos[:HALF], sin[:HALF]], 0)
    first = np.concatenate(high_low(first), 1)
    second_high, second_low = high_low(np.concatenate([cos, sin], 1))
    second = np.concatenate([second_high, second_high, second_low], 0)
    third_high, third_low = high_low(np.block([[cos, sin], [-sin, cos]]))
    third = np.concatenate([third_high, third_high, third_low], 0)
    weight = np.where(line[:HALF] <= EXTENT // 2, 2.0, 0.0)
    weight[0] = weight[EXTENT // 2] = 1.0
    rows = (np.arange(-REACH, REACH) % EXTENT)[:, None]
    angle = 2.0 * np.pi * ((rows * line[None, :HALF]) % EXTENT) / EXTENT
    fourth = np.concatenate([weight * np.cos(angle), -weight * np.sin(angle)], 1)
    fourth_high, fourth_low = high_low(fourth / float(EXTENT * EXTENT))
    fourth = np.concatenate([fourth_high, fourth_high, fourth_low], 1)
    fourth = np.pad(fourth, ((0, 0), (0, 4 * EXTENT - fourth.shape[1])))
    early = np.concatenate([first, second], 0)
    late = np.concatenate([third, fourth[:, : 2 * EXTENT], fourth[:, 2 * EXTENT :]], 0)
    return early, late


def relaxation_map(sections):
    flow = np.eye(sections)
    positions = np.tril(np.ones((sections, sections)))
    for _ in range(RELAX):
        lower = np.zeros_like(positions)
        upper = np.zeros_like(positions)
        lower[1:] = positions[:-1] + flow[1:] - positions[1:]
        upper[:-1] = positions[1:] - flow[1:] - positions[:-1]
        positions = positions + STEP_SIZE * (lower + upper - ANCHOR_WEIGHT * positions)
    return positions.astype(np.float32)


def split(value):
    high = value.astype(BF)
    return high, (value - high.astype(F32)).astype(BF)


def dot(a, b):
    return jnp.dot(a, b, preferred_element_type=F32)


def spectra(patches, table_ref):
    lines = []
    for pair in range(0, len(patches), 2):
        both = jnp.concatenate(patches[pair : pair + 2], 1)
        line = dot(table_ref[: 2 * HALF], jnp.concatenate([both, both], 0))
        lines += [line[:, :EXTENT], line[:, EXTENT:]]
    high, low = split(jnp.concatenate(lines, 0))
    product = dot(jnp.concatenate([high, low, high], 1), table_ref[2 * HALF :])
    result = []
    for k in range(len(patches)):
        a = product[2 * HALF * k : 2 * HALF * k + HALF]
        b = product[2 * HALF * k + HALF : 2 * HALF * (k + 1)]
        result.append((a[:, :EXTENT] - b[:, EXTENT:], -(a[:, EXTENT:] + b[:, :EXTENT])))
    return result


def energy(ref):
    rows = []
    for n in range(ref.shape[0]):
        value = ref[n].astype(F32)
        rows.append(jnp.sum(value * value, axis=0, keepdims=True))
    total = jnp.sum(jnp.concatenate(rows, 0), axis=1, keepdims=True)
    return total * (1.0 / (EXTENT * EXTENT))


def own_kernel(now_ref, table_ref, spectrum_ref, energy_ref):
    shape = (HALF, EXTENT)
    row = lax.broadcasted_iota(jnp.int32, shape, 0)
    mean = (row == 0) & (lax.broadcasted_iota(jnp.int32, shape, 1) == 0)
    for pair in range(0, now_ref.shape[0], 2):
        for k, (real, imag) in enumerate(spectra([now_ref[pair], now_ref[pair + 1]], table_ref)):
            real, imag = jnp.where(mean, 0.0, real), jnp.where(mean, 0.0, imag)
            spectrum_ref[pair + k, :, :EXTENT] = real
            spectrum_ref[pair + k, :, EXTENT:] = imag
    energy_ref[...] = jnp.broadcast_to(energy(now_ref), energy_ref.shape)


def write_names(owner, route_ref, name_ref):
    slots = name_ref.shape[0]
    tile_count = route_ref.shape[1] // slots
    height = EXTENT // SHARE // tile_count
    lane = lax.broadcasted_iota(jnp.int32, (slots, tile_count * slots), 1)
    slot = lax.broadcasted_iota(jnp.int32, (slots, tile_count * slots), 0)
    names = jnp.broadcast_to(route_ref[...], lane.shape).astype(F32)
    place = lax.broadcasted_iota(jnp.int32, (slots, EXTENT), 1)
    here = place // (tile_count * height) == (owner & (SHARE - 1))
    row = jnp.zeros((slots, EXTENT), F32)
    for t in range(tile_count):
        own = jnp.sum(jnp.where(lane == slot + t * slots, names, 0.0), axis=1, keepdims=True)
        row = jnp.where(here & (place // height % tile_count == t), own, row)
    for p in range(slots):
        name_ref[p] = jnp.broadcast_to(row[p : p + 1], (8, EXTENT)).astype(BF)


def flow_kernel(place_ref, peak_ref, route_ref, low_ref, spectrum_ref, energy_ref, table_ref, inverse_ref, out_ref, name_ref):
    count = low_ref.shape[0]
    write_names(place_ref[:, :1], route_ref, name_ref)
    crosses = []
    for n, (lr, li) in enumerate(spectra([low_ref[n] for n in range(count)], table_ref)):
        nr = spectrum_ref[n, :, :EXTENT]
        ni = spectrum_ref[n, :, EXTENT:]
        crosses.append(jnp.concatenate([nr * lr + ni * li, ni * lr - nr * li], 1))
    third = 6 * EXTENT
    fourth = jnp.concatenate(
        [
            inverse_ref[third : third + 2 * REACH],
            inverse_ref[third + 2 * REACH :, : 6 * HALF - 2 * EXTENT],
        ],
        1,
    )
    high, low = split(jnp.concatenate(crosses, 0))
    outer = dot(jnp.concatenate([high, low, high], 1), inverse_ref[:third])
    correlations = []
    for pair in range(0, count, 2):
        columns = []
        for n in (pair, pair + 1):
            block = outer[HALF * n : HALF * (n + 1)]
            columns.append(jnp.concatenate([block[:, :EXTENT], block[:, EXTENT:]], 0))
        high, low = split(jnp.concatenate(columns, 1))
        result = dot(fourth, jnp.concatenate([high, low, high], 0))
        correlations += [result[:, :EXTENT], result[:, EXTENT:]]

    scale = (SCORE_GAIN / EXTENT) / jnp.sqrt(energy_ref[:, :1] * energy(low_ref) + EPSILON)
    shape = (2 * REACH, EXTENT)
    row = lax.broadcasted_iota(jnp.int32, shape, 0) - REACH
    column = lax.broadcasted_iota(jnp.int32, shape, 1)
    scores, relatives, tops = [], [], []
    for n in range(count):
        rel_y = row - peak_ref[0:1, n : n + 1]
        rel_x = ((column - peak_ref[1:2, n : n + 1] + EXTENT // 2) & (EXTENT - 1)) - EXTENT // 2
        quarter = EXTENT // 4
        inside = (rel_y >= -quarter) & (rel_y < quarter) & (rel_x >= -quarter) & (rel_x < quarter)
        score = jnp.where(inside, correlations[n] * scale[n : n + 1], -1e30)
        scores.append(score)
        relatives.append((rel_y.astype(F32), rel_x[:1].astype(F32)))
        tops.append(jnp.max(score, axis=0, keepdims=True))
    top = jnp.max(jnp.concatenate(tops, 0), axis=1, keepdims=True)
    sums, sums_y, sums_x = [], [], []
    for n in range(count):
        weight = jnp.exp(scores[n] - top[n : n + 1])
        rel_y, rel_x = relatives[n]
        along = jnp.sum(weight, axis=0, keepdims=True)
        sums.append(along)
        sums_y.append(jnp.sum(weight * rel_y, axis=0, keepdims=True))
        sums_x.append(along * rel_x)
    total, total_y, total_x = (
        jnp.sum(jnp.concatenate(s, 0), axis=1, keepdims=True) for s in (sums, sums_y, sums_x)
    )
    node = lax.broadcasted_iota(jnp.int32, (count, EXTENT), 0)
    lane = lax.broadcasted_iota(jnp.int32, (count, EXTENT), 1)
    peak_y = jnp.zeros((count, EXTENT), jnp.int32)
    peak_x = jnp.zeros((count, EXTENT), jnp.int32)
    for n in range(count):
        peak_y = jnp.where(node == n, peak_ref[0:1, n : n + 1], peak_y)
        peak_x = jnp.where(node == n, peak_ref[1:2, n : n + 1], peak_x)
    flow_y = peak_y.astype(F32) + total_y / total
    flow_x = peak_x.astype(F32) + total_x / total
    flow = jnp.where(lane == node, flow_y, jnp.where(lane == node + count, flow_x, 0.0))
    flow = jnp.sum(flow, axis=0, keepdims=True)
    out_ref[...] = jnp.broadcast_to(flow[None], out_ref.shape)


def fill_band(target_ref, residual, offset, sub_sign):
    block = EXTENT
    lane = lax.broadcasted_iota(jnp.int32, (1, block), 1)
    tap = (lane - BAND).astype(F32) - residual
    raw = jnp.where(lane <= 2 * BAND, 1.0 / (1.0 + tap * tap), 0.0)
    norm = jnp.sum(raw, axis=1, keepdims=True)
    a = lax.broadcasted_iota(jnp.int32, (block, block), 0)
    b = lax.broadcasted_iota(jnp.int32, (block, block), 1)
    d = sub_sign * (a - b) - offset
    k = ((d + block // 2) & (block - 1)) - block // 2
    away = k.astype(F32) - residual
    value = (1.0 / (1.0 + away * away)) / norm
    blocks = {}
    for step in (-1, 0, 1):
        near = jnp.abs(d + sub_sign * step * block) <= BAND
        blocks[step] = jnp.where(near, value, 0.0).astype(BF)
    zero = jnp.zeros((block, block), BF)
    count = target_ref.shape[0] // block
    for i in range(count):
        for j in range(count):
            target_ref[i * block : (i + 1) * block, j * block : (j + 1) * block] = blocks.get(
                i - j, zero
            )


def render_kernel(band_ref, map_ref, flow_ref, name_ref, tile_ref, position_ref, send_ref, *scratch):
    tile_count, edge, _ = tile_ref.shape
    slots = send_ref.shape[0]
    section = lax.axis_index("gz")
    second_core = section % 2 == 1

    def slot_of(p):
        return jnp.where(second_core, p % WIDE * (slots // WIDE) + p // WIDE, p)

    lanes = lax.broadcasted_iota(jnp.int32, map_ref.shape, 1)
    weights = jnp.sum(jnp.where(lanes == section, map_ref[...], 0.0), axis=1, keepdims=True)
    position = jnp.sum(weights * flow_ref[:, 0, :], axis=0, keepdims=True)
    nodes = position_ref.shape[1]
    for c in range(2):
        position_ref[c : c + 1, :] = position[:, c * nodes : (c + 1) * nodes]
    per_tile = nodes // tile_count
    lanes = lax.broadcasted_iota(jnp.int32, position.shape, 1)
    height = edge // slots
    columns = edge // EXTENT
    chunk = EXTENT
    chunks = edge // chunk

    def fill(t, c, target_ref, sub_sign):
        offset = band_ref[t : t + 1, c : c + 1]
        here = lanes // per_tile == c * tile_count + t
        total = jnp.sum(jnp.where(here, position, 0.0), axis=1, keepdims=True)
        shift = total * (MIP_SCALE / per_tile)
        fill_band(target_ref, shift - offset.astype(F32), offset, sub_sign)

    def first(t, c):
        col_ref, _, pass_ref = scratch[3 * t : 3 * t + 3]
        rows = slice(c * chunk, (c + 1) * chunk)
        pass_ref[rows, :] = dot(tile_ref[t, rows, :], col_ref[...]).astype(BF)

    def second(t, c):
        _, row_ref, pass_ref = scratch[3 * t : 3 * t + 3]
        near = range(max(c - 1, 0), min(c + 2, chunks))
        from_row = near[0] * chunk // (edge // 2) * (edge // 2)
        to_row = edge // 2 if near[-1] * chunk < edge // 2 else edge
        rows = slice(c * chunk, (c + 1) * chunk)
        done = dot(row_ref[rows, from_row:to_row], pass_ref[from_row:to_row, :]).astype(BF)
        each = chunk // height
        done = done.reshape(each, height, edge)
        for p in range(each):
            for j in range(columns):
                at = (t * columns + j) * height
                send_ref[slot_of(c * each + p), at : at + height, :] = done[
                    p, :, j * EXTENT : (j + 1) * EXTENT
                ]

    tail = tile_count * columns * height
    fill(0, 1, scratch[0], 1)
    for t in range(tile_count):
        for c in range(chunks):
            first(t, c)
            if c == 0:
                fill(t, 0, scratch[3 * t + 1], -1)
            if c == 1 and t + 1 < tile_count:
                fill(t + 1, 1, scratch[3 * t + 3], 1)
            if t > 0:
                second(t - 1, c)
    for c in range(chunks):
        second(tile_count - 1, c)
        for p in range(c * slots // chunks, (c + 1) * slots // chunks):
            send_ref[slot_of(p), tail:, :] = name_ref[p]


def gather_kernel(piece_ref, out_ref, data_ref):
    owners, rows, _ = piece_ref.shape
    _, out_rows, edge = out_ref.shape
    height = edge // owners
    columns = edge // EXTENT
    tail = rows - 8
    tile_count = tail // (columns * height)
    part = EXTENT // SHARE // tile_count
    parts = height // part
    depth = owners * tile_count * part
    for d in range(owners):
        for j in range(columns):
            pieces = []
            for t in range(tile_count):
                at = (t * columns + j) * height
                pieces.append(piece_ref[d, at : at + height, :].astype(F32))
            for k in range(parts):
                at = k * depth + d * tile_count * part
                data_ref[at : at + tile_count * part, j * EXTENT : (j + 1) * EXTENT] = (
                    jnp.concatenate([p[k * part : (k + 1) * part] for p in pieces], 0).astype(BF)
                )
    lane = lax.broadcasted_iota(jnp.int32, (EXTENT, EXTENT), 1)
    sub = lax.broadcasted_iota(jnp.int32, (EXTENT, EXTENT), 0)
    same = lane % part == sub % part
    names = [
        sum(piece_ref[d, tail : tail + 8, :].astype(F32) for d in range(start, start + SHARE))[0:1]
        for start in range(0, owners, SHARE)
    ]
    each = EXTENT // part
    for c in range(owners * out_rows // height // each):
        group = (sub // part + c * each).astype(F32)
        hits = [jnp.where(same & (name == group), 1.0, 0.0) for name in names]
        count = jnp.sum(sum(hits), axis=1, keepdims=True)
        scale = 1.0 / jnp.maximum(count, 1.0)
        pick = jnp.concatenate([hit.astype(BF) for hit in hits], 1)
        totals = [
            (dot(pick, data_ref[k * depth : (k + 1) * depth]) * scale).reshape(each, part, edge)
            for k in range(parts)
        ]
        total = jnp.concatenate(totals, 1).astype(BF)
        first, last = c * each * height // out_rows, (c + 1) * each * height // out_rows
        out_ref[first:last] = total.reshape(last - first, out_rows, edge)


def place_kernel(position_ref, cell_ref, moved_ref, out_ref, arrived):
    height = out_ref.shape[2]
    copies = [
        pltpu.make_async_copy(
            cell_ref.at[:, g * height : (g + 1) * height, :], out_ref.at[g], arrived.at[g]
        )
        for g in range(out_ref.shape[0])
    ]
    copies.append(pltpu.make_async_copy(position_ref, moved_ref, arrived.at[len(copies)]))
    for copy in copies:
        copy.start()
    for copy in copies:
        copy.wait()


def in_vmem():
    return pl.BlockSpec(memory_space=pltpu.VMEM)


def in_smem():
    return pl.BlockSpec(memory_space=pltpu.SMEM)


def params():
    return pltpu.CompilerParams(vmem_limit_bytes=40 * 1024 * 1024)


def exchange(value, axis, groups=None):
    return lax.all_to_all(
        value, axis, split_axis=0, concat_axis=0, tiled=True, axis_index_groups=groups
    )


def exchange_x_then_z(value):
    owners, rows, lanes = value.shape
    high = owners // WIDE
    along_x = [[z * WIDE + x for x in range(WIDE)] for z in range(high)]
    along_z = [[z * WIDE + x for z in range(high)] for x in range(WIDE)]
    value = exchange(value.reshape(WIDE, high * rows, lanes), "xy", along_x)
    value = value.reshape(WIDE, high, rows, lanes).transpose(1, 0, 2, 3)
    value = exchange(value.reshape(high, WIDE * rows, lanes), "xy", along_z)
    return value.reshape(owners, rows, lanes)


def body(patches, peak_offsets, tiles, band_offsets, routes):
    sections = lax.axis_size("gz")
    owners = lax.axis_size("xy")
    tile_count, edge = tiles.shape[1], tiles.shape[-1]
    height = edge // PIECES
    share = 2
    count = patches.shape[1]

    section = lax.axis_index("gz")
    below = lax.ppermute(patches, "gz", [(i, i + 1) for i in range(sections - 1)])
    early_table, late_table = (jnp.asarray(t) for t in dft_constants())
    second_core = section % 2 == 1
    place = jnp.stack([lax.axis_index("xy"), second_core.astype(jnp.int32)])[None]
    spectrum, power = pl.pallas_call(
        own_kernel,
        out_shape=(
            jax.ShapeDtypeStruct((count, HALF, 2 * EXTENT), F32),
            jax.ShapeDtypeStruct((count, EXTENT), F32),
        ),
        in_specs=[in_vmem()] * 2,
        out_specs=(in_vmem(),) * 2,
        compiler_params=params(),
        cost_estimate=pl.CostEstimate(flops=10**9, bytes_accessed=2**20, transcendentals=0),
        name="own",
    )(patches[0], early_table)
    flow, names = pl.pallas_call(
        flow_kernel,
        out_shape=(
            jax.ShapeDtypeStruct((sections, 1, EXTENT), F32),
            jax.ShapeDtypeStruct((PIECES, 8, EXTENT), BF),
        ),
        in_specs=[in_vmem()] * 8,
        out_specs=(in_vmem(),) * 2,
        compiler_params=params(),
        name="flow",
    )(place, peak_offsets[0].T, routes[0].T, below[0], spectrum, power, early_table, late_table)
    flow = exchange(flow, "gz")

    position, pieces = pl.pallas_call(
        render_kernel,
        out_shape=(
            jax.ShapeDtypeStruct((2, count), F32),
            jax.ShapeDtypeStruct((PIECES, tile_count * height * edge // EXTENT + 8, EXTENT), BF),
        ),
        in_specs=[in_vmem()] * 5,
        out_specs=(in_vmem(), in_vmem()),
        scratch_shapes=[pltpu.VMEM((edge, edge), BF)] * (3 * tile_count),
        compiler_params=params(),
        name="render",
    )(band_offsets[0], jnp.asarray(relaxation_map(sections).T), flow, names, tiles[0])
    pieces = lax.cond(
        second_core,
        exchange_x_then_z,
        lambda value: exchange(value, "xy"),
        pieces,
    )

    cells = pl.pallas_call(
        gather_kernel,
        out_shape=jax.ShapeDtypeStruct((owners, share * height, edge), BF),
        in_specs=[in_vmem()],
        out_specs=in_vmem(),
        scratch_shapes=[pltpu.VMEM((owners * tile_count * height, edge), BF)],
        compiler_params=params(),
        name="gather",
    )(pieces)
    cells = exchange(cells, "xy")
    position, rendered = pl.pallas_call(
        place_kernel,
        out_shape=(
            jax.ShapeDtypeStruct(position.shape, F32),
            jax.ShapeDtypeStruct((share, PIECES, height, edge), BF),
        ),
        in_specs=[in_vmem()] * 2,
        out_specs=(pl.BlockSpec(memory_space=pl.ANY),) * 2,
        scratch_shapes=[pltpu.SemaphoreType.DMA((share + 1,))],
        compiler_params=params(),
        name="place",
    )(position, cells)
    rendered = rendered.reshape(1, share, edge, edge)
    return position[None], rendered


def solution(mesh):
    placed = (
        P("gz", "xy", None, None),
        P("gz", "xy", None),
        P("gz", "xy", None, None),
        P("gz", "xy", None),
        P("gz", "xy", None),
    )
    return jax.shard_map(
        body,
        mesh=mesh,
        in_specs=placed,
        out_specs=(P("gz", None, "xy"), P("gz", "xy", None, None)),
        check_vma=False,
    )
```

```python
import jax
import jax.numpy as jnp
import numpy as np
from jax import lax
from jax.experimental import pallas as pl
from jax.experimental.pallas import tpu as pltpu
from jax.sharding import PartitionSpec as P

PIECES = 32
WIDE = 4
SHARE = 8
BAND = 6
RELAX = 3
EPSILON = 1e-06
STEP_SIZE = 0.25
ANCHOR_WEIGHT = 0.5
MIP_SCALE = 0.0625
SCORE_GAIN = 6.0

EXTENT = 128
HALF = 72
REACH = 40
BF = jnp.bfloat16
F32 = jnp.float32


def high_low(table):
    high = table.astype(jnp.bfloat16)
    low = (table - high.astype(np.float64)).astype(jnp.bfloat16)
    return high, low


def dft_constants():
    line = np.arange(EXTENT)
    phase = 2.0 * np.pi * ((line[:, None] * line[None, :]) % EXTENT) / EXTENT
    cos, sin = np.cos(phase), np.sin(phase)
    first = np.concatenate([cos[:HALF], sin[:HALF]], 0)
    first = np.concatenate(high_low(first), 1)
    second_high, second_low = high_low(np.concatenate([cos, sin], 1))
    second = np.concatenate([second_high, second_high, second_low], 0)
    third_high, third_low = high_low(np.block([[cos, sin], [-sin, cos]]))
    third = np.concatenate([third_high, third_high, third_low], 0)
    weight = np.where(line[:HALF] <= EXTENT // 2, 2.0, 0.0)
    weight[0] = weight[EXTENT // 2] = 1.0
    rows = (np.arange(-REACH, REACH) % EXTENT)[:, None]
    angle = 2.0 * np.pi * ((rows * line[None, :HALF]) % EXTENT) / EXTENT
    fourth = np.concatenate([weight * np.cos(angle), -weight * np.sin(angle)], 1)
    fourth_high, fourth_low = high_low(fourth / float(EXTENT * EXTENT))
    fourth = np.concatenate([fourth_high, fourth_high, fourth_low], 1)
    fourth = np.pad(fourth, ((0, 0), (0, 4 * EXTENT - fourth.shape[1])))
    early = np.concatenate([first, second], 0)
    late = np.concatenate([third, fourth[:, : 2 * EXTENT], fourth[:, 2 * EXTENT :]], 0)
    return early, late


def relaxation_map(sections):
    flow = np.eye(sections)
    positions = np.tril(np.ones((sections, sections)))
    for _ in range(RELAX):
        lower = np.zeros_like(positions)
        upper = np.zeros_like(positions)
        lower[1:] = positions[:-1] + flow[1:] - positions[1:]
        upper[:-1] = positions[1:] - flow[1:] - positions[:-1]
        positions = positions + STEP_SIZE * (lower + upper - ANCHOR_WEIGHT * positions)
    return positions.astype(np.float32)


def split(value):
    high = value.astype(BF)
    return high, (value - high.astype(F32)).astype(BF)


def dot(a, b):
    return jnp.dot(a, b, preferred_element_type=F32)


def spectra(patches, table_ref):
    lines = []
    for pair in range(0, len(patches), 2):
        both = jnp.concatenate(patches[pair : pair + 2], 1)
        line = dot(table_ref[: 2 * HALF], jnp.concatenate([both, both], 0))
        lines += [line[:, :EXTENT], line[:, EXTENT:]]
    high, low = split(jnp.concatenate(lines, 0))
    product = dot(jnp.concatenate([high, low, high], 1), table_ref[2 * HALF :])
    result = []
    for k in range(len(patches)):
        a = product[2 * HALF * k : 2 * HALF * k + HALF]
        b = product[2 * HALF * k + HALF : 2 * HALF * (k + 1)]
        result.append((a[:, :EXTENT] - b[:, EXTENT:], -(a[:, EXTENT:] + b[:, :EXTENT])))
    return result


def energy(ref):
    rows = []
    for n in range(ref.shape[0]):
        value = ref[n].astype(F32)
        rows.append(jnp.sum(value * value, axis=0, keepdims=True))
    total = jnp.sum(jnp.concatenate(rows, 0), axis=1, keepdims=True)
    return total * (1.0 / (EXTENT * EXTENT))


def own_kernel(now_ref, table_ref, spectrum_ref, energy_ref):
    shape = (HALF, EXTENT)
    row = lax.broadcasted_iota(jnp.int32, shape, 0)
    mean = (row == 0) & (lax.broadcasted_iota(jnp.int32, shape, 1) == 0)
    for pair in range(0, now_ref.shape[0], 2):
        for k, (real, imag) in enumerate(spectra([now_ref[pair], now_ref[pair + 1]], table_ref)):
            real, imag = jnp.where(mean, 0.0, real), jnp.where(mean, 0.0, imag)
            spectrum_ref[pair + k, :, :EXTENT] = real
            spectrum_ref[pair + k, :, EXTENT:] = imag
    energy_ref[...] = jnp.broadcast_to(energy(now_ref), energy_ref.shape)


def write_names(owner, route_ref, name_ref):
    slots = name_ref.shape[0]
    tile_count = route_ref.shape[1] // slots
    height = EXTENT // SHARE // tile_count
    lane = lax.broadcasted_iota(jnp.int32, (slots, tile_count * slots), 1)
    slot = lax.broadcasted_iota(jnp.int32, (slots, tile_count * slots), 0)
    names = jnp.broadcast_to(route_ref[...], lane.shape).astype(F32)
    place = lax.broadcasted_iota(jnp.int32, (slots, EXTENT), 1)
    here = place // (tile_count * height) == (owner & (SHARE - 1))
    row = jnp.zeros((slots, EXTENT), F32)
    for t in range(tile_count):
        own = jnp.sum(jnp.where(lane == slot + t * slots, names, 0.0), axis=1, keepdims=True)
        row = jnp.where(here & (place // height % tile_count == t), own, row)
    for p in range(slots):
        name_ref[p] = jnp.broadcast_to(row[p : p + 1], (8, EXTENT)).astype(BF)


def flow_kernel(place_ref, peak_ref, route_ref, low_ref, spectrum_ref, energy_ref, table_ref, inverse_ref, out_ref, name_ref):
    count = low_ref.shape[0]
    write_names(place_ref[:, :1], route_ref, name_ref)
    crosses = []
    for n, (lr, li) in enumerate(spectra([low_ref[n] for n in range(count)], table_ref)):
        nr = spectrum_ref[n, :, :EXTENT]
        ni = spectrum_ref[n, :, EXTENT:]
        crosses.append(jnp.concatenate([nr * lr + ni * li, ni * lr - nr * li], 1))
    third = 6 * EXTENT
    fourth = jnp.concatenate(
        [
            inverse_ref[third : third + 2 * REACH],
            inverse_ref[third + 2 * REACH :, : 6 * HALF - 2 * EXTENT],
        ],
        1,
    )
    high, low = split(jnp.concatenate(crosses, 0))
    outer = dot(jnp.concatenate([high, low, high], 1), inverse_ref[:third])
    correlations = []
    for pair in range(0, count, 2):
        columns = []
        for n in (pair, pair + 1):
            block = outer[HALF * n : HALF * (n + 1)]
            columns.append(jnp.concatenate([block[:, :EXTENT], block[:, EXTENT:]], 0))
        high, low = split(jnp.concatenate(columns, 1))
        result = dot(fourth, jnp.concatenate([high, low, high], 0))
        correlations += [result[:, :EXTENT], result[:, EXTENT:]]

    scale = (SCORE_GAIN / EXTENT) / jnp.sqrt(energy_ref[:, :1] * energy(low_ref) + EPSILON)
    shape = (2 * REACH, EXTENT)
    row = lax.broadcasted_iota(jnp.int32, shape, 0) - REACH
    column = lax.broadcasted_iota(jnp.int32, shape, 1)
    scores, relatives, tops = [], [], []
    for n in range(count):
        rel_y = row - peak_ref[0:1, n : n + 1]
        rel_x = ((column - peak_ref[1:2, n : n + 1] + EXTENT // 2) & (EXTENT - 1)) - EXTENT // 2
        quarter = EXTENT // 4
        inside = (rel_y >= -quarter) & (rel_y < quarter) & (rel_x >= -quarter) & (rel_x < quarter)
        score = jnp.where(inside, correlations[n] * scale[n : n + 1], -1e30)
        scores.append(score)
        relatives.append((rel_y.astype(F32), rel_x[:1].astype(F32)))
        tops.append(jnp.max(score, axis=0, keepdims=True))
    top = jnp.max(jnp.concatenate(tops, 0), axis=1, keepdims=True)
    sums, sums_y, sums_x = [], [], []
    for n in range(count):
        weight = jnp.exp(scores[n] - top[n : n + 1])
        rel_y, rel_x = relatives[n]
        along = jnp.sum(weight, axis=0, keepdims=True)
        sums.append(along)
        sums_y.append(jnp.sum(weight * rel_y, axis=0, keepdims=True))
        sums_x.append(along * rel_x)
    total, total_y, total_x = (
        jnp.sum(jnp.concatenate(s, 0), axis=1, keepdims=True) for s in (sums, sums_y, sums_x)
    )
    node = lax.broadcasted_iota(jnp.int32, (count, EXTENT), 0)
    lane = lax.broadcasted_iota(jnp.int32, (count, EXTENT), 1)
    peak_y = jnp.zeros((count, EXTENT), jnp.int32)
    peak_x = jnp.zeros((count, EXTENT), jnp.int32)
    for n in range(count):
        peak_y = jnp.where(node == n, peak_ref[0:1, n : n + 1], peak_y)
        peak_x = jnp.where(node == n, peak_ref[1:2, n : n + 1], peak_x)
    flow_y = peak_y.astype(F32) + total_y / total
    flow_x = peak_x.astype(F32) + total_x / total
    flow = jnp.where(lane == node, flow_y, jnp.where(lane == node + count, flow_x, 0.0))
    flow = jnp.sum(flow, axis=0, keepdims=True)
    out_ref[...] = jnp.broadcast_to(flow[None], out_ref.shape)


def fill_band(target_ref, residual, offset, sub_sign):
    block = EXTENT
    lane = lax.broadcasted_iota(jnp.int32, (1, block), 1)
    tap = (lane - BAND).astype(F32) - residual
    raw = jnp.where(lane <= 2 * BAND, 1.0 / (1.0 + tap * tap), 0.0)
    norm = jnp.sum(raw, axis=1, keepdims=True)
    a = lax.broadcasted_iota(jnp.int32, (block, block), 0)
    b = lax.broadcasted_iota(jnp.int32, (block, block), 1)
    d = sub_sign * (a - b) - offset
    k = ((d + block // 2) & (block - 1)) - block // 2
    away = k.astype(F32) - residual
    value = (1.0 / (1.0 + away * away)) / norm
    blocks = {}
    for step in (-1, 0, 1):
        near = jnp.abs(d + sub_sign * step * block) <= BAND
        blocks[step] = jnp.where(near, value, 0.0).astype(BF)
    zero = jnp.zeros((block, block), BF)
    count = target_ref.shape[0] // block
    for i in range(count):
        for j in range(count):
            target_ref[i * block : (i + 1) * block, j * block : (j + 1) * block] = blocks.get(
                i - j, zero
            )


def render_kernel(band_ref, map_ref, flow_ref, name_ref, tile_ref, position_ref, send_ref, *scratch):
    tile_count, edge, _ = tile_ref.shape
    slots = send_ref.shape[0]
    section = lax.axis_index("gz")
    later_core = section % 2 == 0

    def slot_of(p):
        return jnp.where(later_core, p % WIDE * (slots // WIDE) + p // WIDE, p)

    lanes = lax.broadcasted_iota(jnp.int32, map_ref.shape, 1)
    weights = jnp.sum(jnp.where(lanes == section, map_ref[...], 0.0), axis=1, keepdims=True)
    position = jnp.sum(weights * flow_ref[:, 0, :], axis=0, keepdims=True)
    nodes = position_ref.shape[1]
    for c in range(2):
        position_ref[c : c + 1, :] = position[:, c * nodes : (c + 1) * nodes]
    per_tile = nodes // tile_count
    lanes = lax.broadcasted_iota(jnp.int32, position.shape, 1)
    height = edge // slots
    columns = edge // EXTENT
    chunk = EXTENT
    chunks = edge // chunk

    def fill(t, c, target_ref, sub_sign):
        offset = band_ref[t : t + 1, c : c + 1]
        here = lanes // per_tile == c * tile_count + t
        total = jnp.sum(jnp.where(here, position, 0.0), axis=1, keepdims=True)
        shift = total * (MIP_SCALE / per_tile)
        fill_band(target_ref, shift - offset.astype(F32), offset, sub_sign)

    def first(t, c):
        col_ref, _, pass_ref = scratch[3 * t : 3 * t + 3]
        rows = slice(c * chunk, (c + 1) * chunk)
        pass_ref[rows, :] = dot(tile_ref[t, rows, :], col_ref[...]).astype(BF)

    def second(t, c):
        _, row_ref, pass_ref = scratch[3 * t : 3 * t + 3]
        near = range(max(c - 1, 0), min(c + 2, chunks))
        from_row = near[0] * chunk // (edge // 2) * (edge // 2)
        to_row = edge // 2 if near[-1] * chunk < edge // 2 else edge
        rows = slice(c * chunk, (c + 1) * chunk)
        done = dot(row_ref[rows, from_row:to_row], pass_ref[from_row:to_row, :]).astype(BF)
        each = chunk // height
        done = done.reshape(each, height, edge)
        for p in range(each):
            for j in range(columns):
                at = (t * columns + j) * height
                send_ref[slot_of(c * each + p), at : at + height, :] = done[
                    p, :, j * EXTENT : (j + 1) * EXTENT
                ]

    tail = tile_count * columns * height
    fill(0, 1, scratch[0], 1)
    for t in range(tile_count):
        for c in range(chunks):
            first(t, c)
            if c == 0:
                fill(t, 0, scratch[3 * t + 1], -1)
            if c == 1 and t + 1 < tile_count:
                fill(t + 1, 1, scratch[3 * t + 3], 1)
            if t > 0:
                second(t - 1, c)
    for c in range(chunks):
        second(tile_count - 1, c)
        for p in range(c * slots // chunks, (c + 1) * slots // chunks):
            send_ref[slot_of(p), tail:, :] = name_ref[p]


def gather_kernel(piece_ref, out_ref, data_ref):
    owners, rows, _ = piece_ref.shape
    _, out_rows, edge = out_ref.shape
    height = edge // owners
    columns = edge // EXTENT
    tail = rows - 8
    tile_count = tail // (columns * height)
    part = EXTENT // SHARE // tile_count
    parts = height // part
    depth = owners * tile_count * part
    for d in range(owners):
        for j in range(columns):
            pieces = []
            for t in range(tile_count):
                at = (t * columns + j) * height
                pieces.append(piece_ref[d, at : at + height, :].astype(F32))
            for k in range(parts):
                at = k * depth + d * tile_count * part
                data_ref[at : at + tile_count * part, j * EXTENT : (j + 1) * EXTENT] = (
                    jnp.concatenate([p[k * part : (k + 1) * part] for p in pieces], 0).astype(BF)
                )
    lane = lax.broadcasted_iota(jnp.int32, (EXTENT, EXTENT), 1)
    sub = lax.broadcasted_iota(jnp.int32, (EXTENT, EXTENT), 0)
    same = lane % part == sub % part
    names = [
        sum(piece_ref[d, tail : tail + 8, :].astype(F32) for d in range(start, start + SHARE))[0:1]
        for start in range(0, owners, SHARE)
    ]
    each = EXTENT // part
    for c in range(owners * out_rows // height // each):
        group = (sub // part + c * each).astype(F32)
        hits = [jnp.where(same & (name == group), 1.0, 0.0) for name in names]
        count = jnp.sum(sum(hits), axis=1, keepdims=True)
        scale = 1.0 / jnp.maximum(count, 1.0)
        pick = jnp.concatenate([hit.astype(BF) for hit in hits], 1)
        totals = [
            (dot(pick, data_ref[k * depth : (k + 1) * depth]) * scale).reshape(each, part, edge)
            for k in range(parts)
        ]
        total = jnp.concatenate(totals, 1).astype(BF)
        first, last = c * each * height // out_rows, (c + 1) * each * height // out_rows
        out_ref[first:last] = total.reshape(last - first, out_rows, edge)


def place_kernel(position_ref, cell_ref, moved_ref, out_ref, arrived):
    height = out_ref.shape[2]
    copies = [
        pltpu.make_async_copy(
            cell_ref.at[:, g * height : (g + 1) * height, :], out_ref.at[g], arrived.at[g]
        )
        for g in range(out_ref.shape[0])
    ]
    copies.append(pltpu.make_async_copy(position_ref, moved_ref, arrived.at[len(copies)]))
    for copy in copies:
        copy.start()
    for copy in copies:
        copy.wait()


def in_vmem():
    return pl.BlockSpec(memory_space=pltpu.VMEM)


def in_smem():
    return pl.BlockSpec(memory_space=pltpu.SMEM)


def params():
    return pltpu.CompilerParams(vmem_limit_bytes=40 * 1024 * 1024)


def exchange(value, axis, groups=None):
    return lax.all_to_all(
        value, axis, split_axis=0, concat_axis=0, tiled=True, axis_index_groups=groups
    )


def exchange_x_then_z(value):
    owners, rows, lanes = value.shape
    high = owners // WIDE
    along_x = [[z * WIDE + x for x in range(WIDE)] for z in range(high)]
    along_z = [[z * WIDE + x for z in range(high)] for x in range(WIDE)]
    value = exchange(value.reshape(WIDE, high * rows, lanes), "xy", along_x)
    value = value.reshape(WIDE, high, rows, lanes).transpose(1, 0, 2, 3)
    value = exchange(value.reshape(high, WIDE * rows, lanes), "xy", along_z)
    return value.reshape(owners, rows, lanes)


def body(patches, peak_offsets, tiles, band_offsets, routes):
    sections = lax.axis_size("gz")
    owners = lax.axis_size("xy")
    tile_count, edge = tiles.shape[1], tiles.shape[-1]
    height = edge // PIECES
    share = 2
    count = patches.shape[1]

    section = lax.axis_index("gz")
    below = lax.ppermute(patches, "gz", [(i, i + 1) for i in range(sections - 1)])
    early_table, late_table = (jnp.asarray(t) for t in dft_constants())
    later_core = section % 2 == 0
    place = jnp.stack([lax.axis_index("xy"), later_core.astype(jnp.int32)])[None]
    spectrum, power = pl.pallas_call(
        own_kernel,
        out_shape=(
            jax.ShapeDtypeStruct((count, HALF, 2 * EXTENT), F32),
            jax.ShapeDtypeStruct((count, EXTENT), F32),
        ),
        in_specs=[in_vmem()] * 2,
        out_specs=(in_vmem(),) * 2,
        compiler_params=params(),
        cost_estimate=pl.CostEstimate(flops=10**9, bytes_accessed=2**20, transcendentals=0),
        name="own",
    )(patches[0], early_table)
    flow, names = pl.pallas_call(
        flow_kernel,
        out_shape=(
            jax.ShapeDtypeStruct((sections, 1, EXTENT), F32),
            jax.ShapeDtypeStruct((PIECES, 8, EXTENT), BF),
        ),
        in_specs=[in_vmem()] * 8,
        out_specs=(in_vmem(),) * 2,
        compiler_params=params(),
        name="flow",
    )(place, peak_offsets[0].T, routes[0].T, below[0], spectrum, power, early_table, late_table)
    flow = exchange(flow, "gz")

    position, pieces = pl.pallas_call(
        render_kernel,
        out_shape=(
            jax.ShapeDtypeStruct((2, count), F32),
            jax.ShapeDtypeStruct((PIECES, tile_count * height * edge // EXTENT + 8, EXTENT), BF),
        ),
        in_specs=[in_vmem()] * 5,
        out_specs=(in_vmem(), in_vmem()),
        scratch_shapes=[pltpu.VMEM((edge, edge), BF)] * (3 * tile_count),
        compiler_params=params(),
        name="render",
    )(band_offsets[0], jnp.asarray(relaxation_map(sections).T), flow, names, tiles[0])
    pieces = lax.cond(
        later_core,
        exchange_x_then_z,
        lambda value: exchange(value, "xy"),
        pieces,
    )

    cells = pl.pallas_call(
        gather_kernel,
        out_shape=jax.ShapeDtypeStruct((owners, share * height, edge), BF),
        in_specs=[in_vmem()],
        out_specs=in_vmem(),
        scratch_shapes=[pltpu.VMEM((owners * tile_count * height, edge), BF)],
        compiler_params=params(),
        name="gather",
    )(pieces)
    cells = exchange(cells, "xy")
    position, rendered = pl.pallas_call(
        place_kernel,
        out_shape=(
            jax.ShapeDtypeStruct(position.shape, F32),
            jax.ShapeDtypeStruct((share, PIECES, height, edge), BF),
        ),
        in_specs=[in_vmem()] * 2,
        out_specs=(pl.BlockSpec(memory_space=pl.ANY),) * 2,
        scratch_shapes=[pltpu.SemaphoreType.DMA((share + 1,))],
        compiler_params=params(),
        name="place",
    )(position, cells)
    rendered = rendered.reshape(1, share, edge, edge)
    return position[None], rendered


def solution(mesh):
    placed = (
        P("gz", "xy", None, None),
        P("gz", "xy", None),
        P("gz", "xy", None, None),
        P("gz", "xy", None),
        P("gz", "xy", None),
    )
    return jax.shard_map(
        body,
        mesh=mesh,
        in_specs=placed,
        out_specs=(P("gz", None, "xy"), P("gz", "xy", None, None)),
        check_vma=False,
    )
```

```python
import jax
import jax.numpy as jnp
import numpy as np
from jax import lax
from jax.experimental import pallas as pl
from jax.experimental.pallas import tpu as pltpu
from jax.sharding import PartitionSpec as P

PIECES = 32
WIDE = 4
SHARE = 8
BAND = 6
RELAX = 3
EPSILON = 1e-06
STEP_SIZE = 0.25
ANCHOR_WEIGHT = 0.5
MIP_SCALE = 0.0625
SCORE_GAIN = 6.0

EXTENT = 128
HALF = 72
REACH = 40
BF = jnp.bfloat16
F32 = jnp.float32


def high_low(table):
    high = table.astype(jnp.bfloat16)
    low = (table - high.astype(np.float64)).astype(jnp.bfloat16)
    return high, low


def dft_constants():
    line = np.arange(EXTENT)
    phase = 2.0 * np.pi * ((line[:, None] * line[None, :]) % EXTENT) / EXTENT
    cos, sin = np.cos(phase), np.sin(phase)
    first = np.concatenate([cos[:HALF], sin[:HALF]], 0)
    first = np.concatenate(high_low(first), 1)
    second_high, second_low = high_low(np.concatenate([cos, sin], 1))
    second = np.concatenate([second_high, second_high, second_low], 0)
    third_high, third_low = high_low(np.block([[cos, sin], [-sin, cos]]))
    third = np.concatenate([third_high, third_high, third_low], 0)
    weight = np.where(line[:HALF] <= EXTENT // 2, 2.0, 0.0)
    weight[0] = weight[EXTENT // 2] = 1.0
    rows = (np.arange(-REACH, REACH) % EXTENT)[:, None]
    angle = 2.0 * np.pi * ((rows * line[None, :HALF]) % EXTENT) / EXTENT
    fourth = np.concatenate([weight * np.cos(angle), -weight * np.sin(angle)], 1)
    fourth_high, fourth_low = high_low(fourth / float(EXTENT * EXTENT))
    fourth = np.concatenate([fourth_high, fourth_high, fourth_low], 1)
    fourth = np.pad(fourth, ((0, 0), (0, 4 * EXTENT - fourth.shape[1])))
    early = np.concatenate([first, second], 0)
    late = np.concatenate([third, fourth[:, : 2 * EXTENT], fourth[:, 2 * EXTENT :]], 0)
    return early, late


def relaxation_map(sections):
    flow = np.eye(sections)
    positions = np.tril(np.ones((sections, sections)))
    for _ in range(RELAX):
        lower = np.zeros_like(positions)
        upper = np.zeros_like(positions)
        lower[1:] = positions[:-1] + flow[1:] - positions[1:]
        upper[:-1] = positions[1:] - flow[1:] - positions[:-1]
        positions = positions + STEP_SIZE * (lower + upper - ANCHOR_WEIGHT * positions)
    return positions.astype(np.float32)


def split(value):
    high = value.astype(BF)
    return high, (value - high.astype(F32)).astype(BF)


def dot(a, b):
    return jnp.dot(a, b, preferred_element_type=F32)


def spectra(patches, table_ref):
    lines = []
    for pair in range(0, len(patches), 2):
        both = jnp.concatenate(patches[pair : pair + 2], 1)
        line = dot(table_ref[: 2 * HALF], jnp.concatenate([both, both], 0))
        lines += [line[:, :EXTENT], line[:, EXTENT:]]
    high, low = split(jnp.concatenate(lines, 0))
    product = dot(jnp.concatenate([high, low, high], 1), table_ref[2 * HALF :])
    result = []
    for k in range(len(patches)):
        a = product[2 * HALF * k : 2 * HALF * k + HALF]
        b = product[2 * HALF * k + HALF : 2 * HALF * (k + 1)]
        result.append((a[:, :EXTENT] - b[:, EXTENT:], -(a[:, EXTENT:] + b[:, :EXTENT])))
    return result


def energy(ref):
    rows = []
    for n in range(ref.shape[0]):
        value = ref[n].astype(F32)
        rows.append(jnp.sum(value * value, axis=0, keepdims=True))
    total = jnp.sum(jnp.concatenate(rows, 0), axis=1, keepdims=True)
    return total * (1.0 / (EXTENT * EXTENT))


def own_kernel(now_ref, table_ref, spectrum_ref, energy_ref):
    shape = (HALF, EXTENT)
    row = lax.broadcasted_iota(jnp.int32, shape, 0)
    mean = (row == 0) & (lax.broadcasted_iota(jnp.int32, shape, 1) == 0)
    for pair in range(0, now_ref.shape[0], 2):
        for k, (real, imag) in enumerate(spectra([now_ref[pair], now_ref[pair + 1]], table_ref)):
            real, imag = jnp.where(mean, 0.0, real), jnp.where(mean, 0.0, imag)
            spectrum_ref[pair + k, :, :EXTENT] = real
            spectrum_ref[pair + k, :, EXTENT:] = imag
    energy_ref[...] = jnp.broadcast_to(energy(now_ref), energy_ref.shape)


def write_names(owner, route_ref, name_ref):
    slots = name_ref.shape[0]
    tile_count = route_ref.shape[1] // slots
    height = EXTENT // SHARE // tile_count
    lane = lax.broadcasted_iota(jnp.int32, (slots, tile_count * slots), 1)
    slot = lax.broadcasted_iota(jnp.int32, (slots, tile_count * slots), 0)
    names = jnp.broadcast_to(route_ref[...], lane.shape).astype(F32)
    place = lax.broadcasted_iota(jnp.int32, (slots, EXTENT), 1)
    here = place // (tile_count * height) == (owner & (SHARE - 1))
    row = jnp.zeros((slots, EXTENT), F32)
    for t in range(tile_count):
        own = jnp.sum(jnp.where(lane == slot + t * slots, names, 0.0), axis=1, keepdims=True)
        row = jnp.where(here & (place // height % tile_count == t), own, row)
    for p in range(slots):
        name_ref[p] = jnp.broadcast_to(row[p : p + 1], (8, EXTENT)).astype(BF)


def flow_kernel(place_ref, peak_ref, route_ref, low_ref, spectrum_ref, energy_ref, table_ref, inverse_ref, out_ref, name_ref):
    count = low_ref.shape[0]
    write_names(place_ref[:, :1], route_ref, name_ref)
    crosses = []
    for n, (lr, li) in enumerate(spectra([low_ref[n] for n in range(count)], table_ref)):
        nr = spectrum_ref[n, :, :EXTENT]
        ni = spectrum_ref[n, :, EXTENT:]
        crosses.append(jnp.concatenate([nr * lr + ni * li, ni * lr - nr * li], 1))
    third = 6 * EXTENT
    fourth = jnp.concatenate(
        [
            inverse_ref[third : third + 2 * REACH],
            inverse_ref[third + 2 * REACH :, : 6 * HALF - 2 * EXTENT],
        ],
        1,
    )
    high, low = split(jnp.concatenate(crosses, 0))
    outer = dot(jnp.concatenate([high, low, high], 1), inverse_ref[:third])
    correlations = []
    for pair in range(0, count, 2):
        columns = []
        for n in (pair, pair + 1):
            block = outer[HALF * n : HALF * (n + 1)]
            columns.append(jnp.concatenate([block[:, :EXTENT], block[:, EXTENT:]], 0))
        high, low = split(jnp.concatenate(columns, 1))
        result = dot(fourth, jnp.concatenate([high, low, high], 0))
        correlations += [result[:, :EXTENT], result[:, EXTENT:]]

    scale = (SCORE_GAIN / EXTENT) / jnp.sqrt(energy_ref[:, :1] * energy(low_ref) + EPSILON)
    shape = (2 * REACH, EXTENT)
    row = lax.broadcasted_iota(jnp.int32, shape, 0) - REACH
    column = lax.broadcasted_iota(jnp.int32, shape, 1)
    scores, relatives, tops = [], [], []
    for n in range(count):
        rel_y = row - peak_ref[0:1, n : n + 1]
        rel_x = ((column - peak_ref[1:2, n : n + 1] + EXTENT // 2) & (EXTENT - 1)) - EXTENT // 2
        quarter = EXTENT // 4
        inside = (rel_y >= -quarter) & (rel_y < quarter) & (rel_x >= -quarter) & (rel_x < quarter)
        score = jnp.where(inside, correlations[n] * scale[n : n + 1], -1e30)
        scores.append(score)
        relatives.append((rel_y.astype(F32), rel_x[:1].astype(F32)))
        tops.append(jnp.max(score, axis=0, keepdims=True))
    top = jnp.max(jnp.concatenate(tops, 0), axis=1, keepdims=True)
    sums, sums_y, sums_x = [], [], []
    for n in range(count):
        weight = jnp.exp(scores[n] - top[n : n + 1])
        rel_y, rel_x = relatives[n]
        along = jnp.sum(weight, axis=0, keepdims=True)
        sums.append(along)
        sums_y.append(jnp.sum(weight * rel_y, axis=0, keepdims=True))
        sums_x.append(along * rel_x)
    total, total_y, total_x = (
        jnp.sum(jnp.concatenate(s, 0), axis=1, keepdims=True) for s in (sums, sums_y, sums_x)
    )
    node = lax.broadcasted_iota(jnp.int32, (count, EXTENT), 0)
    lane = lax.broadcasted_iota(jnp.int32, (count, EXTENT), 1)
    peak_y = jnp.zeros((count, EXTENT), jnp.int32)
    peak_x = jnp.zeros((count, EXTENT), jnp.int32)
    for n in range(count):
        peak_y = jnp.where(node == n, peak_ref[0:1, n : n + 1], peak_y)
        peak_x = jnp.where(node == n, peak_ref[1:2, n : n + 1], peak_x)
    flow_y = peak_y.astype(F32) + total_y / total
    flow_x = peak_x.astype(F32) + total_x / total
    flow = jnp.where(lane == node, flow_y, jnp.where(lane == node + count, flow_x, 0.0))
    flow = jnp.sum(flow, axis=0, keepdims=True)
    out_ref[...] = jnp.broadcast_to(flow[None], out_ref.shape)


def tap_norm(residual):
    lane = lax.broadcasted_iota(jnp.int32, (1, EXTENT), 1)
    away = (lane - BAND).astype(F32) - residual
    raw = jnp.where(lane <= 2 * BAND, 1.0 / (1.0 + away * away), 0.0)
    return jnp.sum(raw, axis=1, keepdims=True)


def fill_columns(target_ref, residual, offset):
    block = EXTENT
    norm = tap_norm(residual)
    a = lax.broadcasted_iota(jnp.int32, (block, block), 0)
    b = lax.broadcasted_iota(jnp.int32, (block, block), 1)
    d = a - b - offset
    k = ((d + block // 2) & (block - 1)) - block // 2
    away = k.astype(F32) - residual
    value = (1.0 / (1.0 + away * away)) / norm
    blocks = {}
    for step in (-1, 0, 1):
        near = jnp.abs(d + step * block) <= BAND
        blocks[step] = jnp.where(near, value, 0.0).astype(BF)
    zero = jnp.zeros((block, block), BF)
    count = target_ref.shape[0] // block
    for i in range(count):
        for j in range(count):
            target_ref[i * block : (i + 1) * block, j * block : (j + 1) * block] = blocks.get(
                i - j, zero
            )


def window_start(chunk_index, chunk, edge):
    return min(max(chunk_index * chunk - chunk // 2, 0), edge - 2 * chunk)


def fill_rows(target_ref, residual, offset):
    chunk = target_ref.shape[1] // 2
    edge = target_ref.shape[0]
    norm = tap_norm(residual)
    a = lax.broadcasted_iota(jnp.int32, (chunk, chunk), 0)
    b = lax.broadcasted_iota(jnp.int32, (chunk, chunk), 1)
    made = {}
    for c in range(edge // chunk):
        step = window_start(c, chunk, edge) - c * chunk
        if step not in made:
            d = b - a - offset + step
            k = ((d + chunk // 2) & (chunk - 1)) - chunk // 2
            away = k.astype(F32) - residual
            value = (1.0 / (1.0 + away * away)) / norm
            made[step] = [
                jnp.where(jnp.abs(d + j * chunk) <= BAND, value, 0.0).astype(BF) for j in range(2)
            ]
        for j in range(2):
            target_ref[c * chunk : (c + 1) * chunk, j * chunk : (j + 1) * chunk] = made[step][j]


def render_kernel(band_ref, map_ref, flow_ref, name_ref, tile_ref, position_ref, send_ref, *scratch):
    tile_count, edge, _ = tile_ref.shape
    slots = send_ref.shape[0]
    section = lax.axis_index("gz")
    second_core = section % 2 == 1

    def slot_of(p):
        return jnp.where(second_core, p % WIDE * (slots // WIDE) + p // WIDE, p)

    lanes = lax.broadcasted_iota(jnp.int32, map_ref.shape, 1)
    weights = jnp.sum(jnp.where(lanes == section, map_ref[...], 0.0), axis=1, keepdims=True)
    position = jnp.sum(weights * flow_ref[:, 0, :], axis=0, keepdims=True)
    nodes = position_ref.shape[1]
    for c in range(2):
        position_ref[c : c + 1, :] = position[:, c * nodes : (c + 1) * nodes]
    per_tile = nodes // tile_count
    lanes = lax.broadcasted_iota(jnp.int32, position.shape, 1)
    height = edge // slots
    columns = edge // EXTENT
    chunk = EXTENT
    chunks = edge // chunk

    def fill(t, c, target_ref):
        offset = band_ref[t : t + 1, c : c + 1]
        here = lanes // per_tile == c * tile_count + t
        total = jnp.sum(jnp.where(here, position, 0.0), axis=1, keepdims=True)
        shift = total * (MIP_SCALE / per_tile)
        (fill_rows, fill_columns)[c](target_ref, shift - offset.astype(F32), offset)

    def first(t, c):
        col_ref, _, pass_ref = scratch[3 * t : 3 * t + 3]
        rows = slice(c * chunk, (c + 1) * chunk)
        pass_ref[rows, :] = dot(tile_ref[t, rows, :], col_ref[...]).astype(BF)

    def second(t, c):
        _, row_ref, pass_ref = scratch[3 * t : 3 * t + 3]
        start = window_start(c, chunk, edge)
        done = dot(row_ref[c * chunk : (c + 1) * chunk, :], pass_ref[start : start + 2 * chunk, :]).astype(BF)
        each = chunk // height
        done = done.reshape(each, height, edge)
        for p in range(each):
            for j in range(columns):
                at = (t * columns + j) * height
                send_ref[slot_of(c * each + p), at : at + height, :] = done[
                    p, :, j * EXTENT : (j + 1) * EXTENT
                ]

    tail = tile_count * columns * height
    fill(0, 1, scratch[0])
    for t in range(tile_count):
        for c in range(chunks):
            first(t, c)
            if c == 0:
                fill(t, 0, scratch[3 * t + 1])
            if c == 1 and t + 1 < tile_count:
                fill(t + 1, 1, scratch[3 * t + 3])
            if t > 0:
                second(t - 1, c)
    for c in range(chunks):
        second(tile_count - 1, c)
        for p in range(c * slots // chunks, (c + 1) * slots // chunks):
            send_ref[slot_of(p), tail:, :] = name_ref[p]


def gather_kernel(piece_ref, out_ref, data_ref):
    owners, rows, _ = piece_ref.shape
    _, out_rows, edge = out_ref.shape
    height = edge // owners
    columns = edge // EXTENT
    tail = rows - 8
    tile_count = tail // (columns * height)
    part = EXTENT // SHARE // tile_count
    parts = height // part
    depth = owners * tile_count * part
    for d in range(owners):
        for j in range(columns):
            pieces = []
            for t in range(tile_count):
                at = (t * columns + j) * height
                pieces.append(piece_ref[d, at : at + height, :].astype(F32))
            for k in range(parts):
                at = k * depth + d * tile_count * part
                data_ref[at : at + tile_count * part, j * EXTENT : (j + 1) * EXTENT] = (
                    jnp.concatenate([p[k * part : (k + 1) * part] for p in pieces], 0).astype(BF)
                )
    lane = lax.broadcasted_iota(jnp.int32, (EXTENT, EXTENT), 1)
    sub = lax.broadcasted_iota(jnp.int32, (EXTENT, EXTENT), 0)
    same = lane % part == sub % part
    names = [
        sum(piece_ref[d, tail : tail + 8, :].astype(F32) for d in range(start, start + SHARE))[0:1]
        for start in range(0, owners, SHARE)
    ]
    each = EXTENT // part
    for c in range(owners * out_rows // height // each):
        group = (sub // part + c * each).astype(F32)
        hits = [jnp.where(same & (name == group), 1.0, 0.0) for name in names]
        count = jnp.sum(sum(hits), axis=1, keepdims=True)
        scale = 1.0 / jnp.maximum(count, 1.0)
        pick = jnp.concatenate([hit.astype(BF) for hit in hits], 1)
        totals = [
            (dot(pick, data_ref[k * depth : (k + 1) * depth]) * scale).reshape(each, part, edge)
            for k in range(parts)
        ]
        total = jnp.concatenate(totals, 1).astype(BF)
        first, last = c * each * height // out_rows, (c + 1) * each * height // out_rows
        out_ref[first:last] = total.reshape(last - first, out_rows, edge)


def place_kernel(position_ref, cell_ref, moved_ref, out_ref, arrived):
    height = out_ref.shape[2]
    copies = [
        pltpu.make_async_copy(
            cell_ref.at[:, g * height : (g + 1) * height, :], out_ref.at[g], arrived.at[g]
        )
        for g in range(out_ref.shape[0])
    ]
    copies.append(pltpu.make_async_copy(position_ref, moved_ref, arrived.at[len(copies)]))
    for copy in copies:
        copy.start()
    for copy in copies:
        copy.wait()


def in_vmem():
    return pl.BlockSpec(memory_space=pltpu.VMEM)


def in_smem():
    return pl.BlockSpec(memory_space=pltpu.SMEM)


def params():
    return pltpu.CompilerParams(vmem_limit_bytes=40 * 1024 * 1024)


def exchange(value, axis, groups=None):
    return lax.all_to_all(
        value, axis, split_axis=0, concat_axis=0, tiled=True, axis_index_groups=groups
    )


def exchange_x_then_z(value):
    owners, rows, lanes = value.shape
    high = owners // WIDE
    along_x = [[z * WIDE + x for x in range(WIDE)] for z in range(high)]
    along_z = [[z * WIDE + x for z in range(high)] for x in range(WIDE)]
    value = exchange(value.reshape(WIDE, high * rows, lanes), "xy", along_x)
    value = value.reshape(WIDE, high, rows, lanes).transpose(1, 0, 2, 3)
    value = exchange(value.reshape(high, WIDE * rows, lanes), "xy", along_z)
    return value.reshape(owners, rows, lanes)


def body(patches, peak_offsets, tiles, band_offsets, routes):
    sections = lax.axis_size("gz")
    owners = lax.axis_size("xy")
    tile_count, edge = tiles.shape[1], tiles.shape[-1]
    height = edge // PIECES
    share = 2
    count = patches.shape[1]

    section = lax.axis_index("gz")
    below = lax.ppermute(patches, "gz", [(i, i + 1) for i in range(sections - 1)])
    early_table, late_table = (jnp.asarray(t) for t in dft_constants())
    second_core = section % 2 == 1
    place = jnp.stack([lax.axis_index("xy"), second_core.astype(jnp.int32)])[None]
    spectrum, power = pl.pallas_call(
        own_kernel,
        out_shape=(
            jax.ShapeDtypeStruct((count, HALF, 2 * EXTENT), F32),
            jax.ShapeDtypeStruct((count, EXTENT), F32),
        ),
        in_specs=[in_vmem()] * 2,
        out_specs=(in_vmem(),) * 2,
        compiler_params=params(),
        cost_estimate=pl.CostEstimate(flops=10**9, bytes_accessed=2**20, transcendentals=0),
        name="own",
    )(patches[0], early_table)
    flow, names = pl.pallas_call(
        flow_kernel,
        out_shape=(
            jax.ShapeDtypeStruct((sections, 1, EXTENT), F32),
            jax.ShapeDtypeStruct((PIECES, 8, EXTENT), BF),
        ),
        in_specs=[in_vmem()] * 8,
        out_specs=(in_vmem(),) * 2,
        compiler_params=params(),
        name="flow",
    )(place, peak_offsets[0].T, routes[0].T, below[0], spectrum, power, early_table, late_table)
    flow = exchange(flow, "gz")

    position, pieces = pl.pallas_call(
        render_kernel,
        out_shape=(
            jax.ShapeDtypeStruct((2, count), F32),
            jax.ShapeDtypeStruct((PIECES, tile_count * height * edge // EXTENT + 8, EXTENT), BF),
        ),
        in_specs=[in_vmem()] * 5,
        out_specs=(in_vmem(), in_vmem()),
        scratch_shapes=[
            pltpu.VMEM((edge, width), BF) for width in (edge, 2 * EXTENT, edge) * tile_count
        ],
        compiler_params=params(),
        name="render",
    )(band_offsets[0], jnp.asarray(relaxation_map(sections).T), flow, names, tiles[0])
    pieces = lax.cond(
        second_core,
        exchange_x_then_z,
        lambda value: exchange(value, "xy"),
        pieces,
    )

    cells = pl.pallas_call(
        gather_kernel,
        out_shape=jax.ShapeDtypeStruct((owners, share * height, edge), BF),
        in_specs=[in_vmem()],
        out_specs=in_vmem(),
        scratch_shapes=[pltpu.VMEM((owners * tile_count * height, edge), BF)],
        compiler_params=params(),
        name="gather",
    )(pieces)
    cells = exchange(cells, "xy")
    position, rendered = pl.pallas_call(
        place_kernel,
        out_shape=(
            jax.ShapeDtypeStruct(position.shape, F32),
            jax.ShapeDtypeStruct((share, PIECES, height, edge), BF),
        ),
        in_specs=[in_vmem()] * 2,
        out_specs=(pl.BlockSpec(memory_space=pl.ANY),) * 2,
        scratch_shapes=[pltpu.SemaphoreType.DMA((share + 1,))],
        compiler_params=params(),
        name="place",
    )(position, cells)
    rendered = rendered.reshape(1, share, edge, edge)
    return position[None], rendered


def solution(mesh):
    placed = (
        P("gz", "xy", None, None),
        P("gz", "xy", None),
        P("gz", "xy", None, None),
        P("gz", "xy", None),
        P("gz", "xy", None),
    )
    return jax.shard_map(
        body,
        mesh=mesh,
        in_specs=placed,
        out_specs=(P("gz", None, "xy"), P("gz", "xy", None, None)),
        check_vma=False,
    )
```

```python
import jax
import jax.numpy as jnp
import numpy as np
from jax import lax
from jax.experimental import pallas as pl
from jax.experimental.pallas import tpu as pltpu
from jax.sharding import PartitionSpec as P

PIECES = 32
WIDE = 4
SHARE = 8
BAND = 6
RELAX = 3
EPSILON = 1e-06
STEP_SIZE = 0.25
ANCHOR_WEIGHT = 0.5
MIP_SCALE = 0.0625
SCORE_GAIN = 6.0

EXTENT = 128
HALF = 72
REACH = 40
BF = jnp.bfloat16
F32 = jnp.float32


def high_low(table):
    high = table.astype(jnp.bfloat16)
    low = (table - high.astype(np.float64)).astype(jnp.bfloat16)
    return high, low


def dft_constants():
    line = np.arange(EXTENT)
    phase = 2.0 * np.pi * ((line[:, None] * line[None, :]) % EXTENT) / EXTENT
    cos, sin = np.cos(phase), np.sin(phase)
    first = np.concatenate([cos[:HALF], sin[:HALF]], 0)
    first = np.concatenate(high_low(first), 1)
    second_high, second_low = high_low(np.concatenate([cos, sin], 1))
    second = np.concatenate([second_high, second_high, second_low], 0)
    third_high, third_low = high_low(np.block([[cos, sin], [-sin, cos]]))
    third = np.concatenate([third_high, third_high, third_low], 0)
    weight = np.where(line[:HALF] <= EXTENT // 2, 2.0, 0.0)
    weight[0] = weight[EXTENT // 2] = 1.0
    rows = (np.arange(-REACH, REACH) % EXTENT)[:, None]
    angle = 2.0 * np.pi * ((rows * line[None, :HALF]) % EXTENT) / EXTENT
    fourth = np.concatenate([weight * np.cos(angle), -weight * np.sin(angle)], 1)
    fourth_high, fourth_low = high_low(fourth / float(EXTENT * EXTENT))
    fourth = np.concatenate([fourth_high, fourth_high, fourth_low], 1)
    fourth = np.pad(fourth, ((0, 0), (0, 4 * EXTENT - fourth.shape[1])))
    early = np.concatenate([first, second], 0)
    late = np.concatenate([third, fourth[:, : 2 * EXTENT], fourth[:, 2 * EXTENT :]], 0)
    return early, late


def relaxation_map(sections):
    flow = np.eye(sections)
    positions = np.tril(np.ones((sections, sections)))
    for _ in range(RELAX):
        lower = np.zeros_like(positions)
        upper = np.zeros_like(positions)
        lower[1:] = positions[:-1] + flow[1:] - positions[1:]
        upper[:-1] = positions[1:] - flow[1:] - positions[:-1]
        positions = positions + STEP_SIZE * (lower + upper - ANCHOR_WEIGHT * positions)
    return positions.astype(np.float32)


def split(value):
    high = value.astype(BF)
    return high, (value - high.astype(F32)).astype(BF)


def dot(a, b):
    return jnp.dot(a, b, preferred_element_type=F32)


def spectra(patches, table_ref):
    lines = []
    for pair in range(0, len(patches), 2):
        both = jnp.concatenate(patches[pair : pair + 2], 1)
        line = dot(table_ref[: 2 * HALF], jnp.concatenate([both, both], 0))
        lines += [line[:, :EXTENT], line[:, EXTENT:]]
    high, low = split(jnp.concatenate(lines, 0))
    product = dot(jnp.concatenate([high, low, high], 1), table_ref[2 * HALF :])
    result = []
    for k in range(len(patches)):
        a = product[2 * HALF * k : 2 * HALF * k + HALF]
        b = product[2 * HALF * k + HALF : 2 * HALF * (k + 1)]
        result.append((a[:, :EXTENT] - b[:, EXTENT:], -(a[:, EXTENT:] + b[:, :EXTENT])))
    return result


def energy(ref):
    rows = []
    for n in range(ref.shape[0]):
        value = ref[n].astype(F32)
        rows.append(jnp.sum(value * value, axis=0, keepdims=True))
    total = jnp.sum(jnp.concatenate(rows, 0), axis=1, keepdims=True)
    return total * (1.0 / (EXTENT * EXTENT))


def own_kernel(now_ref, table_ref, spectrum_ref, energy_ref):
    shape = (HALF, EXTENT)
    row = lax.broadcasted_iota(jnp.int32, shape, 0)
    mean = (row == 0) & (lax.broadcasted_iota(jnp.int32, shape, 1) == 0)
    for pair in range(0, now_ref.shape[0], 2):
        for k, (real, imag) in enumerate(spectra([now_ref[pair], now_ref[pair + 1]], table_ref)):
            real, imag = jnp.where(mean, 0.0, real), jnp.where(mean, 0.0, imag)
            spectrum_ref[pair + k, :, :EXTENT] = real
            spectrum_ref[pair + k, :, EXTENT:] = imag
    energy_ref[...] = jnp.broadcast_to(energy(now_ref), energy_ref.shape)


def write_names(owner, route_ref, name_ref):
    slots = name_ref.shape[0]
    tile_count = route_ref.shape[1] // slots
    height = EXTENT // SHARE // tile_count
    lane = lax.broadcasted_iota(jnp.int32, (slots, tile_count * slots), 1)
    slot = lax.broadcasted_iota(jnp.int32, (slots, tile_count * slots), 0)
    names = jnp.broadcast_to(route_ref[...], lane.shape).astype(F32)
    place = lax.broadcasted_iota(jnp.int32, (slots, EXTENT), 1)
    here = place // (tile_count * height) == (owner & (SHARE - 1))
    row = jnp.zeros((slots, EXTENT), F32)
    for t in range(tile_count):
        own = jnp.sum(jnp.where(lane == slot + t * slots, names, 0.0), axis=1, keepdims=True)
        row = jnp.where(here & (place // height % tile_count == t), own, row)
    for p in range(slots):
        name_ref[p] = jnp.broadcast_to(row[p : p + 1], (8, EXTENT)).astype(BF)


def flow_kernel(place_ref, peak_ref, route_ref, low_ref, spectrum_ref, energy_ref, table_ref, inverse_ref, out_ref, name_ref):
    count = low_ref.shape[0]
    write_names(place_ref[:, :1], route_ref, name_ref)
    crosses = []
    for n, (lr, li) in enumerate(spectra([low_ref[n] for n in range(count)], table_ref)):
        nr = spectrum_ref[n, :, :EXTENT]
        ni = spectrum_ref[n, :, EXTENT:]
        crosses.append(jnp.concatenate([nr * lr + ni * li, ni * lr - nr * li], 1))
    third = 6 * EXTENT
    fourth = jnp.concatenate(
        [
            inverse_ref[third : third + 2 * REACH],
            inverse_ref[third + 2 * REACH :, : 6 * HALF - 2 * EXTENT],
        ],
        1,
    )
    high, low = split(jnp.concatenate(crosses, 0))
    outer = dot(jnp.concatenate([high, low, high], 1), inverse_ref[:third])
    correlations = []
    for pair in range(0, count, 2):
        columns = []
        for n in (pair, pair + 1):
            block = outer[HALF * n : HALF * (n + 1)]
            columns.append(jnp.concatenate([block[:, :EXTENT], block[:, EXTENT:]], 0))
        high, low = split(jnp.concatenate(columns, 1))
        result = dot(fourth, jnp.concatenate([high, low, high], 0))
        correlations += [result[:, :EXTENT], result[:, EXTENT:]]

    scale = (SCORE_GAIN / EXTENT) / jnp.sqrt(energy_ref[:, :1] * energy(low_ref) + EPSILON)
    shape = (2 * REACH, EXTENT)
    row = lax.broadcasted_iota(jnp.int32, shape, 0) - REACH
    column = lax.broadcasted_iota(jnp.int32, shape, 1)
    scores, relatives, tops = [], [], []
    for n in range(count):
        rel_y = row - peak_ref[0:1, n : n + 1]
        rel_x = ((column - peak_ref[1:2, n : n + 1] + EXTENT // 2) & (EXTENT - 1)) - EXTENT // 2
        quarter = EXTENT // 4
        inside = (rel_y >= -quarter) & (rel_y < quarter) & (rel_x >= -quarter) & (rel_x < quarter)
        score = jnp.where(inside, correlations[n] * scale[n : n + 1], -1e30)
        scores.append(score)
        relatives.append((rel_y.astype(F32), rel_x[:1].astype(F32)))
        tops.append(jnp.max(score, axis=0, keepdims=True))
    top = jnp.max(jnp.concatenate(tops, 0), axis=1, keepdims=True)
    sums, sums_y, sums_x = [], [], []
    for n in range(count):
        weight = jnp.exp(scores[n] - top[n : n + 1])
        rel_y, rel_x = relatives[n]
        along = jnp.sum(weight, axis=0, keepdims=True)
        sums.append(along)
        sums_y.append(jnp.sum(weight * rel_y, axis=0, keepdims=True))
        sums_x.append(along * rel_x)
    total, total_y, total_x = (
        jnp.sum(jnp.concatenate(s, 0), axis=1, keepdims=True) for s in (sums, sums_y, sums_x)
    )
    node = lax.broadcasted_iota(jnp.int32, (count, EXTENT), 0)
    lane = lax.broadcasted_iota(jnp.int32, (count, EXTENT), 1)
    peak_y = jnp.zeros((count, EXTENT), jnp.int32)
    peak_x = jnp.zeros((count, EXTENT), jnp.int32)
    for n in range(count):
        peak_y = jnp.where(node == n, peak_ref[0:1, n : n + 1], peak_y)
        peak_x = jnp.where(node == n, peak_ref[1:2, n : n + 1], peak_x)
    flow_y = peak_y.astype(F32) + total_y / total
    flow_x = peak_x.astype(F32) + total_x / total
    flow = jnp.where(lane == node, flow_y, jnp.where(lane == node + count, flow_x, 0.0))
    flow = jnp.sum(flow, axis=0, keepdims=True)
    out_ref[...] = jnp.broadcast_to(flow[None], out_ref.shape)


def tap_norm(residual):
    lane = lax.broadcasted_iota(jnp.int32, (1, EXTENT), 1)
    away = (lane - BAND).astype(F32) - residual
    raw = jnp.where(lane <= 2 * BAND, 1.0 / (1.0 + away * away), 0.0)
    return jnp.sum(raw, axis=1, keepdims=True)


def fill_columns(target_ref, residual, offset):
    block = EXTENT
    norm = tap_norm(residual)
    a = lax.broadcasted_iota(jnp.int32, (block, block), 0)
    b = lax.broadcasted_iota(jnp.int32, (block, block), 1)
    d = a - b - offset
    k = ((d + block // 2) & (block - 1)) - block // 2
    away = k.astype(F32) - residual
    value = (1.0 / (1.0 + away * away)) / norm
    blocks = {}
    for step in (-1, 0, 1):
        near = jnp.abs(d + step * block) <= BAND
        blocks[step] = jnp.where(near, value, 0.0).astype(BF)
    zero = jnp.zeros((block, block), BF)
    count = target_ref.shape[0] // block
    for i in range(count):
        for j in range(count):
            target_ref[i * block : (i + 1) * block, j * block : (j + 1) * block] = blocks.get(
                i - j, zero
            )


def window_start(chunk_index, chunk, edge):
    return min(max(chunk_index * chunk - chunk // 2, 0), edge - 2 * chunk)


def fill_rows(target_ref, residual, offset):
    chunk = target_ref.shape[1] // 2
    edge = target_ref.shape[0]
    norm = tap_norm(residual)
    a = lax.broadcasted_iota(jnp.int32, (chunk, chunk), 0)
    b = lax.broadcasted_iota(jnp.int32, (chunk, chunk), 1)
    made = {}
    for c in range(edge // chunk):
        step = window_start(c, chunk, edge) - c * chunk
        if step not in made:
            d = b - a - offset + step
            k = ((d + chunk // 2) & (chunk - 1)) - chunk // 2
            away = k.astype(F32) - residual
            value = (1.0 / (1.0 + away * away)) / norm
            made[step] = [
                jnp.where(jnp.abs(d + j * chunk) <= BAND, value, 0.0).astype(BF) for j in range(2)
            ]
        for j in range(2):
            target_ref[c * chunk : (c + 1) * chunk, j * chunk : (j + 1) * chunk] = made[step][j]


def render_kernel(band_ref, map_ref, flow_ref, name_ref, tile_ref, position_ref, send_ref, *scratch):
    tile_count, edge, _ = tile_ref.shape
    slots = send_ref.shape[0]
    section = lax.axis_index("gz")
    second_core = section % 2 == 1

    def slot_of(p):
        return jnp.where(second_core, p % WIDE * (slots // WIDE) + p // WIDE, p)

    lanes = lax.broadcasted_iota(jnp.int32, map_ref.shape, 1)
    weights = jnp.sum(jnp.where(lanes == section, map_ref[...], 0.0), axis=1, keepdims=True)
    position = jnp.sum(weights * flow_ref[:, 0, :], axis=0, keepdims=True)
    nodes = position_ref.shape[1]
    for c in range(2):
        position_ref[c : c + 1, :] = position[:, c * nodes : (c + 1) * nodes]
    per_tile = nodes // tile_count
    lanes = lax.broadcasted_iota(jnp.int32, position.shape, 1)
    height = edge // slots
    columns = edge // EXTENT
    chunk = EXTENT
    chunks = edge // chunk

    def fill(t, c, target_ref):
        offset = band_ref[t : t + 1, c : c + 1]
        here = lanes // per_tile == c * tile_count + t
        total = jnp.sum(jnp.where(here, position, 0.0), axis=1, keepdims=True)
        shift = total * (MIP_SCALE / per_tile)
        (fill_rows, fill_columns)[c](target_ref, shift - offset.astype(F32), offset)

    def first(t, c):
        col_ref, _, pass_ref = scratch[3 * t : 3 * t + 3]
        rows = slice(c * chunk, (c + 1) * chunk)
        pass_ref[rows, :] = dot(tile_ref[t, rows, :], col_ref[...]).astype(BF)

    def second(t, c):
        _, row_ref, pass_ref = scratch[3 * t : 3 * t + 3]
        start = window_start(c, chunk, edge)
        done = dot(row_ref[c * chunk : (c + 1) * chunk, :], pass_ref[start : start + 2 * chunk, :]).astype(BF)
        each = chunk // height
        done = done.reshape(each, height, edge)
        for p in range(each):
            for j in range(columns):
                at = (t * columns + j) * height
                send_ref[slot_of(c * each + p), at : at + height, :] = done[
                    p, :, j * EXTENT : (j + 1) * EXTENT
                ]

    tail = tile_count * columns * height
    fill(0, 1, scratch[0])
    for t in range(tile_count):
        for c in range(chunks):
            first(t, c)
            if c == 0:
                fill(t, 0, scratch[3 * t + 1])
            if c == 1 and t + 1 < tile_count:
                fill(t + 1, 1, scratch[3 * t + 3])
            if t > 0:
                second(t - 1, c)
    for c in range(chunks):
        second(tile_count - 1, c)
        for p in range(c * slots // chunks, (c + 1) * slots // chunks):
            send_ref[slot_of(p), tail:, :] = name_ref[p]


def gather_kernel(piece_ref, out_ref, data_ref):
    owners, rows, _ = piece_ref.shape
    _, out_rows, edge = out_ref.shape
    height = edge // owners
    columns = edge // EXTENT
    tail = rows - 8
    tile_count = tail // (columns * height)
    part = EXTENT // SHARE // tile_count
    parts = height // part
    depth = owners * tile_count * part
    lane = lax.broadcasted_iota(jnp.int32, (EXTENT, EXTENT), 1)
    sub = lax.broadcasted_iota(jnp.int32, (EXTENT, EXTENT), 0)
    same = lane % part == sub % part
    names = [
        sum(piece_ref[d, tail : tail + 8, :].astype(F32) for d in range(start, start + SHARE))[0:1]
        for start in range(0, owners, SHARE)
    ]
    each = EXTENT // part
    picks = []
    for c in range(owners * out_rows // height // each):
        group = (sub // part + c * each).astype(F32)
        hits = [jnp.where(same & (name == group), 1.0, 0.0) for name in names]
        count = jnp.sum(sum(hits), axis=1, keepdims=True)
        picks.append((jnp.concatenate([hit.astype(BF) for hit in hits], 1), 1.0 / jnp.maximum(count, 1.0)))
    wide = edge // 2
    for side in range(2):
        for d in range(owners):
            for j in range(side * columns // 2, (side + 1) * columns // 2):
                pieces = []
                for t in range(tile_count):
                    at = (t * columns + j) * height
                    pieces.append(piece_ref[d, at : at + height, :].astype(F32))
                for k in range(parts):
                    at = k * depth + d * tile_count * part
                    data_ref[at : at + tile_count * part, j * EXTENT : (j + 1) * EXTENT] = (
                        jnp.concatenate([p[k * part : (k + 1) * part] for p in pieces], 0).astype(BF)
                    )
        lanes = slice(side * wide, (side + 1) * wide)
        for c, (pick, scale) in enumerate(picks):
            totals = [
                (dot(pick, data_ref[k * depth : (k + 1) * depth, lanes]) * scale).reshape(each, part, wide)
                for k in range(parts)
            ]
            total = jnp.concatenate(totals, 1).astype(BF)
            first, last = c * each * height // out_rows, (c + 1) * each * height // out_rows
            out_ref[first:last, :, lanes] = total.reshape(last - first, out_rows, wide)


def place_kernel(position_ref, cell_ref, moved_ref, out_ref, arrived):
    height = out_ref.shape[2]
    copies = [
        pltpu.make_async_copy(
            cell_ref.at[:, g * height : (g + 1) * height, :], out_ref.at[g], arrived.at[g]
        )
        for g in range(out_ref.shape[0])
    ]
    copies.append(pltpu.make_async_copy(position_ref, moved_ref, arrived.at[len(copies)]))
    for copy in copies:
        copy.start()
    for copy in copies:
        copy.wait()


def in_vmem():
    return pl.BlockSpec(memory_space=pltpu.VMEM)


def in_smem():
    return pl.BlockSpec(memory_space=pltpu.SMEM)


def params():
    return pltpu.CompilerParams(vmem_limit_bytes=40 * 1024 * 1024)


def exchange(value, axis, groups=None):
    return lax.all_to_all(
        value, axis, split_axis=0, concat_axis=0, tiled=True, axis_index_groups=groups
    )


def exchange_x_then_z(value):
    owners, rows, lanes = value.shape
    high = owners // WIDE
    along_x = [[z * WIDE + x for x in range(WIDE)] for z in range(high)]
    along_z = [[z * WIDE + x for z in range(high)] for x in range(WIDE)]
    value = exchange(value.reshape(WIDE, high * rows, lanes), "xy", along_x)
    value = value.reshape(WIDE, high, rows, lanes).transpose(1, 0, 2, 3)
    value = exchange(value.reshape(high, WIDE * rows, lanes), "xy", along_z)
    return value.reshape(owners, rows, lanes)


def body(patches, peak_offsets, tiles, band_offsets, routes):
    sections = lax.axis_size("gz")
    owners = lax.axis_size("xy")
    tile_count, edge = tiles.shape[1], tiles.shape[-1]
    height = edge // PIECES
    share = 2
    count = patches.shape[1]

    section = lax.axis_index("gz")
    below = lax.ppermute(patches, "gz", [(i, i + 1) for i in range(sections - 1)])
    early_table, late_table = (jnp.asarray(t) for t in dft_constants())
    second_core = section % 2 == 1
    place = jnp.stack([lax.axis_index("xy"), second_core.astype(jnp.int32)])[None]
    spectrum, power = pl.pallas_call(
        own_kernel,
        out_shape=(
            jax.ShapeDtypeStruct((count, HALF, 2 * EXTENT), F32),
            jax.ShapeDtypeStruct((count, EXTENT), F32),
        ),
        in_specs=[in_vmem()] * 2,
        out_specs=(in_vmem(),) * 2,
        compiler_params=params(),
        cost_estimate=pl.CostEstimate(flops=10**9, bytes_accessed=2**20, transcendentals=0),
        name="own",
    )(patches[0], early_table)
    flow, names = pl.pallas_call(
        flow_kernel,
        out_shape=(
            jax.ShapeDtypeStruct((sections, 1, EXTENT), F32),
            jax.ShapeDtypeStruct((PIECES, 8, EXTENT), BF),
        ),
        in_specs=[in_vmem()] * 8,
        out_specs=(in_vmem(),) * 2,
        compiler_params=params(),
        name="flow",
    )(place, peak_offsets[0].T, routes[0].T, below[0], spectrum, power, early_table, late_table)
    flow = exchange(flow, "gz")

    position, pieces = pl.pallas_call(
        render_kernel,
        out_shape=(
            jax.ShapeDtypeStruct((2, count), F32),
            jax.ShapeDtypeStruct((PIECES, tile_count * height * edge // EXTENT + 8, EXTENT), BF),
        ),
        in_specs=[in_vmem()] * 5,
        out_specs=(in_vmem(), in_vmem()),
        scratch_shapes=[
            pltpu.VMEM((edge, width), BF) for width in (edge, 2 * EXTENT, edge) * tile_count
        ],
        compiler_params=params(),
        name="render",
    )(band_offsets[0], jnp.asarray(relaxation_map(sections).T), flow, names, tiles[0])
    pieces = lax.cond(
        second_core,
        exchange_x_then_z,
        lambda value: exchange(value, "xy"),
        pieces,
    )

    cells = pl.pallas_call(
        gather_kernel,
        out_shape=jax.ShapeDtypeStruct((owners, share * height, edge), BF),
        in_specs=[in_vmem()],
        out_specs=in_vmem(),
        scratch_shapes=[pltpu.VMEM((owners * tile_count * height, edge), BF)],
        compiler_params=params(),
        name="gather",
    )(pieces)
    cells = exchange(cells, "xy")
    position, rendered = pl.pallas_call(
        place_kernel,
        out_shape=(
            jax.ShapeDtypeStruct(position.shape, F32),
            jax.ShapeDtypeStruct((share, PIECES, height, edge), BF),
        ),
        in_specs=[in_vmem()] * 2,
        out_specs=(pl.BlockSpec(memory_space=pl.ANY),) * 2,
        scratch_shapes=[pltpu.SemaphoreType.DMA((share + 1,))],
        compiler_params=params(),
        name="place",
    )(position, cells)
    rendered = rendered.reshape(1, share, edge, edge)
    return position[None], rendered


def solution(mesh):
    placed = (
        P("gz", "xy", None, None),
        P("gz", "xy", None),
        P("gz", "xy", None, None),
        P("gz", "xy", None),
        P("gz", "xy", None),
    )
    return jax.shard_map(
        body,
        mesh=mesh,
        in_specs=placed,
        out_specs=(P("gz", None, "xy"), P("gz", "xy", None, None)),
        check_vma=False,
    )
```
